128 devices in a mesh: bulk: 16 (over y, x), seq: 8 (over z, core).
Axes of the slice: x: 4, y: 4, z: 4, core: 2. Of those that a mesh axis runs over, the one named last changes fastest.
Arguments:
- clips: bfloat16 [4096, 4, 4, 4, 192], P(('bulk', 'seq')), may hold values from -6 to 6
- clip_counts: int32 [4096], P(('bulk', 'seq')), may hold values from 1 to 4
- histories: int32 [512, 64], P(('bulk', 'seq')), may hold values from 0 to 4095, as said below
- lengths: int32 [512], P(('bulk', 'seq')), may hold values from 1 to 64
- user_cotangent: float32 [512, 512], P(('bulk', 'seq')), may hold values from -6 to 6
- expand_first: bfloat16 [192, 432], replicated, may hold values from -0.4375 to 0.4375
- spatial_first: bfloat16 [9, 432], replicated, may hold values from -2 to 2
- temporal_first: bfloat16 [3, 432], replicated, may hold values from -3.5 to 3.5
- project_first: bfloat16 [432, 192], replicated, may hold values from -0.3125 to 0.3125
- expand_second: bfloat16 [192, 432], replicated, may hold values from -0.4375 to 0.4375
- spatial_second: bfloat16 [9, 432], replicated, may hold values from -2 to 2
- temporal_second: bfloat16 [3, 432], replicated, may hold values from -3.5 to 3.5
- project_second: bfloat16 [432, 192], replicated, may hold values from -0.3125 to 0.3125
- item_project: bfloat16 [192, 512], replicated, may hold values from -0.4375 to 0.4375
- tower_up: bfloat16 [512, 1024], replicated, may hold values from -0.25 to 0.25
- tower_down: bfloat16 [1024, 512], replicated, may hold values from -0.1875 to 0.1875
Outputs:
- user_vector: float32 [512, 512], P(('bulk', 'seq'))
- grad_expand_first: float32 [192, 432], replicated
- grad_spatial_first: float32 [9, 432], replicated
- grad_temporal_first: float32 [3, 432], replicated
- grad_project_first: float32 [432, 192], replicated
- grad_expand_second: float32 [192, 432], replicated
- grad_spatial_second: float32 [9, 432], replicated
- grad_temporal_second: float32 [3, 432], replicated
- grad_project_second: float32 [432, 192], replicated
- grad_item_project: float32 [192, 512], replicated
- grad_tower_up: float32 [512, 1024], replicated
- grad_tower_down: float32 [1024, 512], replicated
The draws below stay inside these ranges and needn't reach their ends.
Inputs may be any that keep to these rules, and one draw needn't show every extreme that they name: `histories`: items k * 32 to (k + 1) * 32 - 1 belong to the k-th device in bulk+seq order. Among the 256 entries of one device, at most 4 name items of any one device; in every draw one device's items are named exactly 4 times by the entries of every device. Ids may repeat.
All inputs are finite; a program needn't handle non-finite values.
Results may differ from the reference program's by a relative error of at most 0.02.
Values may be sent and summed in bfloat16 or wider, within the bound.
No kernel may reach another device: no remote copies, remote signals or barrier semaphores. Data moves between devices by JAX's collectives and lax.ppermute only.
A program may use at most 192 MiB of HBM per device.

```python
import jax
import jax.numpy as jnp
from jax import lax

C = 192
E = 432
D = 512
FH = 1024
FRAMES = 4
SIDE = 4
LEN = 64
ITEM_DEV = 32
USER_DEV = 4
CAP = 4
ITEMS = 4096
USERS = 512
N_BULK = 16
N_SEQ = 8


def draw_histories(key, part):
    key = jax.random.fold_in(key, 7)
    devices = N_BULK * N_SEQ
    row_count = USER_DEV * LEN
    pool_size = devices * CAP
    busiest = jax.random.randint(jax.random.fold_in(key, 1), (), 0, devices)

    def one_block(index):
        sub_key = jax.random.fold_in(key, index + 2)
        key_pool, key_order, key_local = jax.random.split(sub_key, 3)
        drawn = jax.random.permutation(key_pool, pool_size)
        scores = jnp.where(drawn // CAP == busiest, drawn - pool_size, jnp.arange(pool_size))
        chosen = drawn[jnp.argsort(scores, stable=True)][:row_count]
        chosen = jax.random.permutation(key_order, chosen)
        within = jax.random.randint(key_local, (row_count,), 0, ITEM_DEV)
        return chosen // CAP * ITEM_DEV + within
    blocks = jax.lax.map(one_block, jnp.arange(devices))
    return blocks.reshape(USERS, LEN).astype(jnp.int32)


def plant(result, rng, least, top_value):
    place = [jax.random.randint(jax.random.fold_in(rng, axis), (), 0, length) for axis, length in enumerate(result.shape)]
    widest = result.shape.index(max(result.shape))
    next_to = place[:widest] + [(place[widest] + 1) % result.shape[widest]] + place[widest + 1:]
    return result.at[tuple(place)].set(least).at[tuple(next_to)].set(top_value)


def shard_levels(own_key, shape, pieces, smallest, high):
    level = 1.0
    for dim, shards_of in pieces:
        draws = jax.random.uniform(jax.random.fold_in(jax.random.fold_in(own_key, 6), dim), (shards_of,), jnp.float32, smallest / len(pieces), high / len(pieces))
        level = level * jnp.repeat(jnp.exp(draws), shape[dim] // shards_of).reshape((-1,) + (1,) * (len(shape) - 1 - dim))
    return level


def noise(key, dims, deviation, bound, cuts=(), held_as=jnp.bfloat16):
    entries = deviation * jax.random.normal(key, dims, jnp.float32)
    if cuts:
        entries = entries * shard_levels(key, dims, cuts, -0.22, 0.18)
    return jnp.clip(entries, -bound, bound).astype(held_as)


def setup_inputs(seed: int = 0) -> dict:
    key_of = jax.random.split(jax.random.key(seed), 17)
    return {
        "clips": noise(key_of[0], (ITEMS, FRAMES, SIDE, SIDE, C), 1.0, 6.0, ((0, 128),)),
        "clip_counts": plant(jax.random.randint(key_of[1], (ITEMS,), 1, FRAMES + 1), jax.random.fold_in(key_of[1], 1), 1, FRAMES).astype(jnp.int32),
        "histories": draw_histories(jax.random.fold_in(key_of[16], 71), 0),
        "lengths": plant(jax.random.randint(key_of[3], (USERS,), 1, LEN + 1), jax.random.fold_in(key_of[3], 1), 1, LEN).astype(jnp.int32),
        "user_cotangent": noise(key_of[4], (USERS, D), 1.0, 6.0, ((0, 128),), jnp.float32),
        "expand_first": noise(key_of[5], (C, E), C ** -0.5, 0.4375),
        "spatial_first": noise(key_of[6], (9, E), 9 ** -0.5, 2.0),
        "temporal_first": noise(key_of[7], (3, E), 3 ** -0.5, 3.5),
        "project_first": noise(key_of[8], (E, C), E ** -0.5, 0.3125),
        "expand_second": noise(key_of[9], (C, E), C ** -0.5, 0.4375),
        "spatial_second": noise(key_of[10], (9, E), 9 ** -0.5, 2.0),
        "temporal_second": noise(key_of[11], (3, E), 3 ** -0.5, 3.5),
        "project_second": noise(key_of[12], (E, C), E ** -0.5, 0.3125),
        "item_project": noise(key_of[13], (C, D), C ** -0.5, 0.4375),
        "tower_up": noise(key_of[14], (D, FH), D ** -0.5, 0.25),
        "tower_down": noise(key_of[15], (FH, D), FH ** -0.5, 0.1875),
    }


PRECISE = lax.Precision.HIGHEST

def conv_section(masked, expand, spatial, temporal, project):
    item_count, frames, side_cells, _, channels = masked.shape
    inner_width = expand.shape[1]
    half_side = side_cells // 2
    grown = jnp.dot(masked.reshape(-1, channels), expand, preferred_element_type=jnp.float32)
    grown = jax.nn.silu(grown).astype(jnp.bfloat16).reshape(item_count, frames, side_cells, side_cells, inner_width)
    padded = jnp.pad(grown.astype(jnp.float32), ((0, 0), (0, 0), (1, 1), (1, 1), (0, 0)))
    spatial_taps = spatial.astype(jnp.float32)
    spatial_out = jnp.zeros((item_count, frames, half_side, half_side, inner_width), jnp.float32)
    for offset_row in range(3):
        for offset_col in range(3):
            window = padded[:, :, offset_row:offset_row + 2 * half_side:2, offset_col:offset_col + 2 * half_side:2, :]
            spatial_out = spatial_out + window * spatial_taps[offset_row * 3 + offset_col]
    framed = jnp.pad(spatial_out, ((0, 0), (1, 1), (0, 0), (0, 0), (0, 0)))
    temporal_taps = temporal.astype(jnp.float32)
    summed = framed[:, 0:frames] * temporal_taps[0] + framed[:, 1:frames + 1] * temporal_taps[1]
    summed = summed + framed[:, 2:frames + 2] * temporal_taps[2]
    narrow = jax.nn.silu(summed).astype(jnp.bfloat16)
    projected = jnp.dot(narrow.reshape(-1, inner_width), project, preferred_element_type=jnp.float32)
    return projected.astype(jnp.bfloat16).reshape(item_count, frames, half_side, half_side, channels)

def encode_clips(params, clips, counts):
    frames = clips.shape[1]
    live_mask = jnp.arange(frames)[None, :] < counts[:, None]
    masked = jnp.where(live_mask[:, :, None, None, None], clips, jnp.zeros_like(clips))
    section_one = conv_section(masked, params[0], params[1], params[2], params[3])
    section_two = conv_section(section_one, params[4], params[5], params[6], params[7])
    cell_count = section_two.shape[2] * section_two.shape[3]
    weights = live_mask.astype(jnp.float32) / (counts.astype(jnp.float32)[:, None] * cell_count)
    return jnp.einsum('if,ifpqc->ic', weights, section_two.astype(jnp.float32), precision=PRECISE)

def user_tower(fetched, lengths, tower_up, tower_down, cotangent):
    user_count, length, width = fetched.shape
    flat_rows = fetched.reshape(-1, width)
    hidden_pre = jnp.dot(flat_rows, tower_up, preferred_element_type=jnp.float32)
    hidden_act = jax.nn.gelu(hidden_pre).astype(jnp.bfloat16)
    down_out = jnp.dot(hidden_act, tower_down, preferred_element_type=jnp.float32)
    mixed = (flat_rows.astype(jnp.float32) + down_out).reshape(user_count, length, width)
    pool_weights = (jnp.arange(length)[None, :] < lengths[:, None]).astype(jnp.float32)
    pool_weights = pool_weights / lengths.astype(jnp.float32)[:, None]
    user_vec = jnp.einsum('ul,uld->ud', pool_weights, mixed, precision=PRECISE)
    mixed_grad = (pool_weights[:, :, None] * cotangent[:, None, :]).reshape(-1, width)
    mixed_half = mixed_grad.astype(jnp.bfloat16)
    grad_down = jnp.dot(hidden_act.T, mixed_half, preferred_element_type=jnp.float32)
    act_grad = jnp.dot(mixed_half, tower_down.T, preferred_element_type=jnp.float32)
    gelu_slope = jax.jvp(jax.nn.gelu, (hidden_pre,), (jnp.ones_like(hidden_pre),))[1]
    pre_grad = (act_grad * gelu_slope).astype(jnp.bfloat16)
    grad_up = jnp.dot(flat_rows.T, pre_grad, preferred_element_type=jnp.float32)
    rows_grad = mixed_grad + jnp.dot(pre_grad, tower_up.T, preferred_element_type=jnp.float32)
    return (user_vec, grad_up, grad_down, rows_grad)

def reference(clips, clip_counts, histories, lengths, user_cotangent, expand_first, spatial_first, temporal_first, project_first, expand_second, spatial_second, temporal_second, project_second, item_project, tower_up, tower_down):
    params = (expand_first, spatial_first, temporal_first, project_first, expand_second, spatial_second, temporal_second, project_second)
    devices = N_BULK * N_SEQ
    clip_blocks = clips.reshape((devices, ITEM_DEV) + clips.shape[1:])
    count_blocks = clip_counts.reshape(devices, ITEM_DEV)
    pooled = lax.map(lambda pair: encode_clips(params, pair[0], pair[1]), (clip_blocks, count_blocks))
    pooled = pooled.reshape(ITEMS, C)
    item_vec = jnp.dot(pooled, item_project.astype(jnp.float32), precision=PRECISE).astype(jnp.bfloat16)

    def tower_block(carry, block):
        block_ids, block_lengths, block_cotangent = block
        fetched = item_vec[block_ids]
        user_vec, grad_up, grad_down, rows_grad = user_tower(fetched, block_lengths, tower_up, tower_down, block_cotangent)
        up_total, down_total, item_grads = carry
        item_grads = item_grads.at[block_ids.reshape(-1)].add(rows_grad)
        return ((up_total + grad_up, down_total + grad_down, item_grads), user_vec)
    start = (jnp.zeros((D, FH), jnp.float32), jnp.zeros((FH, D), jnp.float32), jnp.zeros((ITEMS, D), jnp.float32))
    blocks = (histories.reshape(devices, USER_DEV, LEN), lengths.reshape(devices, USER_DEV), user_cotangent.reshape(devices, USER_DEV, D))
    (grad_up, grad_down, item_grads), user_vec = lax.scan(tower_block, start, blocks)
    user_vec = user_vec.reshape(USERS, D)
    pooled_grads = jnp.dot(item_grads, item_project.astype(jnp.float32).T, precision=PRECISE)
    grad_item = jnp.dot(pooled.T, item_grads, precision=PRECISE)

    def encoder_block(totals, block):
        block_clips, block_counts, block_cotangent = block
        _, pullback = jax.vjp(lambda weights: encode_clips(weights, block_clips, block_counts), params)
        terms = pullback(block_cotangent)[0]
        return (tuple((total + term.astype(jnp.float32) for total, term in zip(totals, terms))), None)
    zeros_start = tuple((jnp.zeros(weight.shape, jnp.float32) for weight in params))
    encoder_totals, _ = lax.scan(encoder_block, zeros_start, (clip_blocks, count_blocks, pooled_grads.reshape(devices, ITEM_DEV, C)))
    return (user_vec, encoder_totals[0], encoder_totals[1], encoder_totals[2], encoder_totals[3], encoder_totals[4], encoder_totals[5], encoder_totals[6], encoder_totals[7], grad_item, grad_up, grad_down)
```

```python
import jax
import jax.numpy as jnp
from jax import lax
from jax.experimental import pallas as pl
from jax.experimental.pallas import tpu as pltpu
from jax.sharding import PartitionSpec as P

BF = jnp.bfloat16
F32 = jnp.float32
AXES = ("bulk", "seq")
C, E, D, FH = 192, 432, 512, 1024
FRAMES, SIDE, ITEMS_HERE, USERS_HERE, LENGTH = 4, 4, 32, 4, 64
DEVICES, CHIPS, CAPACITY = 128, 64, 4
ROWS = USERS_HERE * LENGTH
CELLS = SIDE * SIDE
HALF = 2
LINKS_FIRST = [
    (HALF * p + q, SIDE * (2 * p + a - 1) + 2 * q + b - 1, 3 * a + b)
    for p in range(HALF)
    for q in range(HALF)
    for a in range(3)
    for b in range(3)
    if 0 <= 2 * p + a - 1 < SIDE and 0 <= 2 * q + b - 1 < SIDE
]
LINKS_SECOND = [(0, 4), (1, 5), (2, 7), (3, 8)]


def dot_nn(a, b):
    return lax.dot_general(a, b, (((1,), (0,)), ((), ())), preferred_element_type=F32)


def dot_nt(a, b):
    return lax.dot_general(a, b, (((1,), (1,)), ((), ())), preferred_element_type=F32)


def dot_tn(a, b):
    return lax.dot_general(a, b, (((0,), (0,)), ((), ())), preferred_element_type=F32)


def silu_and_slope(v):
    gate = 0.5 * jnp.tanh(0.5 * v) + 0.5
    value = v * gate
    return value, gate + value - value * gate


def conv_forward(
    x, counts, e1, s1, t1, p1, e2, s2, t2, p2,
    block, g1, d1, sp1, n1, h1, o1, g2, d2, sp2, n2, h2,
    framed1, framed2,
):
    zero4 = jnp.zeros((HALF * HALF, ITEMS_HERE, E), F32)
    framed1[0] = zero4
    framed1[FRAMES + 1] = zero4
    zero1 = jnp.zeros((ITEMS_HERE, E), F32)
    framed2[0] = zero1
    framed2[FRAMES + 1] = zero1
    taps1 = s1[...].astype(F32)
    taps2 = s2[...].astype(F32)
    frame1 = t1[...].astype(F32)
    frame2 = t2[...].astype(F32)

    def grow(f, _):
        live = f < counts[...]
        x_f = x[pl.ds(f * CELLS, CELLS)]
        x_f = jnp.where(live[None], x_f, jnp.zeros_like(x_f))
        pre = dot_nn(x_f.reshape(CELLS * ITEMS_HERE, C), e1[...])
        value, slope = silu_and_slope(pre)
        value = value.astype(BF).reshape(CELLS, ITEMS_HERE, E)
        g1[pl.ds(f * CELLS, CELLS)] = value
        d1[pl.ds(f * CELLS, CELLS)] = slope.astype(BF).reshape(CELLS, ITEMS_HERE, E)
        outs = [jnp.zeros((ITEMS_HERE, E), F32)] * 4
        for out_cell, in_cell, tap in LINKS_FIRST:
            outs[out_cell] = outs[out_cell] + value[in_cell].astype(F32) * taps1[tap]
        for out_cell in range(4):
            framed1[f + 1, out_cell] = outs[out_cell]
            sp1[f, out_cell] = outs[out_cell].astype(BF)
        return 0

    lax.fori_loop(0, FRAMES, grow, 0)

    def narrow_first(f, _):
        summed = framed1[f] * frame1[0] + framed1[f + 1] * frame1[1] + framed1[f + 2] * frame1[2]
        value, slope = silu_and_slope(summed)
        n1[pl.ds(f * 4, 4)] = value.astype(BF)
        h1[pl.ds(f * 4, 4)] = slope.astype(BF)
        return 0

    lax.fori_loop(0, FRAMES, narrow_first, 0)
    first = dot_nn(n1[...].reshape(FRAMES * 4 * ITEMS_HERE, E), p1[...]).astype(BF)
    o1[...] = first
    value, slope = silu_and_slope(dot_nn(first, e2[...]))
    value = value.astype(BF).reshape(FRAMES * 4, ITEMS_HERE, E)
    g2[...] = value
    d2[...] = slope.astype(BF).reshape(FRAMES * 4, ITEMS_HERE, E)
    for f in range(FRAMES):
        total = jnp.zeros((ITEMS_HERE, E), F32)
        for cell, tap in LINKS_SECOND:
            total = total + value[f * 4 + cell].astype(F32) * taps2[tap]
        framed2[f + 1] = total
        sp2[f] = total.astype(BF)
    for f in range(FRAMES):
        summed = framed2[f] * frame2[0] + framed2[f + 1] * frame2[1] + framed2[f + 2] * frame2[2]
        value, slope = silu_and_slope(summed)
        n2[f] = value.astype(BF)
        h2[f] = slope.astype(BF)
    second = dot_nn(n2[...].reshape(FRAMES * ITEMS_HERE, E), p2[...]).astype(BF)
    pooled = jnp.zeros((ITEMS_HERE, C), F32)
    for f in range(FRAMES):
        live = (f < counts[...]).astype(F32)
        pooled = pooled + live * second[f * ITEMS_HERE : (f + 1) * ITEMS_HERE].astype(F32)
    pooled = (pooled / counts[...].astype(F32)).astype(BF)
    block[0:32] = pooled[:, 0:128]
    block[32:64] = jnp.concatenate([pooled[:, 128:192], jnp.zeros((ITEMS_HERE, 64), BF)], axis=1)


def tower(
    core, lengths, own, other, ids_col, ids_row, cot, project, up, down,
    sent, factors, user_vec,
):
    ids = ids_col[...]
    owner = ids // ITEMS_HERE
    within = ids - owner * ITEMS_HERE
    chip = owner // 2
    place = chip * ITEMS_HERE + within
    mine = (owner - chip * 2) == core[0]
    lanes = lax.broadcasted_iota(jnp.int32, (ROWS, CHIPS * ITEMS_HERE), 1)
    pick_own = (lanes == jnp.where(mine, place, -1)).astype(F32).astype(BF)
    pick_other = (lanes == jnp.where(mine, -1, place)).astype(F32).astype(BF)

    def rows_of(ref, at):
        return ref[:, at : at + 32, :].reshape(CHIPS * ITEMS_HERE, 128)

    picked_low = (dot_nn(pick_own, rows_of(own, 0)) + dot_nn(pick_other, rows_of(other, 0))).astype(BF)
    picked_high = (dot_nn(pick_own, rows_of(own, 32)) + dot_nn(pick_other, rows_of(other, 32))).astype(BF)
    fetched = dot_nn(picked_low, project[0:128]) + dot_nn(picked_high[:, 0:64], project[128:192])
    fetched = fetched.astype(BF)
    pre = dot_nn(fetched, up[...])
    scale = 0.7978845608028654
    square = pre * pre
    bent = jnp.tanh(scale * pre * (1.0 + 0.044715 * square))
    gate = 0.5 * (1.0 + bent)
    act = (pre * gate).astype(BF)
    slope = gate + 0.5 * pre * (1.0 - bent * bent) * (scale * (1.0 + 3 * 0.044715 * square))

    user = lax.broadcasted_iota(jnp.int32, (8, 1), 0)
    length = jnp.ones((8, 1), jnp.int32)
    for u in range(USERS_HERE):
        length = jnp.where(user == u, lengths[u], length)
    at = lax.broadcasted_iota(jnp.int32, (8, ROWS), 1)
    live = ((at // LENGTH == user) & (at - user * LENGTH < length)).astype(F32)
    live_half = live.astype(BF)
    act_sum = dot_nn(live_half, act)
    low_sum = dot_nn(live_half, picked_low)
    high_sum = dot_nn(live_half, picked_high)
    count = length.astype(F32)
    shared = cot[...] / count[0:4]
    shared_half = shared.astype(BF)
    factors[:, 0:FH] = act_sum[0:4].astype(BF)
    factors[:, FH : FH + 128] = low_sum[0:4].astype(BF)
    factors[:, FH + 128 : FH + 256] = high_sum[0:4].astype(BF)
    factors[:, FH + 256 : FH + 256 + D] = shared_half
    coarse = act_sum.astype(BF)
    fine = (act_sum - coarse.astype(F32)).astype(BF)
    mixed = dot_nn(live_half, fetched) + dot_nn(coarse, down[...]) + dot_nn(fine, down[...])
    user_vec[...] = (mixed / count)[0:4]

    act_grad = dot_nt(jnp.concatenate([shared_half, shared_half], axis=0), down[...])
    position = lax.broadcasted_iota(jnp.int32, (LENGTH, 1), 0)
    pre_parts, base_parts = [], []
    for u in range(USERS_HERE):
        alive = (position < lengths[u]).astype(F32)
        pre_parts.append(alive * act_grad[u : u + 1] * slope[u * LENGTH : (u + 1) * LENGTH])
        base_parts.append(alive * shared[u : u + 1])
    pre_grad = jnp.concatenate(pre_parts, axis=0).astype(BF)
    rows_grad = jnp.concatenate(base_parts, axis=0) + dot_nt(pre_grad, up[...])
    rows_coarse = rows_grad.astype(BF)
    rows_fine = (rows_grad - rows_coarse.astype(F32)).astype(BF)
    low = dot_nt(rows_coarse, project[0:128]) + dot_nt(rows_fine, project[0:128])
    high = dot_nt(rows_coarse, project[64:192]) + dot_nt(rows_fine, project[64:192])
    lane = lax.broadcasted_iota(jnp.int32, (ROWS, 128), 1)
    tag = within.astype(F32)
    low = jnp.where(lane < 96, low, jnp.where(lane == 96, tag, 0.0)).astype(BF)
    high = jnp.where(lane >= 32, high, jnp.where(lane == 0, tag, 0.0)).astype(BF)

    owner_row = ids_row[...] // ITEMS_HERE
    earlier = lax.broadcasted_iota(jnp.int32, (ROWS, ROWS), 0) < lax.broadcasted_iota(jnp.int32, (ROWS, ROWS), 1)
    rank = jnp.sum(((owner == owner_row) & earlier).astype(F32), axis=0, keepdims=True).astype(jnp.int32)
    slot = owner_row * 8 + rank
    sent_at = lax.broadcasted_iota(jnp.int32, (DEVICES * 8, ROWS), 0)
    put_low = (sent_at == slot).astype(F32).astype(BF)
    put_high = (sent_at == slot + CAPACITY).astype(F32).astype(BF)
    back = (dot_nn(put_low, low) + dot_nn(put_high, high)).astype(BF)
    sent[:, 0:8, :] = back.reshape(DEVICES, 8, 128)
    up_low = dot_tn(picked_low, pre_grad).astype(BF)
    up_high = dot_tn(picked_high, pre_grad).astype(BF)
    for j in range(FH // 128):
        cut = slice(j * 128, (j + 1) * 128)
        sent[j * 16 : j * 16 + 8, 8:24, :] = up_low[:, cut].reshape(8, 16, 128)
        sent[j * 16 + 8 : j * 16 + 16, 8:24, :] = up_high[:, cut].reshape(8, 16, 128)


def conv_backward(
    back, x, counts, s1, t1, p1, e2, s2, t2, p2, g1, d1, sp1, n1, h1, o1, g2, d2, sp2, n2, h2,
    packed,
    spatial_grad, wide, small,
):
    taps1 = s1[...].astype(F32)
    taps2 = s2[...].astype(F32)
    frame1 = t1[...].astype(F32)
    frame2 = t2[...].astype(F32)

    def tile_sum(v):
        return jnp.sum(v.reshape(-1, 8, E), axis=0)

    small[...] = jnp.zeros(small.shape, F32)
    wide[...] = jnp.zeros(wide.shape, F32)
    got = back[:, 0:8, :].reshape(DEVICES * 8, 128)
    row = lax.broadcasted_iota(jnp.int32, (DEVICES * 8, 1), 0)
    is_low = (row & 7) < CAPACITY
    got_f = got.astype(F32)
    tag = jnp.where(is_low, got_f[:, 96:97], got_f[:, 0:1]).astype(jnp.int32)
    named = tag == lax.broadcasted_iota(jnp.int32, (DEVICES * 8, ITEMS_HERE), 1)
    low = dot_tn((named & is_low).astype(F32).astype(BF), got)
    high = dot_tn((named & ~is_low).astype(F32).astype(BF), got)
    pooled_grad = jnp.concatenate([low[:, 0:96], high[:, 32:128]], axis=1)
    shared = pooled_grad / counts[...].astype(F32)
    out_grad = jnp.concatenate(
        [(shared * (f < counts[...]).astype(F32)).astype(BF) for f in range(FRAMES)], axis=0
    )
    wide[576:768, 0:E] = dot_tn(out_grad, n2[...].reshape(FRAMES * ITEMS_HERE, E))
    summed_grad = dot_nt(out_grad, p2[...]).reshape(FRAMES, ITEMS_HERE, E) * h2[...].astype(F32)
    spread = []
    for f in range(FRAMES):
        total = summed_grad[f] * frame2[1]
        if f + 1 < FRAMES:
            total = total + summed_grad[f + 1] * frame2[0]
        if f > 0:
            total = total + summed_grad[f - 1] * frame2[2]
        spread.append(total)
    for k in range(3):
        total = jnp.zeros((8, E), F32)
        for f in range(FRAMES):
            if 0 <= f + k - 1 < FRAMES:
                total = total + tile_sum(sp2[f + k - 1].astype(F32) * summed_grad[f])
        small[21 + k] = total
    parts = []
    for f in range(FRAMES):
        for cell, tap in LINKS_SECOND:
            small[12 + tap] += tile_sum(g2[f * 4 + cell].astype(F32) * spread[f])
            parts.append((spread[f] * taps2[tap] * d2[f * 4 + cell].astype(F32)).astype(BF))
    grown_grad = jnp.concatenate(parts, axis=0)
    wide[384:576, 0:E] = dot_tn(o1[...], grown_grad)
    first_grad = dot_nt(grown_grad, e2[...]).astype(BF)
    wide[192:384, 0:E] = dot_tn(first_grad, n1[...].reshape(FRAMES * 4 * ITEMS_HERE, E))
    narrow_grad = dot_nt(first_grad, p1[...]).reshape(FRAMES, 4, ITEMS_HERE, E)
    summed_grad = [narrow_grad[f] * h1[f * 4 : f * 4 + 4].astype(F32) for f in range(FRAMES)]
    for k in range(3):
        total = jnp.zeros((8, E), F32)
        for f in range(FRAMES):
            if 0 <= f + k - 1 < FRAMES:
                total = total + tile_sum(sp1[f + k - 1].astype(F32) * summed_grad[f])
        small[9 + k] = total
    for f in range(FRAMES):
        total = summed_grad[f] * frame1[1]
        if f + 1 < FRAMES:
            total = total + summed_grad[f + 1] * frame1[0]
        if f > 0:
            total = total + summed_grad[f - 1] * frame1[2]
        spatial_grad[f] = total

    def grow_back(f, _):
        live = f < counts[...]
        x_f = x[pl.ds(f * CELLS, CELLS)]
        x_f = jnp.where(live[None], x_f, jnp.zeros_like(x_f)).reshape(CELLS * ITEMS_HERE, C)
        sums = [jnp.zeros((8, E), F32)] * 9
        grads = [jnp.zeros((ITEMS_HERE, E), F32)] * CELLS
        for out_cell, in_cell, tap in LINKS_FIRST:
            from_out = spatial_grad[f, out_cell]
            grads[in_cell] = grads[in_cell] + from_out * taps1[tap]
            sums[tap] = sums[tap] + tile_sum(g1[f * CELLS + in_cell].astype(F32) * from_out)
        for tap in range(9):
            small[tap] += sums[tap]
        grads = [(grads[cell] * d1[f * CELLS + cell].astype(F32)).astype(BF) for cell in range(CELLS)]
        wide[0:192, 0:E] += dot_tn(x_f, jnp.concatenate(grads, axis=0))
        return 0

    lax.fori_loop(0, FRAMES, grow_back, 0)
    sums = jnp.sum(small[...], axis=1).astype(BF)
    put = lax.broadcasted_iota(jnp.int32, (32, 128), 1) == lax.broadcasted_iota(jnp.int32, (32, 128), 0) + 64
    wide[0:E, 384:512] += dot_tn(sums, put.astype(F32).astype(BF))
    for j in range(4):
        packed[j * 768 : (j + 1) * 768] = wide[:, j * 128 : (j + 1) * 128].astype(BF)


def finish_tower(factors, up_total, project, up, grad_item, grad_up, grad_down):
    shared = factors[:, FH + 256 : FH + 256 + D]
    grad_down[...] = dot_tn(factors[:, 0:FH], shared)
    item = dot_tn(factors[:, FH : FH + C], shared)
    for j in range(FH // 128):
        part = up_total[j * 16 : j * 16 + 16].reshape(256, 128)[0:C]
        cut = slice(j * 128, (j + 1) * 128)
        grad_up[:, cut] = dot_tn(project[...], part)
        item = item + dot_nt(part, up[:, cut])
    grad_item[...] = item


def finish_conv(packed, ge1, gs1, gt1, gp1, ge2, gs2, gt2, gp2):
    def unit(n):
        same = lax.broadcasted_iota(jnp.int32, (n, n), 0) == lax.broadcasted_iota(jnp.int32, (n, n), 1)
        return same.astype(F32).astype(BF)

    turn = unit(C)
    for j in range(4):
        width = min(128, E - j * 128)
        at = j * 768
        cut = slice(j * 128, j * 128 + width)
        ge1[:, cut] = packed[at : at + 192].astype(F32)[:, 0:width]
        gp1[cut, :] = dot_tn(packed[at + 192 : at + 384], turn)[0:width]
        ge2[:, cut] = packed[at + 384 : at + 576].astype(F32)[:, 0:width]
        gp2[cut, :] = dot_tn(packed[at + 576 : at + 768], turn)[0:width]
    small = dot_tn(packed[3 * 768 : 3 * 768 + E], unit(E))
    gs1[...] = small[64:73]
    gt1[...] = small[73:76]
    gs2[...] = small[76:85]
    gt2[...] = small[85:88]


def shape(dims, dtype=BF):
    return jax.ShapeDtypeStruct(dims, dtype)


def call(kernel, outs, scratch=(), smem=0):
    def run(*args):
        return pl.pallas_call(
            kernel,
            out_shape=outs,
            in_specs=[
                pl.BlockSpec(memory_space=pltpu.SMEM if i < smem else pltpu.VMEM)
                for i in range(len(args))
            ],
            out_specs=[pl.BlockSpec(memory_space=pltpu.VMEM)] * len(outs),
            scratch_shapes=list(scratch),
            compiler_params=pltpu.CompilerParams(vmem_limit_bytes=56 * 1024 * 1024),
        )(*args)

    return run


def local(
    clips, clip_counts, histories, lengths, user_cotangent,
    expand_first, spatial_first, temporal_first, project_first,
    expand_second, spatial_second, temporal_second, project_second,
    item_project, tower_up, tower_down,
):
    same_core = [[i for i in range(DEVICES) if i % 2 == c] for c in range(2)]
    other_core = [(i, i ^ 1) for i in range(8)]
    core = lax.axis_index("seq") % 2

    def exchange(v):
        return lax.all_to_all(v, AXES, 0, 0, tiled=True)

    x = clips.reshape(ITEMS_HERE, FRAMES * CELLS, C).transpose(1, 0, 2)
    counts = clip_counts.reshape(ITEMS_HERE, 1)
    weights = (
        spatial_first, temporal_first, project_first,
        expand_second, spatial_second, temporal_second, project_second,
    )
    n = ITEMS_HERE
    block, *kept = call(
        conv_forward,
        [
            shape((64, 128)),
            shape((64, n, E)), shape((64, n, E)), shape((4, 4, n, E)), shape((16, n, E)), shape((16, n, E)),
            shape((512, C)), shape((16, n, E)), shape((16, n, E)), shape((4, n, E)), shape((4, n, E)), shape((4, n, E)),
        ],
        [pltpu.VMEM((FRAMES + 2, 4, n, E), F32), pltpu.VMEM((FRAMES + 2, n, E), F32)],
    )(x, counts, expand_first, *weights)
    own = lax.all_to_all(
        jnp.broadcast_to(block[None], (CHIPS, 64, 128)), AXES, 0, 0, axis_index_groups=same_core, tiled=True
    )
    other = lax.ppermute(own, "seq", other_core)
    sent, factors, user_vec = call(
        tower,
        [shape((DEVICES, 24, 128)), shape((USERS_HERE, FH + 256 + D)), shape((USERS_HERE, D), F32)],
        smem=2,
    )(
        core.reshape(1), lengths, own, other, histories.reshape(ROWS, 1), histories.reshape(1, ROWS),
        user_cotangent, item_project, tower_up, tower_down,
    )
    factors = lax.all_gather(factors, AXES, tiled=True)
    back = exchange(sent)
    (packed,) = call(
        conv_backward,
        [shape((3072, 128))],
        [pltpu.VMEM((4, 4, n, E), F32), pltpu.VMEM((768, 512), F32), pltpu.VMEM((32, 8, E), F32)],
    )(back, x, counts, *weights, *kept)
    up_sum = jnp.sum(back[:, 8:24].astype(F32), axis=0).astype(BF)
    third = exchange(
        jnp.concatenate([packed.reshape(DEVICES, 24, 128), jnp.broadcast_to(up_sum[None], (DEVICES, 16, 128))], axis=1)
    )
    conv_sum = jnp.sum(third[:, 0:24].astype(F32), axis=0).astype(BF)
    fourth = exchange(jnp.broadcast_to(conv_sum[None], (DEVICES, 24, 128)))
    grad_item, grad_up, grad_down = call(
        finish_tower, [shape((C, D), F32), shape((D, FH), F32), shape((FH, D), F32)]
    )(factors, third[:, 24:40], item_project, tower_up)
    conv_grads = call(
        finish_conv,
        [shape((C, E), F32), shape((9, E), F32), shape((3, E), F32), shape((E, C), F32)] * 2,
    )(fourth.reshape(3072, 128))
    return (user_vec, *conv_grads, grad_item, grad_up, grad_down)


def solution(mesh):
    spread = P(AXES)
    return jax.shard_map(
        local,
        mesh=mesh,
        in_specs=(spread,) * 5 + (P(),) * 11,
        out_specs=(spread,) + (P(),) * 11,
        check_vma=False,
    )
```

```python
import jax
import jax.numpy as jnp
from jax import lax
from jax.experimental import pallas as pl
from jax.experimental.pallas import tpu as pltpu
from jax.sharding import PartitionSpec as P

BF = jnp.bfloat16
F32 = jnp.float32
AXES = ("bulk", "seq")
C, E, D, FH = 192, 432, 512, 1024
FRAMES, SIDE, ITEMS_HERE, USERS_HERE, LENGTH = 4, 4, 32, 4, 64
DEVICES, CHIPS, CAPACITY = 128, 64, 4
ROWS = USERS_HERE * LENGTH
CELLS = SIDE * SIDE
HALF = 2
LINKS_FIRST = [
    (HALF * p + q, SIDE * (2 * p + a - 1) + 2 * q + b - 1, 3 * a + b)
    for p in range(HALF)
    for q in range(HALF)
    for a in range(3)
    for b in range(3)
    if 0 <= 2 * p + a - 1 < SIDE and 0 <= 2 * q + b - 1 < SIDE
]
LINKS_SECOND = [(0, 4), (1, 5), (2, 7), (3, 8)]


def dot_nn(a, b):
    return lax.dot_general(a, b, (((1,), (0,)), ((), ())), preferred_element_type=F32)


def dot_nt(a, b):
    return lax.dot_general(a, b, (((1,), (1,)), ((), ())), preferred_element_type=F32)


def dot_tn(a, b):
    return lax.dot_general(a, b, (((0,), (0,)), ((), ())), preferred_element_type=F32)


def silu_and_slope(v):
    gate = 0.5 * jnp.tanh(0.5 * v) + 0.5
    value = v * gate
    return value, gate + value - value * gate


def column_of(row):
    n = row.shape[1]
    same = lax.broadcasted_iota(jnp.int32, (n, n), 0) == lax.broadcasted_iota(jnp.int32, (n, n), 1)
    return jnp.sum(jnp.where(same, row.astype(F32), 0.0), axis=1, keepdims=True).astype(jnp.int32)


def per_user(lengths):
    user = lax.broadcasted_iota(jnp.int32, (8, 1), 0)
    length = jnp.ones((8, 1), jnp.int32)
    for u in range(USERS_HERE):
        length = jnp.where(user == u, lengths[u], length)
    return user, length


def conv_forward(
    lengths, x, counts_row, cot, e1, s1, t1, p1, e2, s2, t2, p2, *rest,
):
    *kept, framed1, framed2 = rest
    block = None
    if len(kept) == 1:
        (block,) = kept
    else:
        g1, d1, sp1, n1, h1, o1, g2, d2, sp2, n2, h2 = kept
    counts = column_of(counts_row[...])
    zero4 = jnp.zeros((HALF * HALF, ITEMS_HERE, E), F32)
    framed1[0] = zero4
    framed1[FRAMES + 1] = zero4
    zero1 = jnp.zeros((ITEMS_HERE, E), F32)
    framed2[0] = zero1
    framed2[FRAMES + 1] = zero1
    taps1 = s1[...].astype(F32)
    taps2 = s2[...].astype(F32)
    frame1 = t1[...].astype(F32)
    frame2 = t2[...].astype(F32)

    def grow(f, _):
        live = f < counts
        x_f = x[pl.ds(f * CELLS, CELLS)]
        x_f = jnp.where(live[None], x_f, jnp.zeros_like(x_f))
        pre = dot_nn(x_f.reshape(CELLS * ITEMS_HERE, C), e1[...])
        value, slope = silu_and_slope(pre)
        value = value.astype(BF).reshape(CELLS, ITEMS_HERE, E)
        if block is None:
            g1[pl.ds(f * CELLS, CELLS)] = value
            d1[pl.ds(f * CELLS, CELLS)] = slope.astype(BF).reshape(CELLS, ITEMS_HERE, E)
        outs = [jnp.zeros((ITEMS_HERE, E), F32)] * 4
        for out_cell, in_cell, tap in LINKS_FIRST:
            outs[out_cell] = outs[out_cell] + value[in_cell].astype(F32) * taps1[tap]
        for out_cell in range(4):
            framed1[f + 1, out_cell] = outs[out_cell]
            if block is None:
                sp1[f, out_cell] = outs[out_cell].astype(BF)
        return 0

    lax.fori_loop(0, FRAMES, grow, 0)
    narrow = []
    for f in range(FRAMES):
        summed = framed1[f] * frame1[0] + framed1[f + 1] * frame1[1] + framed1[f + 2] * frame1[2]
        value, slope = silu_and_slope(summed)
        narrow.append(value.astype(BF))
        if block is None:
            h1[f * 4 : f * 4 + 4] = slope.astype(BF)
    narrow = jnp.concatenate(narrow, axis=0)
    first = dot_nt(narrow.reshape(FRAMES * 4 * ITEMS_HERE, E), p1[...]).astype(BF)
    value, slope = silu_and_slope(dot_nn(first, e2[...]))
    value = value.astype(BF).reshape(FRAMES * 4, ITEMS_HERE, E)
    if block is None:
        n1[...] = narrow
        o1[...] = first
        g2[...] = value
        d2[...] = slope.astype(BF).reshape(FRAMES * 4, ITEMS_HERE, E)
    for f in range(FRAMES):
        total = jnp.zeros((ITEMS_HERE, E), F32)
        for cell, tap in LINKS_SECOND:
            total = total + value[f * 4 + cell].astype(F32) * taps2[tap]
        framed2[f + 1] = total
        if block is None:
            sp2[f] = total.astype(BF)
    narrow = []
    for f in range(FRAMES):
        summed = framed2[f] * frame2[0] + framed2[f + 1] * frame2[1] + framed2[f + 2] * frame2[2]
        value, slope = silu_and_slope(summed)
        narrow.append(value.astype(BF))
        if block is None:
            n2[f] = value.astype(BF)
            h2[f] = slope.astype(BF)
    if block is None:
        return
    second = dot_nt(jnp.concatenate(narrow, axis=0), p2[...]).astype(BF)
    pooled = jnp.zeros((ITEMS_HERE, C), F32)
    for f in range(FRAMES):
        live = (f < counts).astype(F32)
        pooled = pooled + live * second[f * ITEMS_HERE : (f + 1) * ITEMS_HERE].astype(F32)
    pooled = pooled / counts.astype(F32)
    _, length = per_user(lengths)
    shared = cot[...] / length[0:4].astype(F32)
    pieces = []
    for k in range(8):
        piece = shared[:, (k // 2) * 128 : (k // 2 + 1) * 128]
        pieces.append(piece if k % 2 else pltpu.roll(piece, 64, 1))
    lane = lax.broadcasted_iota(jnp.int32, (ITEMS_HERE, 128), 1)
    shared = jnp.concatenate(pieces, axis=0)
    high = jnp.concatenate([pooled[:, 128:192], pooled[:, 0:64]], axis=1)
    rows = jnp.concatenate([pooled[:, 0:128], jnp.where(lane < 64, high, shared)], axis=0).astype(BF)
    block[...] = jnp.broadcast_to(rows[None], block.shape)


def tower(
    core, lengths, own, other, ids_ref, cot, project, up, down,
    sent, picked_out, fetched_out, act_out, pre_grad_out,
):
    ids = jnp.concatenate([column_of(ids_ref[u : u + 1]) for u in range(USERS_HERE)], axis=0)
    owner = ids // ITEMS_HERE
    within = ids - owner * ITEMS_HERE
    chip = owner // 2
    place = chip * ITEMS_HERE + within
    mine = (owner - chip * 2) == core[0]
    lanes = lax.broadcasted_iota(jnp.int32, (ROWS, CHIPS * ITEMS_HERE), 1)
    pick_own = (lanes == jnp.where(mine, place, -1)).astype(F32).astype(BF)
    pick_other = (lanes == jnp.where(mine, -1, place)).astype(F32).astype(BF)

    def rows_of(ref):
        low = ref[:, 0:32, :].reshape(CHIPS * ITEMS_HERE, 128)
        high = ref[:, 32:64, :].reshape(CHIPS * ITEMS_HERE, 128)
        return jnp.concatenate([low, high], axis=1)

    picked = (dot_nn(pick_own, rows_of(own)) + dot_nn(pick_other, rows_of(other))).astype(BF)
    fetched = dot_nn(picked[:, 0:C], project[...]).astype(BF)
    pre = dot_nn(fetched, up[...])
    scale = 0.7978845608028654
    square = pre * pre
    bent = jnp.tanh(scale * pre * (1.0 + 0.044715 * square))
    gate = 0.5 * (1.0 + bent)
    picked_out[...] = picked
    fetched_out[...] = fetched
    act_out[...] = (pre * gate).astype(BF)
    slope = gate + 0.5 * pre * (1.0 - bent * bent) * (scale * (1.0 + 3 * 0.044715 * square))
    _, length = per_user(lengths)
    shared = cot[...] / length[0:4].astype(F32)
    shared_half = shared.astype(BF)
    act_grad = dot_nt(jnp.concatenate([shared_half, shared_half], axis=0), down[...])
    position = lax.broadcasted_iota(jnp.int32, (LENGTH, 1), 0)
    pre_parts, base_parts = [], []
    for u in range(USERS_HERE):
        alive = (position < lengths[u]).astype(F32)
        pre_parts.append(alive * act_grad[u : u + 1] * slope[u * LENGTH : (u + 1) * LENGTH])
        base_parts.append(alive * shared[u : u + 1])
    pre_grad = jnp.concatenate(pre_parts, axis=0).astype(BF)
    pre_grad_out[...] = pre_grad
    rows_grad = jnp.concatenate(base_parts, axis=0) + dot_nt(pre_grad, up[...])
    rows_coarse = rows_grad.astype(BF)
    rows_fine = (rows_grad - rows_coarse.astype(F32)).astype(BF)
    low = dot_nt(rows_coarse, project[0:128]) + dot_nt(rows_fine, project[0:128])
    high = dot_nt(rows_coarse, project[64:192]) + dot_nt(rows_fine, project[64:192])
    lane = lax.broadcasted_iota(jnp.int32, (ROWS, 128), 1)
    tag = within.astype(F32)
    low = jnp.where(lane < 96, low, jnp.where(lane == 96, tag, 0.0)).astype(BF)
    high = jnp.where(lane >= 32, high, jnp.where(lane == 0, tag, 0.0)).astype(BF)

    across = lax.broadcasted_iota(jnp.int32, (ROWS, ROWS), 1)
    down_rows = lax.broadcasted_iota(jnp.int32, (ROWS, ROWS), 0)
    owner_row = jnp.sum(jnp.where(across == down_rows, owner.astype(F32), 0.0), axis=0, keepdims=True).astype(jnp.int32)
    earlier = down_rows < across
    rank = jnp.sum(((owner == owner_row) & earlier).astype(F32), axis=0, keepdims=True).astype(jnp.int32)
    slot = owner_row * 8 + rank
    sent_at = lax.broadcasted_iota(jnp.int32, (DEVICES * 8, ROWS), 0)
    put_low = (sent_at == slot).astype(F32).astype(BF)
    put_high = (sent_at == slot + CAPACITY).astype(F32).astype(BF)
    back = (dot_nn(put_low, low) + dot_nn(put_high, high)).astype(BF)
    sent[...] = back.reshape(DEVICES, 8, 128)


def tower_sums(
    core, lengths, picked, fetched, act, pre_grad, down,
    up_keep, up_send, factors, user_vec,
    halves,
):
    user, length = per_user(lengths)
    at = lax.broadcasted_iota(jnp.int32, (8, ROWS), 1)
    live = ((at // LENGTH == user) & (at - user * LENGTH < length)).astype(F32).astype(BF)
    act_sum = dot_nn(live, act[...])
    picked_sum = dot_nn(live, picked[...])
    pieces = [act_sum[0:4, j * 128 : (j + 1) * 128] for j in range(8)]
    pieces += [picked_sum[0:4, j * 128 : (j + 1) * 128] for j in range(2)]
    factors[...] = jnp.concatenate(pieces, axis=0).astype(BF)
    coarse = act_sum.astype(BF)
    fine = (act_sum - coarse.astype(F32)).astype(BF)
    mixed = dot_nn(live, fetched[...]) + dot_nn(coarse, down[...]) + dot_nn(fine, down[...])
    user_vec[...] = (mixed / length.astype(F32))[0:4]
    up_grad = dot_tn(picked[...], pre_grad[...]).astype(BF)
    for j in range(FH // 128):
        halves[j // 4, (j % 4) * 256 : (j % 4 + 1) * 256] = up_grad[:, j * 128 : (j + 1) * 128]
    up_keep[...] = halves[core[0]]
    up_send[...] = halves[1 - core[0]]


def conv_backward(
    core, back, x, counts_row, s1, t1, p1, e2, s2, t2, p2, g1, d1, sp1, n1, h1, o1, g2, d2, sp2, n2, h2,
    keep, send,
    spatial_grad, wide, small, halves,
):
    counts = column_of(counts_row[...])
    taps1 = s1[...].astype(F32)
    taps2 = s2[...].astype(F32)
    frame1 = t1[...].astype(F32)
    frame2 = t2[...].astype(F32)

    def tile_sum(v):
        return jnp.sum(v.reshape(-1, 8, E), axis=0)

    small[...] = jnp.zeros(small.shape, F32)
    wide[...] = jnp.zeros(wide.shape, F32)
    got = back[...].reshape(DEVICES * 8, 128)
    row = lax.broadcasted_iota(jnp.int32, (DEVICES * 8, 1), 0)
    is_low = (row & 7) < CAPACITY
    got_f = got.astype(F32)
    tag = jnp.where(is_low, got_f[:, 96:97], got_f[:, 0:1]).astype(jnp.int32)
    named = tag == lax.broadcasted_iota(jnp.int32, (DEVICES * 8, ITEMS_HERE), 1)
    low = dot_tn((named & is_low).astype(F32).astype(BF), got)
    high = dot_tn((named & ~is_low).astype(F32).astype(BF), got)
    pooled_grad = jnp.concatenate([low[:, 0:96], high[:, 32:128]], axis=1)
    shared = pooled_grad / counts.astype(F32)
    out_grad = jnp.concatenate(
        [(shared * (f < counts).astype(F32)).astype(BF) for f in range(FRAMES)], axis=0
    )
    wide[576:768, 0:E] = dot_tn(out_grad, n2[...].reshape(FRAMES * ITEMS_HERE, E))
    summed_grad = dot_nn(out_grad, p2[...]).reshape(FRAMES, ITEMS_HERE, E) * h2[...].astype(F32)
    spread = []
    for f in range(FRAMES):
        total = summed_grad[f] * frame2[1]
        if f + 1 < FRAMES:
            total = total + summed_grad[f + 1] * frame2[0]
        if f > 0:
            total = total + summed_grad[f - 1] * frame2[2]
        spread.append(total)
    for k in range(3):
        total = jnp.zeros((8, E), F32)
        for f in range(FRAMES):
            if 0 <= f + k - 1 < FRAMES:
                total = total + tile_sum(sp2[f + k - 1].astype(F32) * summed_grad[f])
        small[21 + k] = total
    parts = []
    for f in range(FRAMES):
        for cell, tap in LINKS_SECOND:
            small[12 + tap] += tile_sum(g2[f * 4 + cell].astype(F32) * spread[f])
            parts.append((spread[f] * taps2[tap] * d2[f * 4 + cell].astype(F32)).astype(BF))
    grown_grad = jnp.concatenate(parts, axis=0)
    wide[384:576, 0:E] = dot_tn(o1[...], grown_grad)
    first_grad = dot_nt(grown_grad, e2[...]).astype(BF)
    wide[192:384, 0:E] = dot_tn(first_grad, n1[...].reshape(FRAMES * 4 * ITEMS_HERE, E))
    narrow_grad = dot_nn(first_grad, p1[...]).reshape(FRAMES, 4, ITEMS_HERE, E)
    summed_grad = [narrow_grad[f] * h1[f * 4 : f * 4 + 4].astype(F32) for f in range(FRAMES)]
    for k in range(3):
        total = jnp.zeros((8, E), F32)
        for f in range(FRAMES):
            if 0 <= f + k - 1 < FRAMES:
                total = total + tile_sum(sp1[f + k - 1].astype(F32) * summed_grad[f])
        small[9 + k] = total
    for f in range(FRAMES):
        total = summed_grad[f] * frame1[1]
        if f + 1 < FRAMES:
            total = total + summed_grad[f + 1] * frame1[0]
        if f > 0:
            total = total + summed_grad[f - 1] * frame1[2]
        spatial_grad[f] = total

    def grow_back(f, _):
        live = f < counts
        x_f = x[pl.ds(f * CELLS, CELLS)]
        x_f = jnp.where(live[None], x_f, jnp.zeros_like(x_f)).reshape(CELLS * ITEMS_HERE, C)
        sums = [jnp.zeros((8, E), F32)] * 9
        grads = [jnp.zeros((ITEMS_HERE, E), F32)] * CELLS
        for out_cell, in_cell, tap in LINKS_FIRST:
            from_out = spatial_grad[f, out_cell]
            grads[in_cell] = grads[in_cell] + from_out * taps1[tap]
            sums[tap] = sums[tap] + tile_sum(g1[f * CELLS + in_cell].astype(F32) * from_out)
        for tap in range(9):
            small[tap] += sums[tap]
        grads = [(grads[cell] * d1[f * CELLS + cell].astype(F32)).astype(BF) for cell in range(CELLS)]
        wide[0:192, 0:E] += dot_tn(x_f, jnp.concatenate(grads, axis=0))
        return 0

    lax.fori_loop(0, FRAMES, grow_back, 0)
    sums = jnp.sum(small[...], axis=1).astype(BF)
    put = lax.broadcasted_iota(jnp.int32, (32, 128), 1) == lax.broadcasted_iota(jnp.int32, (32, 128), 0) + 64
    wide[0:E, 384:512] += dot_tn(sums, put.astype(F32).astype(BF))
    for j in range(4):
        halves[j // 2, (j % 2) * 768 : (j % 2 + 1) * 768] = wide[:, j * 128 : (j + 1) * 128].astype(BF)
    keep[...] = halves[core[0]]
    send[...] = halves[1 - core[0]]


def merge(conv_a, conv_b, up_a, up_b, factors, out):
    conv = (conv_a[...].astype(F32) + conv_b[...].astype(F32)).astype(BF)
    up = (up_a[...].astype(F32) + up_b[...].astype(F32)).astype(BF)
    rows = [conv.reshape(CHIPS, 24, 128), up.reshape(CHIPS, 16, 128)]
    rows.append(jnp.broadcast_to(factors[...][None], (CHIPS, 40, 128)))
    out[...] = jnp.concatenate(rows, axis=1)


def sum_chips(third, out):
    total = jnp.sum(third[:, 0:40, :].astype(F32), axis=0).astype(BF)
    out[...] = jnp.broadcast_to(total[None], out.shape)


def finish_low_rank(own, other, third, third_other, grad_down, item_base):
    row = lax.broadcasted_iota(jnp.int32, (CHIPS * 8, 128), 0) & 7
    lane = lax.broadcasted_iota(jnp.int32, (CHIPS * 8, 128), 1)
    even = []
    for src in (own, other):
        parts = []
        for k in range(4):
            got = src[:, 32 + 8 * k : 40 + 8 * k, :].reshape(CHIPS * 8, 128).astype(F32)
            left = pltpu.roll(got, 64, 1)
            right = pltpu.roll(got, CHIPS * 8 - 4, 0)
            parts.append(jnp.where(row < 4, jnp.where(lane < 64, left, right), 0.0))
        even.append(jnp.concatenate(parts, axis=1))
    odd = jnp.concatenate([pltpu.roll(v, 4, 0) for v in even], axis=0).astype(BF)
    even = jnp.concatenate(even, axis=0).astype(BF)
    for j in range(5):
        cut = slice(40 + 8 * j, 48 + 8 * j)
        left = jnp.concatenate(
            [src[:, cut, :].reshape(CHIPS * 8, 128) for src in (third, third_other)], axis=0
        )
        first, second = dot_tn(left, even), dot_tn(left, odd)
        if j < 4:
            grad_down[j * 256 : j * 256 + 128] = first
            grad_down[j * 256 + 128 : j * 256 + 256] = second
        else:
            item_base[0:128] = first
            item_base[128:C] = second[0:64]


def finish(
    core, mine, theirs, item_base, project, up,
    ge1, gs1, gt1, gp1, ge2, gs2, gt2, gp2, grad_item, grad_up,
    halves,
):
    halves[core[0]] = mine[...]
    halves[1 - core[0]] = theirs[...]
    for j in range(4):
        width = min(128, E - j * 128)
        part = halves[j // 2, :, 0:24, :].reshape(1536, 128)[(j % 2) * 768 : (j % 2 + 1) * 768].astype(F32)
        cut = slice(j * 128, j * 128 + width)
        for i, out in enumerate((ge1, gp1, ge2, gp2)):
            out[:, cut] = part[i * 192 : (i + 1) * 192, 0:width]
    same = lax.broadcasted_iota(jnp.int32, (E, E), 0) == lax.broadcasted_iota(jnp.int32, (E, E), 1)
    small = dot_tn(part[0:E].astype(BF), same.astype(F32).astype(BF))
    gs1[...] = small[64:73]
    gt1[...] = small[73:76]
    gs2[...] = small[76:85]
    gt2[...] = small[85:88]
    item = item_base[...]
    for j in range(FH // 128):
        part = halves[j // 4, :, 24:40, :].reshape(1024, 128)[(j % 4) * 256 : (j % 4) * 256 + C]
        cut = slice(j * 128, (j + 1) * 128)
        grad_up[:, cut] = dot_tn(project[...], part)
        item = item + dot_nt(part, up[:, cut])
    grad_item[...] = item


def shape(dims, dtype=BF):
    return jax.ShapeDtypeStruct(dims, dtype)


def call(kernel, outs, scratch=(), smem=0, flops=10**9, moved=10**7):
    def run(*args):
        return pl.pallas_call(
            kernel,
            out_shape=outs,
            in_specs=[
                pl.BlockSpec(memory_space=pltpu.SMEM if i < smem else pltpu.VMEM)
                for i in range(len(args))
            ],
            out_specs=[pl.BlockSpec(memory_space=pltpu.VMEM)] * len(outs),
            scratch_shapes=list(scratch),
            cost_estimate=pl.CostEstimate(flops=flops, bytes_accessed=moved, transcendentals=10**6),
            compiler_params=pltpu.CompilerParams(vmem_limit_bytes=32 * 1024 * 1024),
        )(*args)

    return run


def local(
    clips, clip_counts, histories, lengths, user_cotangent,
    expand_first, spatial_first, temporal_first, project_first,
    expand_second, spatial_second, temporal_second, project_second,
    item_project, tower_up, tower_down,
):
    same_core = [[i for i in range(DEVICES) if i % 2 == c] for c in range(2)]
    core = (lax.axis_index("seq") % 2).reshape(1)

    def across_chips(v):
        return lax.all_to_all(v, AXES, 0, 0, axis_index_groups=same_core, tiled=True)

    def swap(v):
        return lax.ppermute(v, "seq", [(i, i ^ 1) for i in range(8)])

    x = clips.reshape(ITEMS_HERE, FRAMES * CELLS, C).transpose(1, 0, 2)
    counts = clip_counts.reshape(1, ITEMS_HERE)
    weights = (
        spatial_first, temporal_first, project_first.T,
        expand_second, spatial_second, temporal_second, project_second.T,
    )
    n = ITEMS_HERE
    framed = [pltpu.VMEM((FRAMES + 2, 4, n, E), F32), pltpu.VMEM((FRAMES + 2, n, E), F32)]
    (block,) = call(conv_forward, [shape((CHIPS, 64, 128))], framed, 1)(
        lengths, x, counts, user_cotangent, expand_first, *weights
    )
    kept = call(
        conv_forward,
        [
            shape((64, n, E)), shape((64, n, E)), shape((4, 4, n, E)), shape((16, n, E)), shape((16, n, E)),
            shape((512, C)), shape((16, n, E)), shape((16, n, E)), shape((4, n, E)), shape((4, n, E)), shape((4, n, E)),
        ],
        framed,
        1,
    )(lengths, x, counts, user_cotangent, expand_first, *weights)
    own = across_chips(block)
    other = swap(own)
    sent, *seen = call(
        tower,
        [shape((DEVICES, 8, 128)), shape((ROWS, 256)), shape((ROWS, D)), shape((ROWS, FH)), shape((ROWS, FH))],
        smem=2,
    )(core, lengths, own, other, histories, user_cotangent, item_project, tower_up, tower_down)
    back = lax.all_to_all(sent, AXES, 0, 0, tiled=True)
    up_keep, up_send, factors, user_vec = call(
        tower_sums,
        [shape((1024, 128)), shape((1024, 128)), shape((40, 128)), shape((USERS_HERE, D), F32)],
        [pltpu.VMEM((2, 1024, 128), BF)],
        2,
    )(core, lengths, *seen, tower_down)
    up_other = swap(up_send)
    conv_keep, conv_send = call(
        conv_backward,
        [shape((1536, 128)), shape((1536, 128))],
        [
            pltpu.VMEM((4, 4, n, E), F32),
            pltpu.VMEM((768, 512), F32),
            pltpu.VMEM((32, 8, E), F32),
            pltpu.VMEM((2, 1536, 128), BF),
        ],
        1,
    )(core, back, x, counts, *weights, *kept)
    (third,) = call(merge, [shape((CHIPS, 80, 128))])(conv_keep, swap(conv_send), up_keep, up_other, factors)
    third = across_chips(third)
    (fourth,) = call(sum_chips, [shape((CHIPS, 40, 128))])(third)
    fourth = across_chips(fourth)
    grad_down, item_base = call(finish_low_rank, [shape((FH, D), F32), shape((C, D), F32)])(
        own, other, third, swap(third)
    )
    *conv_grads, grad_item, grad_up = call(
        finish,
        [shape((C, E), F32), shape((9, E), F32), shape((3, E), F32), shape((C, E), F32)] * 2
        + [shape((C, D), F32), shape((D, FH), F32)],
        [pltpu.VMEM((2, CHIPS, 40, 128), BF)],
        1,
    )(core, fourth, swap(fourth), item_base, item_project, tower_up)
    conv_grads[3] = conv_grads[3].T
    conv_grads[7] = conv_grads[7].T
    return (user_vec, *conv_grads, grad_item, grad_up, grad_down)


def solution(mesh):
    spread = P(AXES)
    return jax.shard_map(
        local,
        mesh=mesh,
        in_specs=(spread,) * 5 + (P(),) * 11,
        out_specs=(spread,) + (P(),) * 11,
        check_vma=False,
    )
```

```python
import jax
import jax.numpy as jnp
from jax import lax
from jax.experimental import pallas as pl
from jax.experimental.pallas import tpu as pltpu
from jax.sharding import PartitionSpec as P

BF = jnp.bfloat16
F32 = jnp.float32
AXES = ("bulk", "seq")
C, E, D, FH = 192, 432, 512, 1024
FRAMES, SIDE, ITEMS_HERE, USERS_HERE, LENGTH = 4, 4, 32, 4, 64
DEVICES, CHIPS, CAPACITY = 128, 64, 4
ROWS = USERS_HERE * LENGTH
CELLS = SIDE * SIDE
HALF = 2
LINKS_FIRST = [
    (HALF * p + q, SIDE * (2 * p + a - 1) + 2 * q + b - 1, 3 * a + b)
    for p in range(HALF)
    for q in range(HALF)
    for a in range(3)
    for b in range(3)
    if 0 <= 2 * p + a - 1 < SIDE and 0 <= 2 * q + b - 1 < SIDE
]
LINKS_SECOND = [(0, 4), (1, 5), (2, 7), (3, 8)]


def dot_nn(a, b):
    return lax.dot_general(a, b, (((1,), (0,)), ((), ())), preferred_element_type=F32)


def dot_nt(a, b):
    return lax.dot_general(a, b, (((1,), (1,)), ((), ())), preferred_element_type=F32)


def dot_tn(a, b):
    return lax.dot_general(a, b, (((0,), (0,)), ((), ())), preferred_element_type=F32)


def silu_and_slope(v):
    gate = 0.5 * jnp.tanh(0.5 * v) + 0.5
    value = v * gate
    return value, gate + value - value * gate


def column_of(row):
    n = row.shape[1]
    same = lax.broadcasted_iota(jnp.int32, (n, n), 0) == lax.broadcasted_iota(jnp.int32, (n, n), 1)
    return jnp.sum(jnp.where(same, row.astype(F32), 0.0), axis=1, keepdims=True).astype(jnp.int32)


def per_user(lengths):
    user = lax.broadcasted_iota(jnp.int32, (8, 1), 0)
    length = jnp.ones((8, 1), jnp.int32)
    for u in range(USERS_HERE):
        length = jnp.where(user == u, lengths[u], length)
    return user, length


def conv_forward(
    lengths, x, counts_row, cot, e1, s1, t1, p1, e2, s2, t2, p2, *rest,
):
    *kept, framed1, framed2 = rest
    block = None
    if len(kept) == 1:
        (block,) = kept
    else:
        taps, g1, d1, sp1, n1, h1, o1, g2, d2, sp2, n2, h2 = kept
    counts = column_of(counts_row[...])
    zero4 = jnp.zeros((HALF * HALF, ITEMS_HERE, E), F32)
    framed1[0] = zero4
    framed1[FRAMES + 1] = zero4
    zero1 = jnp.zeros((ITEMS_HERE, E), F32)
    framed2[0] = zero1
    framed2[FRAMES + 1] = zero1
    taps1 = s1[...].astype(F32)
    taps2 = s2[...].astype(F32)
    frame1 = t1[...].astype(F32)
    frame2 = t2[...].astype(F32)
    if block is None:
        taps[...] = jnp.zeros((56, E), F32)
        for at, ref in ((0, s1), (9, t1), (12, s2), (21, t2)):
            taps[at : at + ref.shape[0]] = ref[...].astype(F32)
        taps[24:56, 0:128] = jnp.broadcast_to(counts.astype(F32), (ITEMS_HERE, 128))

    if block is None:
        x.ready(), e1.ready()

    def grow(f, _):
        live = f < counts
        x_f = x[pl.ds(f * CELLS, CELLS)]
        x_f = jnp.where(live[None], x_f, jnp.zeros_like(x_f))
        pre = dot_nn(x_f.reshape(CELLS * ITEMS_HERE, C), e1[...])
        value, slope = silu_and_slope(pre)
        value = value.astype(BF).reshape(CELLS, ITEMS_HERE, E)
        if block is None:
            g1[pl.ds(f * CELLS, CELLS)] = value
            d1[pl.ds(f * CELLS, CELLS)] = slope.astype(BF).reshape(CELLS, ITEMS_HERE, E)
        outs = [jnp.zeros((ITEMS_HERE, E), F32)] * 4
        for out_cell, in_cell, tap in LINKS_FIRST:
            outs[out_cell] = outs[out_cell] + value[in_cell].astype(F32) * taps1[tap]
        for out_cell in range(4):
            framed1[f + 1, out_cell] = outs[out_cell]
            if block is None:
                sp1[f, out_cell] = outs[out_cell].astype(BF)
        return 0

    lax.fori_loop(0, FRAMES, grow, 0)
    narrow = []
    for f in range(FRAMES):
        summed = framed1[f] * frame1[0] + framed1[f + 1] * frame1[1] + framed1[f + 2] * frame1[2]
        value, slope = silu_and_slope(summed)
        narrow.append(value.astype(BF))
        if block is None:
            h1[f * 4 : f * 4 + 4] = slope.astype(BF)
    narrow = jnp.concatenate(narrow, axis=0)
    first = dot_nt(narrow.reshape(FRAMES * 4 * ITEMS_HERE, E), p1[...]).astype(BF)
    value, slope = silu_and_slope(dot_nn(first, e2[...]))
    value = value.astype(BF).reshape(FRAMES * 4, ITEMS_HERE, E)
    if block is None:
        n1[...] = narrow
        o1[...] = first
        g2[...] = value
        d2[...] = slope.astype(BF).reshape(FRAMES * 4, ITEMS_HERE, E)
    for f in range(FRAMES):
        total = jnp.zeros((ITEMS_HERE, E), F32)
        for cell, tap in LINKS_SECOND:
            total = total + value[f * 4 + cell].astype(F32) * taps2[tap]
        framed2[f + 1] = total
        if block is None:
            sp2[f] = total.astype(BF)
    narrow = []
    for f in range(FRAMES):
        summed = framed2[f] * frame2[0] + framed2[f + 1] * frame2[1] + framed2[f + 2] * frame2[2]
        value, slope = silu_and_slope(summed)
        narrow.append(value.astype(BF))
        if block is None:
            n2[f] = value.astype(BF)
            h2[f] = slope.astype(BF)
    if block is None:
        return
    second = dot_nt(jnp.concatenate(narrow, axis=0), p2[...]).astype(BF)
    pooled = jnp.zeros((ITEMS_HERE, C), F32)
    for f in range(FRAMES):
        live = (f < counts).astype(F32)
        pooled = pooled + live * second[f * ITEMS_HERE : (f + 1) * ITEMS_HERE].astype(F32)
    pooled = pooled / counts.astype(F32)
    _, length = per_user(lengths)
    shared = cot[...] / length[0:4].astype(F32)
    pieces = []
    for k in range(8):
        piece = shared[:, (k // 2) * 128 : (k // 2 + 1) * 128]
        pieces.append(piece if k % 2 else pltpu.roll(piece, 64, 1))
    lane = lax.broadcasted_iota(jnp.int32, (ITEMS_HERE, 128), 1)
    shared = jnp.concatenate(pieces, axis=0)
    high = jnp.concatenate([pooled[:, 128:192], pooled[:, 0:64]], axis=1)
    rows = jnp.concatenate([pooled[:, 0:128], jnp.where(lane < 64, high, shared)], axis=0).astype(BF)
    block[...] = jnp.broadcast_to(rows[None], (CHIPS, 64, 128))


def tower(
    core, lengths, own, other, ids_ref, cot, project, up, down,
    sent, picked_out, fetched_out, act_out, pre_grad_out, mixed_own, mixed_other,
):
    ids = jnp.concatenate([column_of(ids_ref[u : u + 1]) for u in range(USERS_HERE)], axis=0)
    owner = ids // ITEMS_HERE
    within = ids - owner * ITEMS_HERE
    chip = owner // 2
    place = chip * ITEMS_HERE + within
    mine = (owner - chip * 2) == core[0]
    lanes = lax.broadcasted_iota(jnp.int32, (ROWS, CHIPS * ITEMS_HERE), 1)
    pick_own = (lanes == jnp.where(mine, place, -1)).astype(F32).astype(BF)
    pick_other = (lanes == jnp.where(mine, -1, place)).astype(F32).astype(BF)

    def rows_of(ref):
        low = ref[:, 0:32, :].reshape(CHIPS * ITEMS_HERE, 128)
        high = ref[:, 32:64, :].reshape(CHIPS * ITEMS_HERE, 128)
        return jnp.concatenate([low, high], axis=1)

    own, other = own.ready(), other.ready()
    for late in (project, up, down):
        late.begin()
    mixed_own.leave(own.at[:, 32:64, :])
    mixed_other.leave(other.at[:, 32:64, :])
    picked = (dot_nn(pick_own, rows_of(own)) + dot_nn(pick_other, rows_of(other))).astype(BF)
    fetched = dot_nn(picked[:, 0:C], project[...]).astype(BF)
    pre = dot_nn(fetched, up[...])
    scale = 0.7978845608028654
    square = pre * pre
    bent = jnp.tanh(scale * pre * (1.0 + 0.044715 * square))
    gate = 0.5 * (1.0 + bent)
    picked_out[...] = picked
    fetched_out[...] = fetched
    act_out[...] = (pre * gate).astype(BF)
    for out in (picked_out, fetched_out, act_out):
        out.leave()
    slope = gate + 0.5 * pre * (1.0 - bent * bent) * (scale * (1.0 + 3 * 0.044715 * square))
    _, length = per_user(lengths)
    shared = cot[...] / length[0:4].astype(F32)
    shared_half = shared.astype(BF)
    act_grad = dot_nt(jnp.concatenate([shared_half, shared_half], axis=0), down[...])
    position = lax.broadcasted_iota(jnp.int32, (LENGTH, 1), 0)
    pre_parts, base_parts = [], []
    for u in range(USERS_HERE):
        alive = (position < lengths[u]).astype(F32)
        pre_parts.append(alive * act_grad[u : u + 1] * slope[u * LENGTH : (u + 1) * LENGTH])
        base_parts.append(alive * shared[u : u + 1])
    pre_grad = jnp.concatenate(pre_parts, axis=0).astype(BF)
    pre_grad_out[...] = pre_grad
    pre_grad_out.leave()
    rows_grad = jnp.concatenate(base_parts, axis=0) + dot_nt(pre_grad, up[...])
    rows_coarse = rows_grad.astype(BF)
    rows_fine = (rows_grad - rows_coarse.astype(F32)).astype(BF)
    low = dot_nt(rows_coarse, project[0:128]) + dot_nt(rows_fine, project[0:128])
    high = dot_nt(rows_coarse, project[64:192]) + dot_nt(rows_fine, project[64:192])
    lane = lax.broadcasted_iota(jnp.int32, (ROWS, 128), 1)
    tag = within.astype(F32)
    low = jnp.where(lane < 96, low, jnp.where(lane == 96, tag, 0.0)).astype(BF)
    high = jnp.where(lane >= 32, high, jnp.where(lane == 0, tag, 0.0)).astype(BF)

    across = lax.broadcasted_iota(jnp.int32, (ROWS, ROWS), 1)
    down_rows = lax.broadcasted_iota(jnp.int32, (ROWS, ROWS), 0)
    owner_row = jnp.sum(jnp.where(across == down_rows, owner.astype(F32), 0.0), axis=0, keepdims=True).astype(jnp.int32)
    earlier = down_rows < across
    rank = jnp.sum(((owner == owner_row) & earlier).astype(F32), axis=0, keepdims=True).astype(jnp.int32)
    slot = owner_row * 8 + rank
    sent_at = lax.broadcasted_iota(jnp.int32, (DEVICES * 8, ROWS), 0)
    put_low = (sent_at == slot).astype(F32).astype(BF)
    put_high = (sent_at == slot + CAPACITY).astype(F32).astype(BF)
    back = (dot_nn(put_low, low) + dot_nn(put_high, high)).astype(BF)
    sent[...] = back.reshape(DEVICES, 8, 128)


def tower_sums(
    core, lengths, picked, fetched, act, pre_grad, down,
    up_keep, up_send, factors, user_vec,
    halves,
):
    user, length = per_user(lengths)
    at = lax.broadcasted_iota(jnp.int32, (8, ROWS), 1)
    live = ((at // LENGTH == user) & (at - user * LENGTH < length)).astype(F32).astype(BF)
    act_sum = dot_nn(live, act[...])
    picked_sum = dot_nn(live, picked[...])
    pieces = [act_sum[0:4, j * 128 : (j + 1) * 128] for j in range(8)]
    pieces += [picked_sum[0:4, j * 128 : (j + 1) * 128] for j in range(2)]
    factors[...] = jnp.concatenate(pieces + [jnp.zeros((8, 128), F32)], axis=0).astype(BF)
    coarse = act_sum.astype(BF)
    fine = (act_sum - coarse.astype(F32)).astype(BF)
    mixed = dot_nn(live, fetched[...]) + dot_nn(coarse, down[...]) + dot_nn(fine, down[...])
    user_vec[...] = (mixed / length.astype(F32))[0:4]
    up_grad = dot_tn(picked[...], pre_grad[...]).astype(BF)
    for j in range(FH // 128):
        halves[j // 4, (j % 4) * 256 : (j % 4 + 1) * 256] = up_grad[:, j * 128 : (j + 1) * 128]
    up_keep.leave(halves.at[core[0]])
    up_send.leave(halves.at[1 - core[0]])


def conv_backward(
    core, back, taps, n2, p2, h2, sp2, g2, d2, o1, e2, n1, p1, h1, sp1, x, g1, d1,
    keep, send,
    spatial_grad, wide, small, halves,
):
    taps1, frame1, taps2, frame2 = taps[0:9], taps[9:12], taps[12:21], taps[21:24]
    counts = taps[24:56, 0:1]
    for late in (n2, p2, h2, sp2, g2, d2, o1, e2):
        late.ready()
    for late in (x, g1, d1):
        late.begin()

    def tile_sum(v):
        return jnp.sum(v.reshape(-1, 8, E), axis=0)

    small[...] = jnp.zeros(small.shape, F32)
    wide[...] = jnp.zeros(wide.shape, F32)
    got = back[...].reshape(DEVICES * 8, 128)
    row = lax.broadcasted_iota(jnp.int32, (DEVICES * 8, 1), 0)
    is_low = (row & 7) < CAPACITY
    got_f = got.astype(F32)
    tag = jnp.where(is_low, got_f[:, 96:97], got_f[:, 0:1]).astype(jnp.int32)
    named = tag == lax.broadcasted_iota(jnp.int32, (DEVICES * 8, ITEMS_HERE), 1)
    low = dot_tn((named & is_low).astype(F32).astype(BF), got)
    high = dot_tn((named & ~is_low).astype(F32).astype(BF), got)
    pooled_grad = jnp.concatenate([low[:, 0:96], high[:, 32:128]], axis=1)
    shared = pooled_grad / counts
    out_grad = jnp.concatenate(
        [(shared * (counts > f).astype(F32)).astype(BF) for f in range(FRAMES)], axis=0
    )
    wide[576:768, 0:E] = dot_tn(out_grad, n2[...].reshape(FRAMES * ITEMS_HERE, E))
    summed_grad = dot_nn(out_grad, p2[...]).reshape(FRAMES, ITEMS_HERE, E) * h2[...].astype(F32)
    spread = []
    for f in range(FRAMES):
        total = summed_grad[f] * frame2[1]
        if f + 1 < FRAMES:
            total = total + summed_grad[f + 1] * frame2[0]
        if f > 0:
            total = total + summed_grad[f - 1] * frame2[2]
        spread.append(total)
    for k in range(3):
        total = jnp.zeros((8, E), F32)
        for f in range(FRAMES):
            if 0 <= f + k - 1 < FRAMES:
                total = total + tile_sum(sp2[f + k - 1].astype(F32) * summed_grad[f])
        small[21 + k] = total
    parts = []
    for f in range(FRAMES):
        for cell, tap in LINKS_SECOND:
            small[12 + tap] += tile_sum(g2[f * 4 + cell].astype(F32) * spread[f])
            parts.append((spread[f] * taps2[tap] * d2[f * 4 + cell].astype(F32)).astype(BF))
    grown_grad = jnp.concatenate(parts, axis=0)
    wide[384:576, 0:E] = dot_tn(o1[...], grown_grad)
    first_grad = dot_nt(grown_grad, e2[...]).astype(BF)
    wide[192:384, 0:E] = dot_tn(first_grad, n1[...].reshape(FRAMES * 4 * ITEMS_HERE, E))
    narrow_grad = dot_nn(first_grad, p1[...]).reshape(FRAMES, 4, ITEMS_HERE, E)
    summed_grad = [narrow_grad[f] * h1[f * 4 : f * 4 + 4].astype(F32) for f in range(FRAMES)]
    for k in range(3):
        total = jnp.zeros((8, E), F32)
        for f in range(FRAMES):
            if 0 <= f + k - 1 < FRAMES:
                total = total + tile_sum(sp1[f + k - 1].astype(F32) * summed_grad[f])
        small[9 + k] = total
    for f in range(FRAMES):
        total = summed_grad[f] * frame1[1]
        if f + 1 < FRAMES:
            total = total + summed_grad[f + 1] * frame1[0]
        if f > 0:
            total = total + summed_grad[f - 1] * frame1[2]
        spatial_grad[f] = total

    x.ready(), g1.ready(), d1.ready()

    def grow_back(f, _):
        live = counts > lax.convert_element_type(f, F32)
        x_f = x[pl.ds(f * CELLS, CELLS)]
        x_f = jnp.where(live[None], x_f, jnp.zeros_like(x_f)).reshape(CELLS * ITEMS_HERE, C)
        sums = [jnp.zeros((8, E), F32)] * 9
        grads = [jnp.zeros((ITEMS_HERE, E), F32)] * CELLS
        for out_cell, in_cell, tap in LINKS_FIRST:
            from_out = spatial_grad[f, out_cell]
            grads[in_cell] = grads[in_cell] + from_out * taps1[tap]
            sums[tap] = sums[tap] + tile_sum(g1[f * CELLS + in_cell].astype(F32) * from_out)
        for tap in range(9):
            small[tap] += sums[tap]
        grads = [(grads[cell] * d1[f * CELLS + cell].astype(F32)).astype(BF) for cell in range(CELLS)]
        wide[0:192, 0:E] += dot_tn(x_f, jnp.concatenate(grads, axis=0))
        return 0

    lax.fori_loop(0, FRAMES, grow_back, 0)
    sums = jnp.sum(small[...], axis=1).astype(BF)
    put = lax.broadcasted_iota(jnp.int32, (32, 128), 1) == lax.broadcasted_iota(jnp.int32, (32, 128), 0) + 64
    wide[0:E, 384:512] += dot_tn(sums, put.astype(F32).astype(BF))
    for j in range(4):
        halves[j // 2, (j % 2) * 768 : (j % 2 + 1) * 768] = wide[:, j * 128 : (j + 1) * 128].astype(BF)
    keep[...] = halves[core[0]]
    send[...] = halves[1 - core[0]]


def merge(conv_a, conv_b, up_a, up_b, factors, out):
    conv = (conv_a[...].astype(F32) + conv_b[...].astype(F32)).astype(BF)
    up = (up_a[...].astype(F32) + up_b[...].astype(F32)).astype(BF)
    out[:, 0:24, :] = conv.reshape(CHIPS, 24, 128)
    out[:, 24:40, :] = up.reshape(CHIPS, 16, 128)
    out[:, 40:80, :] = jnp.broadcast_to(factors[0:40][None], (CHIPS, 40, 128))


def sum_chips(third, out, factors):
    factors[...] = third[:, 40:80, :]
    factors.leave()
    total = jnp.sum(third[:, 0:40, :].astype(F32), axis=0).astype(BF)
    out[...] = jnp.broadcast_to(total[None], (CHIPS, 40, 128))


def finish_low_rank(own, other, factors, factors_other, grad_down, item_base):
    row = lax.broadcasted_iota(jnp.int32, (CHIPS * 8, 128), 0) & 7
    lane = lax.broadcasted_iota(jnp.int32, (CHIPS * 8, 128), 1)
    even = []
    for src in (own, other):
        parts = []
        for k in range(4):
            got = src[:, 8 * k : 8 * k + 8, :].reshape(CHIPS * 8, 128).astype(F32)
            left = pltpu.roll(got, 64, 1)
            right = pltpu.roll(got, CHIPS * 8 - 4, 0)
            parts.append(jnp.where(row < 4, jnp.where(lane < 64, left, right), 0.0))
        even.append(jnp.concatenate(parts, axis=1))
    odd = jnp.concatenate([pltpu.roll(v, 4, 0) for v in even], axis=0).astype(BF)
    even = jnp.concatenate(even, axis=0).astype(BF)
    for j in range(5):
        cut = slice(8 * j, 8 * j + 8)
        left = jnp.concatenate(
            [src[:, cut, :].reshape(CHIPS * 8, 128) for src in (factors, factors_other)], axis=0
        )
        first, second = dot_tn(left, even), dot_tn(left, odd)
        if j < 4:
            grad_down[j * 256 : j * 256 + 128] = first
            grad_down[j * 256 + 128 : j * 256 + 256] = second
        else:
            item_base[0:128] = first
            item_base[128:C] = second[0:64]


def finish(
    core, mine, theirs, item_base, project, up,
    ge1, gs1, gt1, gp1, ge2, gs2, gt2, gp2, grad_item, grad_up,
    halves,
):
    halves[core[0]] = mine[...]
    halves[1 - core[0]] = theirs[...]
    for j in range(4):
        width = min(128, E - j * 128)
        part = halves[j // 2, :, 0:24, :].reshape(1536, 128)[(j % 2) * 768 : (j % 2 + 1) * 768].astype(F32)
        cut = slice(j * 128, j * 128 + width)
        for i, out in enumerate((ge1, gp1, ge2, gp2)):
            out[:, cut] = part[i * 192 : (i + 1) * 192, 0:width]
    same = lax.broadcasted_iota(jnp.int32, (E, E), 0) == lax.broadcasted_iota(jnp.int32, (E, E), 1)
    for out in (ge1, gp1, ge2, gp2):
        out.leave()
    small = dot_tn(part[0:E].astype(BF), same.astype(F32).astype(BF))
    gs1[...] = small[64:73]
    gt1[...] = small[73:76]
    gs2[...] = small[76:85]
    gt2[...] = small[85:88]
    item = item_base[...]
    for j in range(FH // 128):
        part = halves[j // 4, :, 24:40, :].reshape(1024, 128)[(j % 4) * 256 : (j % 4) * 256 + C]
        cut = slice(j * 128, (j + 1) * 128)
        grad_up[:, cut] = dot_tn(project[...], part)
        item = item + dot_nt(part, up[:, cut])
    grad_item[...] = item


def shape(dims, dtype=BF):
    return jax.ShapeDtypeStruct(dims, dtype)


class Arriving:
    def __init__(self, copy, ref):
        self.copy, self.ref, self.begun = copy, ref, False

    def begin(self):
        if not self.begun:
            self.copy.start()
            self.begun = True

    def ready(self):
        if self.copy is not None:
            self.begin()
            self.copy.wait()
            self.copy = None
        return self.ref

    def __getitem__(self, index):
        return self.ready()[index]


class Leaving:
    def __init__(self, ref, target, semaphore):
        self.ref, self.target, self.semaphore, self.copy = ref, target, semaphore, None

    def __setitem__(self, index, value):
        self.ref[index] = value

    def leave(self, source=None):
        source = self.ref if source is None else source
        self.copy = pltpu.make_async_copy(source, self.target, self.semaphore)
        self.copy.start()


def call(kernel, outs, places, out_places, scratch=(), unstaged=(), megabytes=58):
    staged_in = [i for i, p in enumerate(places) if p in "hw"]
    staged_out = [i for i, p in enumerate(out_places) if p == "h"]
    spaces = {"s": pltpu.SMEM, "v": pltpu.VMEM, "h": pl.ANY, "w": pl.ANY}

    def run(*args):
        stages = [pltpu.VMEM(args[i].shape, args[i].dtype) for i in staged_in]
        stages += [pltpu.VMEM((16, 128) if i in unstaged else outs[i].shape, outs[i].dtype) for i in staged_out]
        sems = [pltpu.SemaphoreType.DMA((max(len(v), 1),)) for v in (staged_in, staged_out)]

        def body(*refs):
            ins, rest = list(refs[: len(args)]), list(refs[len(args) :])
            results, rest = rest[: len(outs)], rest[len(outs) :]
            own, rest = rest[: len(scratch)], rest[len(scratch) :]
            sem_in, sem_out = rest[-2:]
            for k, i in enumerate(staged_in):
                copy = pltpu.make_async_copy(ins[i], rest[k], sem_in.at[k])
                ins[i] = Arriving(copy, rest[k])
                if places[i] == "h":
                    ins[i].begin()
            for k, i in enumerate(staged_out):
                results[i] = Leaving(rest[len(staged_in) + k], results[i], sem_out.at[k])
            kernel(*ins, *results, *own)
            for i in staged_in:
                ins[i].ready()
            for i in staged_out:
                if results[i].copy is None:
                    results[i].leave()
            for i in staged_out:
                results[i].copy.wait()

        return pl.pallas_call(
            body,
            out_shape=outs,
            in_specs=[pl.BlockSpec(memory_space=spaces[p]) for p in places],
            out_specs=[pl.BlockSpec(memory_space=spaces[p]) for p in out_places],
            scratch_shapes=list(scratch) + stages + sems,
            cost_estimate=pl.CostEstimate(flops=10**9, bytes_accessed=10**7, transcendentals=10**6),
            compiler_params=pltpu.CompilerParams(vmem_limit_bytes=megabytes * 1024 * 1024),
        )(*args)

    return run


def local(
    clips, clip_counts, histories, lengths, user_cotangent,
    expand_first, spatial_first, temporal_first, project_first,
    expand_second, spatial_second, temporal_second, project_second,
    item_project, tower_up, tower_down,
):
    same_core = [[i for i in range(DEVICES) if i % 2 == c] for c in range(2)]
    core = (lax.axis_index("seq") % 2).reshape(1)

    def across_chips(v):
        return lax.all_to_all(v, AXES, 0, 0, axis_index_groups=same_core, tiled=True)

    def swap(v):
        return lax.ppermute(v, "seq", [(i, i ^ 1) for i in range(8)])

    x = clips.reshape(ITEMS_HERE, FRAMES * CELLS, C).transpose(1, 0, 2)
    counts = clip_counts.reshape(1, ITEMS_HERE)
    weights = (
        spatial_first, temporal_first, project_first.T,
        expand_second, spatial_second, temporal_second, project_second.T,
    )
    n = ITEMS_HERE
    framed = [pltpu.VMEM((FRAMES + 2, 4, n, E), F32), pltpu.VMEM((FRAMES + 2, n, E), F32)]
    (block,) = call(conv_forward, [shape((CHIPS, 64, 128))], "svvvvvvvvvvv", "v", framed, megabytes=24)(
        lengths, x, counts, user_cotangent, expand_first, *weights
    )
    taps, g1, d1, sp1, n1, h1, o1, g2, d2, sp2, n2, h2 = call(
        conv_forward,
        [
            shape((56, E), F32),
            shape((64, n, E)), shape((64, n, E)), shape((4, 4, n, E)), shape((16, n, E)), shape((16, n, E)),
            shape((512, C)), shape((16, n, E)), shape((16, n, E)), shape((4, n, E)), shape((4, n, E)), shape((4, n, E)),
        ],
        "shvvhvvhhvvh",
        "h" * 12,
        framed,
    )(lengths, x, counts, user_cotangent, expand_first, *weights)
    own = across_chips(block)
    own, taps = lax.optimization_barrier((own, taps))
    sent, *seen, mixed_own, mixed_other = call(
        tower,
        [
            shape((DEVICES, 8, 128)), shape((ROWS, 256)), shape((ROWS, D)), shape((ROWS, FH)), shape((ROWS, FH)),
            shape((CHIPS, 32, 128)), shape((CHIPS, 32, 128)),
        ],
        "sshhvvwww",
        "hhhhhhh",
        unstaged=(5, 6),
    )(core, lengths, own, swap(own), histories, user_cotangent, item_project, tower_up, tower_down)
    back = lax.all_to_all(sent, AXES, 0, 0, tiled=True)
    up_keep, up_send, factors, user_vec = call(
        tower_sums,
        [shape((1024, 128)), shape((1024, 128)), shape((48, 128)), shape((USERS_HERE, D), F32)],
        "sshhhhh",
        "hhhv",
        [pltpu.VMEM((2, 1024, 128), BF)],
        unstaged=(0, 1),
    )(core, lengths, *seen, tower_down)
    back, up_send = lax.optimization_barrier((back, up_send))
    up_other = swap(up_send)
    conv_keep, conv_send = call(
        conv_backward,
        [shape((1536, 128)), shape((1536, 128))],
        "sv" + "h" * 13 + "www",
        "vv",
        [
            pltpu.VMEM((4, 4, n, E), F32),
            pltpu.VMEM((768, 512), F32),
            pltpu.VMEM((32, 8, E), F32),
            pltpu.VMEM((2, 1536, 128), BF),
        ],
    )(
        core, back, taps, n2, weights[6], h2, sp2, g2, d2, o1, weights[3], n1, weights[2], h1, sp1, x, g1, d1,
    )
    (third,) = call(merge, [shape((CHIPS, 80, 128))], "vvvvv", "v", megabytes=16)(
        conv_keep, swap(conv_send), up_keep, up_other, factors
    )
    third = across_chips(third)
    fourth, factors = call(
        sum_chips, [shape((CHIPS, 40, 128)), shape((CHIPS, 40, 128))], "v", "vh", megabytes=16
    )(third)
    fourth = across_chips(fourth)
    grad_down, item_base = call(finish_low_rank, [shape((FH, D), F32), shape((C, D), F32)], "hhhh", "hh")(
        mixed_own, mixed_other, factors, swap(factors)
    )
    fourth, item_base = lax.optimization_barrier((fourth, item_base))
    *conv_grads, grad_item, grad_up = call(
        finish,
        [shape((C, E), F32), shape((9, E), F32), shape((3, E), F32), shape((C, E), F32)] * 2
        + [shape((C, D), F32), shape((D, FH), F32)],
        "svvhhh",
        "hvvhhvvhhh",
        [pltpu.VMEM((2, CHIPS, 40, 128), BF)],
        megabytes=32,
    )(core, fourth, swap(fourth), item_base, item_project, tower_up)
    conv_grads[3] = conv_grads[3].T
    conv_grads[7] = conv_grads[7].T
    return (user_vec, *conv_grads, grad_item, grad_up, grad_down)


def solution(mesh):
    spread = P(AXES)
    return jax.shard_map(
        local,
        mesh=mesh,
        in_specs=(spread,) * 5 + (P(),) * 11,
        out_specs=(spread,) + (P(),) * 11,
        check_vma=False,
    )
```

```python
import jax
import jax.numpy as jnp
from jax import lax
from jax.experimental import pallas as pl
from jax.experimental.pallas import tpu as pltpu
from jax.sharding import PartitionSpec as P

BF = jnp.bfloat16
F32 = jnp.float32
AXES = ("bulk", "seq")
C, E, D, FH = 192, 432, 512, 1024
FRAMES, SIDE, ITEMS_HERE, USERS_HERE, LENGTH = 4, 4, 32, 4, 64
DEVICES, CHIPS, CAPACITY = 128, 64, 4
ROWS = USERS_HERE * LENGTH
CELLS = SIDE * SIDE
HALF = 2
LINKS_FIRST = [
    (HALF * p + q, SIDE * (2 * p + a - 1) + 2 * q + b - 1, 3 * a + b)
    for p in range(HALF)
    for q in range(HALF)
    for a in range(3)
    for b in range(3)
    if 0 <= 2 * p + a - 1 < SIDE and 0 <= 2 * q + b - 1 < SIDE
]
LINKS_SECOND = [(0, 4), (1, 5), (2, 7), (3, 8)]


AT_N2, AT_H2, AT_SP2, AT_G2, AT_D2, AT_N1, AT_H1, AT_SP1, INNER = 0, 4, 8, 12, 28, 44, 60, 76, 92


def dot_nn(a, b):
    return lax.dot_general(a, b, (((1,), (0,)), ((), ())), preferred_element_type=F32)


def dot_nt(a, b):
    return lax.dot_general(a, b, (((1,), (1,)), ((), ())), preferred_element_type=F32)


def dot_tn(a, b):
    return lax.dot_general(a, b, (((0,), (0,)), ((), ())), preferred_element_type=F32)


def silu_and_slope(v):
    gate = 0.5 * jnp.tanh(0.5 * v) + 0.5
    value = v * gate
    return value, gate + value - value * gate


def column_of(row):
    n = row.shape[1]
    same = lax.broadcasted_iota(jnp.int32, (n, n), 0) == lax.broadcasted_iota(jnp.int32, (n, n), 1)
    return jnp.sum(jnp.where(same, row.astype(F32), 0.0), axis=1, keepdims=True).astype(jnp.int32)


def per_user(lengths):
    user = lax.broadcasted_iota(jnp.int32, (8, 1), 0)
    length = jnp.ones((8, 1), jnp.int32)
    for u in range(USERS_HERE):
        length = jnp.where(user == u, lengths[u], length)
    return user, length


def conv_forward(
    lengths, x, counts_row, cot, e1, s1, t1, p1, e2, s2, t2, p2, *rest,
):
    *kept, framed1, framed2 = rest
    block = None
    if len(kept) == 1:
        (block,) = kept
    else:
        taps, weights, outer, inner, o1 = kept
    counts = column_of(counts_row[...])
    zero4 = jnp.zeros((HALF * HALF, ITEMS_HERE, E), F32)
    framed1[0] = zero4
    framed1[FRAMES + 1] = zero4
    zero1 = jnp.zeros((ITEMS_HERE, E), F32)
    framed2[0] = zero1
    framed2[FRAMES + 1] = zero1
    taps1 = s1[...].astype(F32)
    taps2 = s2[...].astype(F32)
    frame1 = t1[...].astype(F32)
    frame2 = t2[...].astype(F32)
    if block is None:
        taps[...] = jnp.zeros((56, E), F32)
        for at, ref in ((0, s1), (9, t1), (12, s2), (21, t2)):
            taps[at : at + ref.shape[0]] = ref[...].astype(F32)
        taps[24:56, 0:128] = jnp.broadcast_to(counts.astype(F32), (ITEMS_HERE, 128))

    if block is None:
        x.ready(), e1.ready()

    def grow(f, _):
        live = f < counts
        x_f = x[pl.ds(f * CELLS, CELLS)]
        x_f = jnp.where(live[None], x_f, jnp.zeros_like(x_f))
        pre = dot_nn(x_f.reshape(CELLS * ITEMS_HERE, C), e1[...])
        value, slope = silu_and_slope(pre)
        value = value.astype(BF).reshape(CELLS, ITEMS_HERE, E)
        if block is None:
            outer[pl.ds(f * CELLS, CELLS)] = value
            outer[pl.ds((FRAMES + f) * CELLS, CELLS)] = slope.astype(BF).reshape(CELLS, ITEMS_HERE, E)
        outs = [jnp.zeros((ITEMS_HERE, E), F32)] * 4
        for out_cell, in_cell, tap in LINKS_FIRST:
            outs[out_cell] = outs[out_cell] + value[in_cell].astype(F32) * taps1[tap]
        for out_cell in range(4):
            framed1[f + 1, out_cell] = outs[out_cell]
            if block is None:
                inner[AT_SP1 + f * 4 + out_cell] = outs[out_cell].astype(BF)
        return 0

    lax.fori_loop(0, FRAMES, grow, 0, unroll=True)
    narrow = []
    for f in range(FRAMES):
        summed = framed1[f] * frame1[0] + framed1[f + 1] * frame1[1] + framed1[f + 2] * frame1[2]
        value, slope = silu_and_slope(summed)
        narrow.append(value.astype(BF))
        if block is None:
            inner[AT_H1 + f * 4 : AT_H1 + f * 4 + 4] = slope.astype(BF)
    narrow = jnp.concatenate(narrow, axis=0)
    first = dot_nt(narrow.reshape(FRAMES * 4 * ITEMS_HERE, E), p1[...]).astype(BF)
    value, slope = silu_and_slope(dot_nn(first, e2[...]))
    value = value.astype(BF).reshape(FRAMES * 4, ITEMS_HERE, E)
    if block is None:
        inner[AT_N1 : AT_N1 + 16] = narrow
        o1[...] = first
        inner[AT_G2 : AT_G2 + 16] = value
        inner[AT_D2 : AT_D2 + 16] = slope.astype(BF).reshape(FRAMES * 4, ITEMS_HERE, E)
        weights[0:192] = p2[...]
        weights[192:384] = e2[...]
        weights[384:576] = p1[...]
    for f in range(FRAMES):
        total = jnp.zeros((ITEMS_HERE, E), F32)
        for cell, tap in LINKS_SECOND:
            total = total + value[f * 4 + cell].astype(F32) * taps2[tap]
        framed2[f + 1] = total
        if block is None:
            inner[AT_SP2 + f] = total.astype(BF)
    narrow = []
    for f in range(FRAMES):
        summed = framed2[f] * frame2[0] + framed2[f + 1] * frame2[1] + framed2[f + 2] * frame2[2]
        value, slope = silu_and_slope(summed)
        narrow.append(value.astype(BF))
        if block is None:
            inner[AT_N2 + f] = value.astype(BF)
            inner[AT_H2 + f] = slope.astype(BF)
    if block is None:
        return
    second = dot_nt(jnp.concatenate(narrow, axis=0), p2[...]).astype(BF)
    pooled = jnp.zeros((ITEMS_HERE, C), F32)
    for f in range(FRAMES):
        live = (f < counts).astype(F32)
        pooled = pooled + live * second[f * ITEMS_HERE : (f + 1) * ITEMS_HERE].astype(F32)
    pooled = pooled / counts.astype(F32)
    _, length = per_user(lengths)
    shared = cot[...] / length[0:4].astype(F32)
    pieces = []
    for k in range(8):
        piece = shared[:, (k // 2) * 128 : (k // 2 + 1) * 128]
        pieces.append(piece if k % 2 else pltpu.roll(piece, 64, 1))
    lane = lax.broadcasted_iota(jnp.int32, (ITEMS_HERE, 128), 1)
    shared = jnp.concatenate(pieces, axis=0)
    high = jnp.concatenate([pooled[:, 128:192], pooled[:, 0:64]], axis=1)
    rows = jnp.concatenate([pooled[:, 0:128], jnp.where(lane < 64, high, shared)], axis=0).astype(BF)
    block[...] = jnp.broadcast_to(rows[None], (CHIPS, 64, 128))


def tower_middle(picked, lengths, cot, project, up, down):
    fetched = dot_nn(picked[:, 0:C], project[...]).astype(BF)
    pre = dot_nn(fetched, up[...])
    scale = 0.7978845608028654
    square = pre * pre
    bent = jnp.tanh(scale * pre * (1.0 + 0.044715 * square))
    gate = 0.5 * (1.0 + bent)
    act = (pre * gate).astype(BF)
    slope = gate + 0.5 * pre * (1.0 - bent * bent) * (scale * (1.0 + 3 * 0.044715 * square))
    _, length = per_user(lengths)
    shared = cot[...] / length[0:4].astype(F32)
    shared_half = shared.astype(BF)
    act_grad = dot_nt(jnp.concatenate([shared_half, shared_half], axis=0), down[...])
    position = lax.broadcasted_iota(jnp.int32, (LENGTH, 1), 0)
    pre_parts, base_parts = [], []
    for u in range(USERS_HERE):
        alive = (position < lengths[u]).astype(F32)
        pre_parts.append(alive * act_grad[u : u + 1] * slope[u * LENGTH : (u + 1) * LENGTH])
        base_parts.append(alive * shared[u : u + 1])
    pre_grad = jnp.concatenate(pre_parts, axis=0).astype(BF)
    return fetched, act, pre_grad, jnp.concatenate(base_parts, axis=0)


def tower(
    core, lengths, own, other, ids_ref, cot, project, up, down,
    sent, picked_out,
):
    ids = jnp.concatenate([column_of(ids_ref[u : u + 1]) for u in range(USERS_HERE)], axis=0)
    owner = ids // ITEMS_HERE
    within = ids - owner * ITEMS_HERE
    chip = owner // 2
    place = chip * ITEMS_HERE + within
    mine = (owner - chip * 2) == core[0]
    lanes = lax.broadcasted_iota(jnp.int32, (ROWS, CHIPS * ITEMS_HERE), 1)
    pick_own = (lanes == jnp.where(mine, place, -1)).astype(F32).astype(BF)
    pick_other = (lanes == jnp.where(mine, -1, place)).astype(F32).astype(BF)

    def rows_of(ref):
        low = ref[:, 0:32, :].reshape(CHIPS * ITEMS_HERE, 128)
        high = ref[:, 32:64, :].reshape(CHIPS * ITEMS_HERE, 128)
        return jnp.concatenate([low, high], axis=1)

    own, other = own.ready(), other.ready()
    for late in (project, up, down):
        late.begin()
    picked = (dot_nn(pick_own, rows_of(own)) + dot_nn(pick_other, rows_of(other))).astype(BF)
    picked_out[...] = picked
    picked_out.leave()
    _, _, pre_grad, base = tower_middle(picked, lengths, cot, project, up, down)
    rows_grad = base + dot_nt(pre_grad, up[...])
    rows_coarse = rows_grad.astype(BF)
    rows_fine = (rows_grad - rows_coarse.astype(F32)).astype(BF)
    low = dot_nt(rows_coarse, project[0:128]) + dot_nt(rows_fine, project[0:128])
    high = dot_nt(rows_coarse, project[64:192]) + dot_nt(rows_fine, project[64:192])
    lane = lax.broadcasted_iota(jnp.int32, (ROWS, 128), 1)
    tag = within.astype(F32)
    low = jnp.where(lane < 96, low, jnp.where(lane == 96, tag, 0.0)).astype(BF)
    high = jnp.where(lane >= 32, high, jnp.where(lane == 0, tag, 0.0)).astype(BF)

    across = lax.broadcasted_iota(jnp.int32, (ROWS, ROWS), 1)
    down_rows = lax.broadcasted_iota(jnp.int32, (ROWS, ROWS), 0)
    owner_row = jnp.sum(jnp.where(across == down_rows, owner.astype(F32), 0.0), axis=0, keepdims=True).astype(jnp.int32)
    earlier = down_rows < across
    rank = jnp.sum(((owner == owner_row) & earlier).astype(F32), axis=0, keepdims=True).astype(jnp.int32)
    slot = owner_row * 8 + rank
    sent_at = lax.broadcasted_iota(jnp.int32, (DEVICES * 8, ROWS), 0)
    put_low = (sent_at == slot).astype(F32).astype(BF)
    put_high = (sent_at == slot + CAPACITY).astype(F32).astype(BF)
    back = (dot_nn(put_low, low) + dot_nn(put_high, high)).astype(BF)
    sent[...] = back.reshape(DEVICES, 8, 128)


def tower_sums(
    core, lengths, picked, cot, project, up, down,
    up_keep, up_send, factors, user_vec,
    halves,
):
    picked = picked[...]
    fetched, act, pre_grad, _ = tower_middle(picked, lengths, cot, project, up, down)
    user, length = per_user(lengths)
    at = lax.broadcasted_iota(jnp.int32, (8, ROWS), 1)
    live = ((at // LENGTH == user) & (at - user * LENGTH < length)).astype(F32).astype(BF)
    act_sum = dot_nn(live, act)
    picked_sum = dot_nn(live, picked)
    pieces = [act_sum[0:4, j * 128 : (j + 1) * 128] for j in range(8)]
    pieces += [picked_sum[0:4, j * 128 : (j + 1) * 128] for j in range(2)]
    factors[...] = jnp.concatenate(pieces + [jnp.zeros((8, 128), F32)], axis=0).astype(BF)
    coarse = act_sum.astype(BF)
    fine = (act_sum - coarse.astype(F32)).astype(BF)
    mixed = dot_nn(live, fetched) + dot_nn(coarse, down[...]) + dot_nn(fine, down[...])
    user_vec[...] = (mixed / length.astype(F32))[0:4]
    up_grad = dot_tn(picked, pre_grad).astype(BF)
    for j in range(FH // 128):
        halves[j // 4, (j % 4) * 256 : (j % 4 + 1) * 256] = up_grad[:, j * 128 : (j + 1) * 128]
    up_keep.leave(halves.at[core[0]])
    up_send.leave(halves.at[1 - core[0]])


def conv_backward(
    core, back, inner, taps, weights, o1, x, outer,
    keep, send,
    spatial_grad, wide, small, halves,
):
    taps1, frame1, taps2, frame2 = taps[0:9], taps[9:12], taps[12:21], taps[21:24]
    counts = taps[24:56, 0:1]
    inner.ready(), weights.ready(), o1.ready()
    p2, e2, p1 = weights[0:192], weights[192:384], weights[384:576]

    def tile_sum(v):
        return jnp.sum(v.reshape(-1, 8, E), axis=0)

    small[...] = jnp.zeros(small.shape, F32)
    wide[...] = jnp.zeros(wide.shape, F32)
    got = back[...].reshape(DEVICES * 8, 128)
    row = lax.broadcasted_iota(jnp.int32, (DEVICES * 8, 1), 0)
    is_low = (row & 7) < CAPACITY
    got_f = got.astype(F32)
    tag = jnp.where(is_low, got_f[:, 96:97], got_f[:, 0:1]).astype(jnp.int32)
    named = tag == lax.broadcasted_iota(jnp.int32, (DEVICES * 8, ITEMS_HERE), 1)
    low = dot_tn((named & is_low).astype(F32).astype(BF), got)
    high = dot_tn((named & ~is_low).astype(F32).astype(BF), got)
    pooled_grad = jnp.concatenate([low[:, 0:96], high[:, 32:128]], axis=1)
    shared = pooled_grad / counts
    out_grad = jnp.concatenate(
        [(shared * (counts > f).astype(F32)).astype(BF) for f in range(FRAMES)], axis=0
    )
    wide[576:768, 0:E] = dot_tn(out_grad, inner[AT_N2 : AT_N2 + 4].reshape(FRAMES * ITEMS_HERE, E))
    summed_grad = dot_nn(out_grad, p2).reshape(FRAMES, ITEMS_HERE, E) * inner[AT_H2 : AT_H2 + 4].astype(F32)
    spread = []
    for f in range(FRAMES):
        total = summed_grad[f] * frame2[1]
        if f + 1 < FRAMES:
            total = total + summed_grad[f + 1] * frame2[0]
        if f > 0:
            total = total + summed_grad[f - 1] * frame2[2]
        spread.append(total)
    for k in range(3):
        total = jnp.zeros((8, E), F32)
        for f in range(FRAMES):
            if 0 <= f + k - 1 < FRAMES:
                total = total + tile_sum(inner[AT_SP2 + f + k - 1].astype(F32) * summed_grad[f])
        small[21 + k] = total
    parts = []
    for f in range(FRAMES):
        for cell, tap in LINKS_SECOND:
            small[12 + tap] += tile_sum(inner[AT_G2 + f * 4 + cell].astype(F32) * spread[f])
            parts.append((spread[f] * taps2[tap] * inner[AT_D2 + f * 4 + cell].astype(F32)).astype(BF))
    grown_grad = jnp.concatenate(parts, axis=0)
    wide[384:576, 0:E] = dot_tn(o1[...], grown_grad)
    first_grad = dot_nt(grown_grad, e2).astype(BF)
    wide[192:384, 0:E] = dot_tn(first_grad, inner[AT_N1 : AT_N1 + 16].reshape(FRAMES * 4 * ITEMS_HERE, E))
    narrow_grad = dot_nn(first_grad, p1).reshape(FRAMES, 4, ITEMS_HERE, E)
    summed_grad = [narrow_grad[f] * inner[AT_H1 + f * 4 : AT_H1 + f * 4 + 4].astype(F32) for f in range(FRAMES)]
    for k in range(3):
        total = jnp.zeros((8, E), F32)
        for f in range(FRAMES):
            if 0 <= f + k - 1 < FRAMES:
                total = total + tile_sum(inner[AT_SP1 + f * 4 + 4 * k - 4 : AT_SP1 + f * 4 + 4 * k].astype(F32) * summed_grad[f])
        small[9 + k] = total
    for f in range(FRAMES):
        total = summed_grad[f] * frame1[1]
        if f + 1 < FRAMES:
            total = total + summed_grad[f + 1] * frame1[0]
        if f > 0:
            total = total + summed_grad[f - 1] * frame1[2]
        spatial_grad[f] = total.astype(BF)

    x.ready(), outer.ready()
    half_taps = taps1.astype(BF)

    def grow_back(f, _):
        live = counts > lax.convert_element_type(f, F32)
        x_f = x[pl.ds(f * CELLS, CELLS)]
        x_f = jnp.where(live[None], x_f, jnp.zeros_like(x_f)).reshape(CELLS * ITEMS_HERE, C)
        outs = [spatial_grad[f, cell] for cell in range(4)]
        sums = [None] * 9
        grads = [None] * CELLS
        for out_cell, in_cell, tap in LINKS_FIRST:
            term = outs[out_cell] * half_taps[tap]
            grads[in_cell] = term if grads[in_cell] is None else grads[in_cell] + term
            term = outer[f * CELLS + in_cell] * outs[out_cell]
            sums[tap] = term if sums[tap] is None else sums[tap] + term
        for tap in range(9):
            small[tap] += tile_sum(sums[tap].astype(F32))
        grads = [grads[cell] * outer[(FRAMES + f) * CELLS + cell] for cell in range(CELLS)]
        wide[0:192, 0:E] += dot_tn(x_f, jnp.concatenate(grads, axis=0))
        return 0

    lax.fori_loop(0, FRAMES, grow_back, 0, unroll=True)
    sums = jnp.sum(small[...], axis=1).astype(BF)
    put = lax.broadcasted_iota(jnp.int32, (32, 128), 1) == lax.broadcasted_iota(jnp.int32, (32, 128), 0) + 64
    wide[0:E, 384:512] += dot_tn(sums, put.astype(F32).astype(BF))
    for j in range(4):
        halves[j // 2, (j % 2) * 768 : (j % 2 + 1) * 768] = wide[:, j * 128 : (j + 1) * 128].astype(BF)
    keep[...] = halves[core[0]]
    send[...] = halves[1 - core[0]]


def merge(conv_a, conv_b, up_a, up_b, factors, out):
    conv = (conv_a[...].astype(F32) + conv_b[...].astype(F32)).astype(BF)
    up = (up_a[...].astype(F32) + up_b[...].astype(F32)).astype(BF)
    out[:, 0:24, :] = conv.reshape(CHIPS, 24, 128)
    out[:, 24:40, :] = up.reshape(CHIPS, 16, 128)
    out[:, 40:80, :] = jnp.broadcast_to(factors[0:40][None], (CHIPS, 40, 128))


def sum_chips(third, out, factors):
    factors[...] = third[:, 40:80, :]
    factors.leave()
    total = jnp.sum(third[:, 0:40, :].astype(F32), axis=0).astype(BF)
    out[...] = jnp.broadcast_to(total[None], (CHIPS, 40, 128))


def finish_low_rank(own, other, factors, factors_other, grad_down, item_base):
    row = lax.broadcasted_iota(jnp.int32, (CHIPS * 8, 128), 0) & 7
    lane = lax.broadcasted_iota(jnp.int32, (CHIPS * 8, 128), 1)
    even = []
    for src in (own, other):
        parts = []
        for k in range(4):
            got = src[:, 32 + 8 * k : 40 + 8 * k, :].reshape(CHIPS * 8, 128).astype(F32)
            left = pltpu.roll(got, 64, 1)
            right = pltpu.roll(got, CHIPS * 8 - 4, 0)
            parts.append(jnp.where(row < 4, jnp.where(lane < 64, left, right), 0.0))
        even.append(jnp.concatenate(parts, axis=1))
    odd = jnp.concatenate([pltpu.roll(v, 4, 0) for v in even], axis=0).astype(BF)
    even = jnp.concatenate(even, axis=0).astype(BF)
    for j in range(5):
        cut = slice(8 * j, 8 * j + 8)
        left = jnp.concatenate(
            [src[:, cut, :].reshape(CHIPS * 8, 128) for src in (factors, factors_other)], axis=0
        )
        first, second = dot_tn(left, even), dot_tn(left, odd)
        if j < 4:
            grad_down[j * 256 : j * 256 + 128] = first
            grad_down[j * 256 + 128 : j * 256 + 256] = second
        else:
            item_base[0:128] = first
            item_base[128:C] = second[0:64]


def finish(
    core, mine, theirs, item_base, project, up,
    ge1, gs1, gt1, gp1, ge2, gs2, gt2, gp2, grad_item, grad_up,
    halves,
):
    halves[core[0]] = mine[...]
    halves[1 - core[0]] = theirs[...]
    for j in range(4):
        width = min(128, E - j * 128)
        part = halves[j // 2, :, 0:24, :].reshape(1536, 128)[(j % 2) * 768 : (j % 2 + 1) * 768].astype(F32)
        cut = slice(j * 128, j * 128 + width)
        for i, out in enumerate((ge1, gp1, ge2, gp2)):
            out[:, cut] = part[i * 192 : (i + 1) * 192, 0:width]
    same = lax.broadcasted_iota(jnp.int32, (E, E), 0) == lax.broadcasted_iota(jnp.int32, (E, E), 1)
    for out in (ge1, gp1, ge2, gp2):
        out.leave()
    small = dot_tn(part[0:E].astype(BF), same.astype(F32).astype(BF))
    gs1[...] = small[64:73]
    gt1[...] = small[73:76]
    gs2[...] = small[76:85]
    gt2[...] = small[85:88]
    item = item_base[...]
    for j in range(FH // 128):
        part = halves[j // 4, :, 24:40, :].reshape(1024, 128)[(j % 4) * 256 : (j % 4) * 256 + C]
        cut = slice(j * 128, (j + 1) * 128)
        grad_up[:, cut] = dot_tn(project[...], part)
        item = item + dot_nt(part, up[:, cut])
    grad_item[...] = item


def shape(dims, dtype=BF):
    return jax.ShapeDtypeStruct(dims, dtype)


class Arriving:
    def __init__(self, copy, ref):
        self.copy, self.ref, self.begun = copy, ref, False

    def begin(self):
        if not self.begun:
            self.copy.start()
            self.begun = True

    def ready(self):
        if self.copy is not None:
            self.begin()
            self.copy.wait()
            self.copy = None
        return self.ref

    def __getitem__(self, index):
        return self.ready()[index]


class Leaving:
    def __init__(self, ref, target, semaphore):
        self.ref, self.target, self.semaphore, self.copy = ref, target, semaphore, None

    def __setitem__(self, index, value):
        self.ref[index] = value

    def leave(self, source=None):
        source = self.ref if source is None else source
        self.copy = pltpu.make_async_copy(source, self.target, self.semaphore)
        self.copy.start()


def call(kernel, outs, places, out_places, scratch=(), unstaged=(), megabytes=58):
    staged_in = [i for i, p in enumerate(places) if p in "hw"]
    staged_out = [i for i, p in enumerate(out_places) if p == "h"]
    spaces = {"s": pltpu.SMEM, "v": pltpu.VMEM, "h": pl.ANY, "w": pl.ANY}

    def run(*args):
        stages = [pltpu.VMEM(args[i].shape, args[i].dtype) for i in staged_in]
        stages += [pltpu.VMEM((16, 128) if i in unstaged else outs[i].shape, outs[i].dtype) for i in staged_out]
        sems = [pltpu.SemaphoreType.DMA((max(len(v), 1),)) for v in (staged_in, staged_out)]

        def body(*refs):
            ins, rest = list(refs[: len(args)]), list(refs[len(args) :])
            results, rest = rest[: len(outs)], rest[len(outs) :]
            own, rest = rest[: len(scratch)], rest[len(scratch) :]
            sem_in, sem_out = rest[-2:]
            for k, i in enumerate(staged_in):
                copy = pltpu.make_async_copy(ins[i], rest[k], sem_in.at[k])
                ins[i] = Arriving(copy, rest[k])
                if places[i] == "h":
                    ins[i].begin()
            for k, i in enumerate(staged_out):
                results[i] = Leaving(rest[len(staged_in) + k], results[i], sem_out.at[k])
            kernel(*ins, *results, *own)
            for i in staged_in:
                ins[i].ready()
            for i in staged_out:
                if results[i].copy is None:
                    results[i].leave()
            for i in staged_out:
                results[i].copy.wait()

        return pl.pallas_call(
            body,
            out_shape=outs,
            in_specs=[pl.BlockSpec(memory_space=spaces[p]) for p in places],
            out_specs=[pl.BlockSpec(memory_space=spaces[p]) for p in out_places],
            scratch_shapes=list(scratch) + stages + sems,
            cost_estimate=pl.CostEstimate(flops=10**9, bytes_accessed=10**7, transcendentals=10**6),
            compiler_params=pltpu.CompilerParams(vmem_limit_bytes=megabytes * 1024 * 1024),
        )(*args)

    return run


def local(
    clips, clip_counts, histories, lengths, user_cotangent,
    expand_first, spatial_first, temporal_first, project_first,
    expand_second, spatial_second, temporal_second, project_second,
    item_project, tower_up, tower_down,
):
    same_core = [[i for i in range(DEVICES) if i % 2 == c] for c in range(2)]
    core = (lax.axis_index("seq") % 2).reshape(1)

    def across_chips(v):
        return lax.all_to_all(v, AXES, 0, 0, axis_index_groups=same_core, tiled=True)

    def swap(v):
        return lax.ppermute(v, "seq", [(i, i ^ 1) for i in range(8)])

    x = clips.reshape(ITEMS_HERE, FRAMES * CELLS, C).transpose(1, 0, 2)
    counts = clip_counts.reshape(1, ITEMS_HERE)
    weights = (
        spatial_first, temporal_first, project_first.T,
        expand_second, spatial_second, temporal_second, project_second.T,
    )
    n = ITEMS_HERE
    framed = [pltpu.VMEM((FRAMES + 2, 4, n, E), F32), pltpu.VMEM((FRAMES + 2, n, E), F32)]
    (block,) = call(conv_forward, [shape((CHIPS, 64, 128))], "svvvvvvvvvvv", "v", framed, megabytes=24)(
        lengths, x, counts, user_cotangent, expand_first, *weights
    )
    kept = call(
        conv_forward,
        [shape((56, E), F32), shape((576, E)), shape((2 * 64, n, E)), shape((INNER, n, E)), shape((512, C))],
        "shvvhvvhhvvh",
        "h" * 5,
        framed,
    )(lengths, x, counts, user_cotangent, expand_first, *weights)
    own = across_chips(block)
    own, (taps, kept_weights, outer, inner, o1) = lax.optimization_barrier((own, kept))
    other = swap(own)
    sent, picked = call(tower, [shape((DEVICES, 8, 128)), shape((ROWS, 256))], "sshhvvwww", "hh")(
        core, lengths, own, other, histories, user_cotangent, item_project, tower_up, tower_down
    )
    back = lax.all_to_all(sent, AXES, 0, 0, tiled=True)
    up_keep, up_send, factors, user_vec = call(
        tower_sums,
        [shape((1024, 128)), shape((1024, 128)), shape((48, 128)), shape((USERS_HERE, D), F32)],
        "sshvhhh",
        "hhhv",
        [pltpu.VMEM((2, 1024, 128), BF)],
        unstaged=(0, 1),
    )(core, lengths, picked, user_cotangent, item_project, tower_up, tower_down)
    back, up_send = lax.optimization_barrier((back, up_send))
    up_other = swap(up_send)
    conv_keep, conv_send = call(
        conv_backward,
        [shape((1536, 128)), shape((1536, 128))],
        "sv" + "h" * 6,
        "vv",
        [
            pltpu.VMEM((4, 4, n, E), BF),
            pltpu.VMEM((768, 512), F32),
            pltpu.VMEM((32, 8, E), F32),
            pltpu.VMEM((2, 1536, 128), BF),
        ],
        megabytes=50,
    )(core, back, inner, taps, kept_weights, o1, x, outer)
    (third,) = call(merge, [shape((CHIPS, 80, 128))], "vvvvv", "v", megabytes=16)(
        conv_keep, swap(conv_send), up_keep, up_other, factors
    )
    third = across_chips(third)
    fourth, factors = call(
        sum_chips, [shape((CHIPS, 40, 128)), shape((CHIPS, 40, 128))], "v", "vh", megabytes=16
    )(third)
    fourth = across_chips(fourth)
    grad_down, item_base = call(finish_low_rank, [shape((FH, D), F32), shape((C, D), F32)], "hhhh", "hh")(
        own, other, factors, swap(factors)
    )
    fourth, item_base = lax.optimization_barrier((fourth, item_base))
    *conv_grads, grad_item, grad_up = call(
        finish,
        [shape((C, E), F32), shape((9, E), F32), shape((3, E), F32), shape((C, E), F32)] * 2
        + [shape((C, D), F32), shape((D, FH), F32)],
        "svvhhh",
        "hvvhhvvhhh",
        [pltpu.VMEM((2, CHIPS, 40, 128), BF)],
        megabytes=32,
    )(core, fourth, swap(fourth), item_base, item_project, tower_up)
    conv_grads[3] = conv_grads[3].T
    conv_grads[7] = conv_grads[7].T
    return (user_vec, *conv_grads, grad_item, grad_up, grad_down)


def solution(mesh):
    spread = P(AXES)
    return jax.shard_map(
        local,
        mesh=mesh,
        in_specs=(spread,) * 5 + (P(),) * 11,
        out_specs=(spread,) + (P(),) * 11,
        check_vma=False,
    )
```

```python
import jax
import jax.numpy as jnp
from jax import lax
from jax.experimental import pallas as pl
from jax.experimental.pallas import tpu as pltpu
from jax.sharding import PartitionSpec as P

BF = jnp.bfloat16
F32 = jnp.float32
AXES = ("bulk", "seq")
C, E, D, FH = 192, 432, 512, 1024
FRAMES, SIDE, ITEMS_HERE, USERS_HERE, LENGTH = 4, 4, 32, 4, 64
DEVICES, CHIPS, CAPACITY = 128, 64, 4
ROWS = USERS_HERE * LENGTH
CELLS = SIDE * SIDE
HALF = 2
LINKS_FIRST = [
    (HALF * p + q, SIDE * (2 * p + a - 1) + 2 * q + b - 1, 3 * a + b)
    for p in range(HALF)
    for q in range(HALF)
    for a in range(3)
    for b in range(3)
    if 0 <= 2 * p + a - 1 < SIDE and 0 <= 2 * q + b - 1 < SIDE
]
LINKS_SECOND = [(0, 4), (1, 5), (2, 7), (3, 8)]


AT_N2, AT_H2, AT_SP2, AT_G2, AT_D2, AT_N1, AT_H1, AT_SP1, INNER = 0, 4, 8, 12, 28, 44, 60, 76, 92


def dot_nn(a, b):
    return lax.dot_general(a, b, (((1,), (0,)), ((), ())), preferred_element_type=F32)


def dot_nt(a, b):
    return lax.dot_general(a, b, (((1,), (1,)), ((), ())), preferred_element_type=F32)


def dot_tn(a, b):
    return lax.dot_general(a, b, (((0,), (0,)), ((), ())), preferred_element_type=F32)


def silu_and_slope(v):
    gate = 0.5 * jnp.tanh(0.5 * v) + 0.5
    value = v * gate
    return value, gate + value - value * gate


def column_of(row):
    n = row.shape[1]
    same = lax.broadcasted_iota(jnp.int32, (n, n), 0) == lax.broadcasted_iota(jnp.int32, (n, n), 1)
    return jnp.sum(jnp.where(same, row.astype(F32), 0.0), axis=1, keepdims=True).astype(jnp.int32)


def per_user(lengths):
    user = lax.broadcasted_iota(jnp.int32, (8, 1), 0)
    length = jnp.ones((8, 1), jnp.int32)
    for u in range(USERS_HERE):
        length = jnp.where(user == u, lengths[u], length)
    return user, length


def conv_forward(
    lengths, x, counts_row, cot, e1, s1, t1, p1, e2, s2, t2, p2, *rest,
):
    *kept, framed1, framed2 = rest
    block = None
    if len(kept) == 1:
        (block,) = kept
    else:
        taps, weights, outer, inner, o1 = kept
    counts = column_of(counts_row[...])
    zero4 = jnp.zeros((HALF * HALF, ITEMS_HERE, E), F32)
    framed1[0] = zero4
    framed1[FRAMES + 1] = zero4
    zero1 = jnp.zeros((ITEMS_HERE, E), F32)
    framed2[0] = zero1
    framed2[FRAMES + 1] = zero1
    taps1 = s1[...].astype(F32)
    taps2 = s2[...].astype(F32)
    frame1 = t1[...].astype(F32)
    frame2 = t2[...].astype(F32)
    if block is None:
        taps[...] = jnp.zeros((56, E), F32)
        for at, ref in ((0, s1), (9, t1), (12, s2), (21, t2)):
            taps[at : at + ref.shape[0]] = ref[...].astype(F32)
        taps[24:56, 0:128] = jnp.broadcast_to(counts.astype(F32), (ITEMS_HERE, 128))

    if block is None:
        x.ready(), e1.ready()

    def grow(f, _):
        live = f < counts
        x_f = x[pl.ds(f * CELLS, CELLS)]
        x_f = jnp.where(live[None], x_f, jnp.zeros_like(x_f))
        pre = dot_nn(x_f.reshape(CELLS * ITEMS_HERE, C), e1[...])
        value, slope = silu_and_slope(pre)
        value = value.astype(BF).reshape(CELLS, ITEMS_HERE, E)
        if block is None:
            outer[pl.ds(f * CELLS, CELLS)] = value
            outer[pl.ds((FRAMES + f) * CELLS, CELLS)] = slope.astype(BF).reshape(CELLS, ITEMS_HERE, E)
        outs = [jnp.zeros((ITEMS_HERE, E), F32)] * 4
        for out_cell, in_cell, tap in LINKS_FIRST:
            outs[out_cell] = outs[out_cell] + value[in_cell].astype(F32) * taps1[tap]
        for out_cell in range(4):
            framed1[f + 1, out_cell] = outs[out_cell]
            if block is None:
                inner[AT_SP1 + f * 4 + out_cell] = outs[out_cell].astype(BF)
        return 0

    lax.fori_loop(0, FRAMES, grow, 0, unroll=True)
    narrow = []
    for f in range(FRAMES):
        summed = framed1[f] * frame1[0] + framed1[f + 1] * frame1[1] + framed1[f + 2] * frame1[2]
        value, slope = silu_and_slope(summed)
        narrow.append(value.astype(BF))
        if block is None:
            inner[AT_H1 + f * 4 : AT_H1 + f * 4 + 4] = slope.astype(BF)
    narrow = jnp.concatenate(narrow, axis=0)
    first = dot_nt(narrow.reshape(FRAMES * 4 * ITEMS_HERE, E), p1[...]).astype(BF)
    value, slope = silu_and_slope(dot_nn(first, e2[...]))
    value = value.astype(BF).reshape(FRAMES * 4, ITEMS_HERE, E)
    if block is None:
        inner[AT_N1 : AT_N1 + 16] = narrow
        o1[...] = first
        inner[AT_G2 : AT_G2 + 16] = value
        inner[AT_D2 : AT_D2 + 16] = slope.astype(BF).reshape(FRAMES * 4, ITEMS_HERE, E)
        weights[0:192] = p2[...]
        weights[192:384] = e2[...]
        weights[384:576] = p1[...]
    for f in range(FRAMES):
        total = jnp.zeros((ITEMS_HERE, E), F32)
        for cell, tap in LINKS_SECOND:
            total = total + value[f * 4 + cell].astype(F32) * taps2[tap]
        framed2[f + 1] = total
        if block is None:
            inner[AT_SP2 + f] = total.astype(BF)
    narrow = []
    for f in range(FRAMES):
        summed = framed2[f] * frame2[0] + framed2[f + 1] * frame2[1] + framed2[f + 2] * frame2[2]
        value, slope = silu_and_slope(summed)
        narrow.append(value.astype(BF))
        if block is None:
            inner[AT_N2 + f] = value.astype(BF)
            inner[AT_H2 + f] = slope.astype(BF)
    if block is None:
        return
    second = dot_nt(jnp.concatenate(narrow, axis=0), p2[...]).astype(BF)
    pooled = jnp.zeros((ITEMS_HERE, C), F32)
    for f in range(FRAMES):
        live = (f < counts).astype(F32)
        pooled = pooled + live * second[f * ITEMS_HERE : (f + 1) * ITEMS_HERE].astype(F32)
    pooled = pooled / counts.astype(F32)
    _, length = per_user(lengths)
    shared = cot[...] / length[0:4].astype(F32)
    pieces = []
    for k in range(8):
        piece = shared[:, (k // 2) * 128 : (k // 2 + 1) * 128]
        pieces.append(piece if k % 2 else pltpu.roll(piece, 64, 1))
    lane = lax.broadcasted_iota(jnp.int32, (ITEMS_HERE, 128), 1)
    shared = jnp.concatenate(pieces, axis=0)
    high = jnp.concatenate([pooled[:, 128:192], pooled[:, 0:64]], axis=1)
    rows = jnp.concatenate([pooled[:, 0:128], jnp.where(lane < 64, high, shared)], axis=0).astype(BF)
    block[...] = jnp.broadcast_to(rows[None], (CHIPS, 64, 128))


def tower_middle(picked, lengths, cot, project, up, down):
    fetched = dot_nn(picked[:, 0:C], project[...]).astype(BF)
    pre = dot_nn(fetched, up[...])
    scale = 0.7978845608028654
    square = pre * pre
    bent = jnp.tanh(scale * pre * (1.0 + 0.044715 * square))
    gate = 0.5 * (1.0 + bent)
    act = (pre * gate).astype(BF)
    slope = gate + 0.5 * pre * (1.0 - bent * bent) * (scale * (1.0 + 3 * 0.044715 * square))
    _, length = per_user(lengths)
    shared = cot[...] / length[0:4].astype(F32)
    shared_half = shared.astype(BF)
    act_grad = dot_nt(jnp.concatenate([shared_half, shared_half], axis=0), down[...])
    position = lax.broadcasted_iota(jnp.int32, (LENGTH, 1), 0)
    pre_parts, base_parts = [], []
    for u in range(USERS_HERE):
        alive = (position < lengths[u]).astype(F32)
        pre_parts.append(alive * act_grad[u : u + 1] * slope[u * LENGTH : (u + 1) * LENGTH])
        base_parts.append(alive * shared[u : u + 1])
    pre_grad = jnp.concatenate(pre_parts, axis=0).astype(BF)
    return fetched, act, pre_grad, jnp.concatenate(base_parts, axis=0)


def tower(
    core, lengths, own, other, ids_ref, cot, project, up, down,
    sent, picked_out,
):
    ids = jnp.concatenate([column_of(ids_ref[u : u + 1]) for u in range(USERS_HERE)], axis=0)
    owner = ids // ITEMS_HERE
    within = ids - owner * ITEMS_HERE
    chip = owner // 2
    place = chip * ITEMS_HERE + within
    mine = (owner - chip * 2) == core[0]
    lanes = lax.broadcasted_iota(jnp.int32, (ROWS, CHIPS * ITEMS_HERE), 1)
    pick_own = (lanes == jnp.where(mine, place, -1)).astype(F32).astype(BF)
    pick_other = (lanes == jnp.where(mine, -1, place)).astype(F32).astype(BF)

    def rows_of(ref):
        low = ref[:, 0:32, :].reshape(CHIPS * ITEMS_HERE, 128)
        high = ref[:, 32:64, :].reshape(CHIPS * ITEMS_HERE, 128)
        return jnp.concatenate([low, high], axis=1)

    across = lax.broadcasted_iota(jnp.int32, (ROWS, ROWS), 1)
    down_rows = lax.broadcasted_iota(jnp.int32, (ROWS, ROWS), 0)
    owner_row = jnp.sum(jnp.where(across == down_rows, owner.astype(F32), 0.0), axis=0, keepdims=True).astype(jnp.int32)
    earlier = down_rows < across
    rank = jnp.sum(((owner == owner_row) & earlier).astype(F32), axis=0, keepdims=True).astype(jnp.int32)
    slot = owner_row * 8 + rank
    sent_at = lax.broadcasted_iota(jnp.int32, (DEVICES * 8, ROWS), 0)
    put_low = (sent_at == slot).astype(F32).astype(BF)
    put_high = (sent_at == slot + CAPACITY).astype(F32).astype(BF)
    own, other = own.ready(), other.ready()
    picked = (dot_nn(pick_own, rows_of(own)) + dot_nn(pick_other, rows_of(other))).astype(BF)
    picked_out[...] = picked
    picked_out.leave()
    _, _, pre_grad, base = tower_middle(picked, lengths, cot, project, up, down)
    rows_grad = base + dot_nt(pre_grad, up[...])
    rows_coarse = rows_grad.astype(BF)
    rows_fine = (rows_grad - rows_coarse.astype(F32)).astype(BF)
    low = dot_nt(rows_coarse, project[0:128]) + dot_nt(rows_fine, project[0:128])
    high = dot_nt(rows_coarse, project[64:192]) + dot_nt(rows_fine, project[64:192])
    lane = lax.broadcasted_iota(jnp.int32, (ROWS, 128), 1)
    tag = within.astype(F32)
    low = jnp.where(lane < 96, low, jnp.where(lane == 96, tag, 0.0)).astype(BF)
    high = jnp.where(lane >= 32, high, jnp.where(lane == 0, tag, 0.0)).astype(BF)

    back = (dot_nn(put_low, low) + dot_nn(put_high, high)).astype(BF)
    sent[...] = back.reshape(DEVICES, 8, 128)


def tower_sums(
    core, lengths, picked, cot, project, up, down,
    up_keep, up_send, factors, user_vec,
    halves,
):
    picked = picked[...]
    fetched, act, pre_grad, _ = tower_middle(picked, lengths, cot, project, up, down)
    user, length = per_user(lengths)
    at = lax.broadcasted_iota(jnp.int32, (8, ROWS), 1)
    live = ((at // LENGTH == user) & (at - user * LENGTH < length)).astype(F32).astype(BF)
    act_sum = dot_nn(live, act)
    picked_sum = dot_nn(live, picked)
    pieces = [act_sum[0:4, j * 128 : (j + 1) * 128] for j in range(8)]
    pieces += [picked_sum[0:4, j * 128 : (j + 1) * 128] for j in range(2)]
    factors[...] = jnp.concatenate(pieces + [jnp.zeros((8, 128), F32)], axis=0).astype(BF)
    coarse = act_sum.astype(BF)
    fine = (act_sum - coarse.astype(F32)).astype(BF)
    mixed = dot_nn(live, fetched) + dot_nn(coarse, down[...]) + dot_nn(fine, down[...])
    user_vec[...] = (mixed / length.astype(F32))[0:4]
    up_grad = dot_tn(picked, pre_grad).astype(BF)
    for j in range(FH // 128):
        halves[j // 4, (j % 4) * 256 : (j % 4 + 1) * 256] = up_grad[:, j * 128 : (j + 1) * 128]
    up_keep.leave(halves.at[core[0]])
    up_send.leave(halves.at[1 - core[0]])


def conv_backward(
    core, back, inner, taps, weights, o1, x, outer,
    keep, send,
    spatial_grad, wide, small, halves,
):
    taps1, frame1, taps2, frame2 = taps[0:9], taps[9:12], taps[12:21], taps[21:24]
    counts = taps[24:56, 0:1]

    def tile_sum(v):
        return jnp.sum(v.reshape(-1, 8, E), axis=0)

    small[...] = jnp.zeros(small.shape, F32)
    wide[...] = jnp.zeros(wide.shape, F32)
    got = back[...].reshape(DEVICES * 8, 128)
    row = lax.broadcasted_iota(jnp.int32, (DEVICES * 8, 1), 0)
    is_low = (row & 7) < CAPACITY
    got_f = got.astype(F32)
    tag = jnp.where(is_low, got_f[:, 96:97], got_f[:, 0:1]).astype(jnp.int32)
    named = tag == lax.broadcasted_iota(jnp.int32, (DEVICES * 8, ITEMS_HERE), 1)
    low = dot_tn((named & is_low).astype(F32).astype(BF), got)
    high = dot_tn((named & ~is_low).astype(F32).astype(BF), got)
    pooled_grad = jnp.concatenate([low[:, 0:96], high[:, 32:128]], axis=1)
    shared = pooled_grad / counts
    out_grad = jnp.concatenate(
        [(shared * (counts > f).astype(F32)).astype(BF) for f in range(FRAMES)], axis=0
    )
    inner.ready(), weights.ready(), o1.ready()
    p2, e2, p1 = weights[0:192], weights[192:384], weights[384:576]
    wide[576:768, 0:E] = dot_tn(out_grad, inner[AT_N2 : AT_N2 + 4].reshape(FRAMES * ITEMS_HERE, E))
    summed_grad = dot_nn(out_grad, p2).reshape(FRAMES, ITEMS_HERE, E) * inner[AT_H2 : AT_H2 + 4].astype(F32)
    spread = []
    for f in range(FRAMES):
        total = summed_grad[f] * frame2[1]
        if f + 1 < FRAMES:
            total = total + summed_grad[f + 1] * frame2[0]
        if f > 0:
            total = total + summed_grad[f - 1] * frame2[2]
        spread.append(total)
    for k in range(3):
        total = jnp.zeros((8, E), F32)
        for f in range(FRAMES):
            if 0 <= f + k - 1 < FRAMES:
                total = total + tile_sum(inner[AT_SP2 + f + k - 1].astype(F32) * summed_grad[f])
        small[21 + k] = total
    parts = []
    for f in range(FRAMES):
        for cell, tap in LINKS_SECOND:
            small[12 + tap] += tile_sum(inner[AT_G2 + f * 4 + cell].astype(F32) * spread[f])
            parts.append((spread[f] * taps2[tap] * inner[AT_D2 + f * 4 + cell].astype(F32)).astype(BF))
    grown_grad = jnp.concatenate(parts, axis=0)
    wide[384:576, 0:E] = dot_tn(o1[...], grown_grad)
    first_grad = dot_nt(grown_grad, e2).astype(BF)
    wide[192:384, 0:E] = dot_tn(first_grad, inner[AT_N1 : AT_N1 + 16].reshape(FRAMES * 4 * ITEMS_HERE, E))
    narrow_grad = dot_nn(first_grad, p1).reshape(FRAMES, 4, ITEMS_HERE, E)
    summed_grad = [narrow_grad[f] * inner[AT_H1 + f * 4 : AT_H1 + f * 4 + 4].astype(F32) for f in range(FRAMES)]
    for k in range(3):
        total = jnp.zeros((8, E), F32)
        for f in range(FRAMES):
            if 0 <= f + k - 1 < FRAMES:
                total = total + tile_sum(inner[AT_SP1 + f * 4 + 4 * k - 4 : AT_SP1 + f * 4 + 4 * k].astype(F32) * summed_grad[f])
        small[9 + k] = total
    for f in range(FRAMES):
        total = summed_grad[f] * frame1[1]
        if f + 1 < FRAMES:
            total = total + summed_grad[f + 1] * frame1[0]
        if f > 0:
            total = total + summed_grad[f - 1] * frame1[2]
        spatial_grad[f] = total.astype(BF)

    x.ready(), outer.ready()
    half_taps = taps1.astype(BF)

    def grow_back(f, _):
        live = counts > lax.convert_element_type(f, F32)
        x_f = x[pl.ds(f * CELLS, CELLS)]
        x_f = jnp.where(live[None], x_f, jnp.zeros_like(x_f)).reshape(CELLS * ITEMS_HERE, C)
        outs = [spatial_grad[f, cell] for cell in range(4)]
        sums = [None] * 9
        grads = [None] * CELLS
        for out_cell, in_cell, tap in LINKS_FIRST:
            term = outs[out_cell] * half_taps[tap]
            grads[in_cell] = term if grads[in_cell] is None else grads[in_cell] + term
            term = outer[f * CELLS + in_cell] * outs[out_cell]
            sums[tap] = term if sums[tap] is None else sums[tap] + term
        for tap in range(9):
            small[tap] += tile_sum(sums[tap].astype(F32))
        grads = [grads[cell] * outer[(FRAMES + f) * CELLS + cell] for cell in range(CELLS)]
        wide[0:192, 0:E] += dot_tn(x_f, jnp.concatenate(grads, axis=0))
        return 0

    lax.fori_loop(0, FRAMES, grow_back, 0, unroll=True)
    sums = jnp.sum(small[...], axis=1).astype(BF)
    put = lax.broadcasted_iota(jnp.int32, (32, 128), 1) == lax.broadcasted_iota(jnp.int32, (32, 128), 0) + 64
    wide[0:E, 384:512] += dot_tn(sums, put.astype(F32).astype(BF))
    for j in range(4):
        halves[j // 2, (j % 2) * 768 : (j % 2 + 1) * 768] = wide[:, j * 128 : (j + 1) * 128].astype(BF)
    keep[...] = halves[core[0]]
    send[...] = halves[1 - core[0]]


def merge(conv_a, conv_b, up_a, up_b, factors, out):
    conv = (conv_a[...].astype(F32) + conv_b[...].astype(F32)).astype(BF)
    up = (up_a[...].astype(F32) + up_b[...].astype(F32)).astype(BF)
    out[:, 0:24, :] = conv.reshape(CHIPS, 24, 128)
    out[:, 24:40, :] = up.reshape(CHIPS, 16, 128)
    out[:, 40:80, :] = jnp.broadcast_to(factors[0:40][None], (CHIPS, 40, 128))


def sum_chips(third, out, factors):
    factors[...] = third[:, 40:80, :]
    factors.leave()
    total = jnp.sum(third[:, 0:40, :].astype(F32), axis=0).astype(BF)
    out[...] = jnp.broadcast_to(total[None], (CHIPS, 40, 128))


def finish_low_rank(own, other, factors, factors_other, grad_down, item_base):
    row = lax.broadcasted_iota(jnp.int32, (CHIPS * 8, 128), 0) & 7
    lane = lax.broadcasted_iota(jnp.int32, (CHIPS * 8, 128), 1)
    even = []
    for src in (own, other):
        parts = []
        for k in range(4):
            got = src[:, 32 + 8 * k : 40 + 8 * k, :].reshape(CHIPS * 8, 128).astype(F32)
            left = pltpu.roll(got, 64, 1)
            right = pltpu.roll(got, CHIPS * 8 - 4, 0)
            parts.append(jnp.where(row < 4, jnp.where(lane < 64, left, right), 0.0))
        even.append(jnp.concatenate(parts, axis=1))
    odd = jnp.concatenate([pltpu.roll(v, 4, 0) for v in even], axis=0).astype(BF)
    even = jnp.concatenate(even, axis=0).astype(BF)
    for j in range(5):
        cut = slice(8 * j, 8 * j + 8)
        left = jnp.concatenate(
            [src[:, cut, :].reshape(CHIPS * 8, 128) for src in (factors, factors_other)], axis=0
        )
        first, second = dot_tn(left, even), dot_tn(left, odd)
        if j < 4:
            grad_down[j * 256 : j * 256 + 128] = first
            grad_down[j * 256 + 128 : j * 256 + 256] = second
        else:
            item_base[0:128] = first
            item_base[128:C] = second[0:64]


def finish(
    core, mine, theirs, item_base, project, up,
    ge1, gs1, gt1, gp1, ge2, gs2, gt2, gp2, grad_item, grad_up,
    halves, part_sems,
):
    halves[core[0]] = mine[...]
    halves[1 - core[0]] = theirs[...]
    for j in range(4):
        width = min(128, E - j * 128)
        part = halves[j // 2, :, 0:24, :].reshape(1536, 128)[(j % 2) * 768 : (j % 2 + 1) * 768].astype(F32)
        cut = slice(j * 128, j * 128 + width)
        for i, out in enumerate((ge1, gp1, ge2, gp2)):
            out[:, cut] = part[i * 192 : (i + 1) * 192, 0:width]
    same = lax.broadcasted_iota(jnp.int32, (E, E), 0) == lax.broadcasted_iota(jnp.int32, (E, E), 1)
    for out in (ge1, gp1, ge2, gp2):
        out.leave()
    small = dot_tn(part[0:E].astype(BF), same.astype(F32).astype(BF))
    gs1[...] = small[64:73]
    gt1[...] = small[73:76]
    gs2[...] = small[76:85]
    gt2[...] = small[85:88]
    item = item_base[...]
    parts = []
    for j in range(FH // 128):
        part = halves[j // 4, :, 24:40, :].reshape(1024, 128)[(j % 4) * 256 : (j % 4) * 256 + C]
        cut = slice(j * 128, (j + 1) * 128)
        grad_up[:, cut] = dot_tn(project[...], part)
        item = item + dot_nt(part, up[:, cut])
        if j % 2:
            parts.append(grad_up.leave_part((slice(None), pl.ds((j - 1) * 128, 256)), part_sems.at[j // 2]))
    grad_item[...] = item
    grad_item.leave()
    for part in parts:
        part.wait()


def shape(dims, dtype=BF):
    return jax.ShapeDtypeStruct(dims, dtype)


class Arriving:
    def __init__(self, copy, ref):
        self.copy, self.ref, self.begun = copy, ref, False

    def begin(self):
        if not self.begun:
            self.copy.start()
            self.begun = True

    def ready(self):
        if self.copy is not None:
            self.begin()
            self.copy.wait()
            self.copy = None
        return self.ref

    def __getitem__(self, index):
        return self.ready()[index]


class Leaving:
    def __init__(self, ref, target, semaphore):
        self.ref, self.target, self.semaphore, self.copy = ref, target, semaphore, None

    def __setitem__(self, index, value):
        self.ref[index] = value

    def leave_part(self, index, semaphore):
        part = pltpu.make_async_copy(self.ref.at[index], self.target.at[index], semaphore)
        part.start()
        return part

    def leave(self, source=None):
        source = self.ref if source is None else source
        self.copy = pltpu.make_async_copy(source, self.target, self.semaphore)
        self.copy.start()


def call(kernel, outs, places, out_places, scratch=(), unstaged=(), megabytes=58):
    staged_in = [i for i, p in enumerate(places) if p in "hw"]
    staged_out = [i for i, p in enumerate(out_places) if p in "hw"]
    spaces = {"s": pltpu.SMEM, "v": pltpu.VMEM, "h": pl.ANY, "w": pl.ANY}

    def run(*args):
        stages = [pltpu.VMEM(args[i].shape, args[i].dtype) for i in staged_in]
        stages += [pltpu.VMEM((16, 128) if i in unstaged else outs[i].shape, outs[i].dtype) for i in staged_out]
        sems = [pltpu.SemaphoreType.DMA((max(len(v), 1),)) for v in (staged_in, staged_out)]

        def body(*refs):
            ins, rest = list(refs[: len(args)]), list(refs[len(args) :])
            results, rest = rest[: len(outs)], rest[len(outs) :]
            own, rest = rest[: len(scratch)], rest[len(scratch) :]
            sem_in, sem_out = rest[-2:]
            for k, i in enumerate(staged_in):
                copy = pltpu.make_async_copy(ins[i], rest[k], sem_in.at[k])
                ins[i] = Arriving(copy, rest[k])
                if places[i] == "h":
                    ins[i].begin()
            for k, i in enumerate(staged_out):
                results[i] = Leaving(rest[len(staged_in) + k], results[i], sem_out.at[k])
            kernel(*ins, *results, *own)
            for i in staged_in:
                ins[i].ready()
            for i in staged_out:
                if results[i].copy is None and out_places[i] == "h":
                    results[i].leave()
            for i in staged_out:
                if results[i].copy is not None:
                    results[i].copy.wait()

        return pl.pallas_call(
            body,
            out_shape=outs,
            in_specs=[pl.BlockSpec(memory_space=spaces[p]) for p in places],
            out_specs=[pl.BlockSpec(memory_space=spaces[p]) for p in out_places],
            scratch_shapes=list(scratch) + stages + sems,
            cost_estimate=pl.CostEstimate(flops=10**9, bytes_accessed=10**7, transcendentals=10**6),
            compiler_params=pltpu.CompilerParams(vmem_limit_bytes=megabytes * 1024 * 1024),
        )(*args)

    return run


def local(
    clips, clip_counts, histories, lengths, user_cotangent,
    expand_first, spatial_first, temporal_first, project_first,
    expand_second, spatial_second, temporal_second, project_second,
    item_project, tower_up, tower_down,
):
    same_core = [[i for i in range(DEVICES) if i % 2 == c] for c in range(2)]
    core = (lax.axis_index("seq") % 2).reshape(1)

    def across_chips(v):
        return lax.all_to_all(v, AXES, 0, 0, axis_index_groups=same_core, tiled=True)

    def swap(v):
        return lax.ppermute(v, "seq", [(i, i ^ 1) for i in range(8)])

    x = clips.reshape(ITEMS_HERE, FRAMES * CELLS, C).transpose(1, 0, 2)
    counts = clip_counts.reshape(1, ITEMS_HERE)
    weights = (
        spatial_first, temporal_first, project_first.T,
        expand_second, spatial_second, temporal_second, project_second.T,
    )
    n = ITEMS_HERE
    framed = [pltpu.VMEM((FRAMES + 2, 4, n, E), F32), pltpu.VMEM((FRAMES + 2, n, E), F32)]
    (block,) = call(conv_forward, [shape((CHIPS, 64, 128))], "svvvvvvvvvvv", "v", framed, megabytes=24)(
        lengths, x, counts, user_cotangent, expand_first, *weights
    )
    kept = call(
        conv_forward,
        [shape((56, E), F32), shape((576, E)), shape((2 * 64, n, E)), shape((INNER, n, E)), shape((512, C))],
        "shvvhvvhhvvh",
        "h" * 5,
        framed,
    )(lengths, x, counts, user_cotangent, expand_first, *weights)
    own = across_chips(block)
    own, (taps, kept_weights, outer, inner, o1) = lax.optimization_barrier((own, kept))
    other = swap(own)
    sent, picked = call(tower, [shape((DEVICES, 8, 128)), shape((ROWS, 256))], "sshhvvhhh", "hh")(
        core, lengths, own, other, histories, user_cotangent, item_project, tower_up, tower_down
    )
    back = lax.all_to_all(sent, AXES, 0, 0, tiled=True)
    up_keep, up_send, factors, user_vec = call(
        tower_sums,
        [shape((1024, 128)), shape((1024, 128)), shape((48, 128)), shape((USERS_HERE, D), F32)],
        "sshvhhh",
        "hhhv",
        [pltpu.VMEM((2, 1024, 128), BF)],
        unstaged=(0, 1),
    )(core, lengths, picked, user_cotangent, item_project, tower_up, tower_down)
    back, up_send = lax.optimization_barrier((back, up_send))
    up_other = swap(up_send)
    conv_keep, conv_send = call(
        conv_backward,
        [shape((1536, 128)), shape((1536, 128))],
        "sv" + "h" * 6,
        "vv",
        [
            pltpu.VMEM((4, 4, n, E), BF),
            pltpu.VMEM((768, 512), F32),
            pltpu.VMEM((32, 8, E), F32),
            pltpu.VMEM((2, 1536, 128), BF),
        ],
        megabytes=50,
    )(core, back, inner, taps, kept_weights, o1, x, outer)
    (third,) = call(merge, [shape((CHIPS, 80, 128))], "vvvvv", "v", megabytes=16)(
        conv_keep, swap(conv_send), up_keep, up_other, factors
    )
    third = across_chips(third)
    fourth, factors = call(
        sum_chips, [shape((CHIPS, 40, 128)), shape((CHIPS, 40, 128))], "v", "vh", megabytes=16
    )(third)
    fourth = across_chips(fourth)
    grad_down, item_base = call(finish_low_rank, [shape((FH, D), F32), shape((C, D), F32)], "hhhh", "hh")(
        own, other, factors, swap(factors)
    )
    fourth, _ = lax.optimization_barrier((fourth, item_base))
    *conv_grads, grad_item, grad_up = call(
        finish,
        [shape((C, E), F32), shape((9, E), F32), shape((3, E), F32), shape((C, E), F32)] * 2
        + [shape((C, D), F32), shape((D, FH), F32)],
        "svvhhh",
        "hvvhhvvhhw",
        [pltpu.VMEM((2, CHIPS, 40, 128), BF), pltpu.SemaphoreType.DMA((4,))],
        megabytes=32,
    )(core, fourth, swap(fourth), item_base, item_project, tower_up)
    conv_grads[3] = conv_grads[3].T
    conv_grads[7] = conv_grads[7].T
    return (user_vec, *conv_grads, grad_item, grad_up, grad_down)


def solution(mesh):
    spread = P(AXES)
    return jax.shard_map(
        local,
        mesh=mesh,
        in_specs=(spread,) * 5 + (P(),) * 11,
        out_specs=(spread,) + (P(),) * 11,
        check_vma=False,
    )
```

```python
import jax
import jax.numpy as jnp
from jax import lax
from jax.experimental import pallas as pl
from jax.experimental.pallas import tpu as pltpu
from jax.sharding import PartitionSpec as P

BF = jnp.bfloat16
F32 = jnp.float32
AXES = ("bulk", "seq")
C, E, D, FH = 192, 432, 512, 1024
FRAMES, SIDE, ITEMS_HERE, USERS_HERE, LENGTH = 4, 4, 32, 4, 64
DEVICES, CHIPS, CAPACITY = 128, 64, 4
ROWS = USERS_HERE * LENGTH
CELLS = SIDE * SIDE
HALF = 2
LINKS_FIRST = [
    (HALF * p + q, SIDE * (2 * p + a - 1) + 2 * q + b - 1, 3 * a + b)
    for p in range(HALF)
    for q in range(HALF)
    for a in range(3)
    for b in range(3)
    if 0 <= 2 * p + a - 1 < SIDE and 0 <= 2 * q + b - 1 < SIDE
]
LINKS_SECOND = [(0, 4), (1, 5), (2, 7), (3, 8)]


AT_N2, AT_H2, AT_SP2, AT_G2, AT_D2, AT_N1, AT_H1, AT_SP1, INNER = 0, 4, 8, 12, 28, 44, 60, 76, 92


def dot_nn(a, b):
    return lax.dot_general(a, b, (((1,), (0,)), ((), ())), preferred_element_type=F32)


def dot_nt(a, b):
    return lax.dot_general(a, b, (((1,), (1,)), ((), ())), preferred_element_type=F32)


def dot_tn(a, b):
    return lax.dot_general(a, b, (((0,), (0,)), ((), ())), preferred_element_type=F32)


def silu_and_slope(v):
    gate = 0.5 * jnp.tanh(0.5 * v) + 0.5
    value = v * gate
    return value, gate + value - value * gate


def column_of(row):
    n = row.shape[1]
    same = lax.broadcasted_iota(jnp.int32, (n, n), 0) == lax.broadcasted_iota(jnp.int32, (n, n), 1)
    return jnp.sum(jnp.where(same, row.astype(F32), 0.0), axis=1, keepdims=True).astype(jnp.int32)


def per_user(lengths):
    user = lax.broadcasted_iota(jnp.int32, (8, 1), 0)
    length = jnp.ones((8, 1), jnp.int32)
    for u in range(USERS_HERE):
        length = jnp.where(user == u, lengths[u], length)
    return user, length


def conv_forward(
    lengths, x, counts_row, cot, e1, s1, t1, p1, e2, s2, t2, p2, *rest,
):
    *kept, framed1, framed2 = rest
    block = None
    if len(kept) == 1:
        (block,) = kept
    else:
        taps, weights, outer, inner, o1 = kept
    counts = column_of(counts_row[...])
    zero4 = jnp.zeros((HALF * HALF, ITEMS_HERE, E), F32)
    framed1[0] = zero4
    framed1[FRAMES + 1] = zero4
    zero1 = jnp.zeros((ITEMS_HERE, E), F32)
    framed2[0] = zero1
    framed2[FRAMES + 1] = zero1
    taps1 = s1[...].astype(F32)
    taps2 = s2[...].astype(F32)
    frame1 = t1[...].astype(F32)
    frame2 = t2[...].astype(F32)
    if block is None:
        taps[...] = jnp.zeros((56, E), F32)
        for at, ref in ((0, s1), (9, t1), (12, s2), (21, t2)):
            taps[at : at + ref.shape[0]] = ref[...].astype(F32)
        taps[24:56, 0:128] = jnp.broadcast_to(counts.astype(F32), (ITEMS_HERE, 128))

    if block is None:
        x.ready(), e1.ready()

    def grow(f, _):
        live = f < counts
        x_f = x[pl.ds(f * CELLS, CELLS)]
        x_f = jnp.where(live[None], x_f, jnp.zeros_like(x_f))
        pre = dot_nn(x_f.reshape(CELLS * ITEMS_HERE, C), e1[...])
        value, slope = silu_and_slope(pre)
        value = value.astype(BF).reshape(CELLS, ITEMS_HERE, E)
        if block is None:
            outer[pl.ds(f * CELLS, CELLS)] = value
            outer[pl.ds((FRAMES + f) * CELLS, CELLS)] = slope.astype(BF).reshape(CELLS, ITEMS_HERE, E)
        outs = [jnp.zeros((ITEMS_HERE, E), F32)] * 4
        for out_cell, in_cell, tap in LINKS_FIRST:
            outs[out_cell] = outs[out_cell] + value[in_cell].astype(F32) * taps1[tap]
        for out_cell in range(4):
            framed1[f + 1, out_cell] = outs[out_cell]
            if block is None:
                inner[AT_SP1 + f * 4 + out_cell] = outs[out_cell].astype(BF)
        return 0

    lax.fori_loop(0, FRAMES, grow, 0, unroll=True)
    narrow = []
    for f in range(FRAMES):
        summed = framed1[f] * frame1[0] + framed1[f + 1] * frame1[1] + framed1[f + 2] * frame1[2]
        value, slope = silu_and_slope(summed)
        narrow.append(value.astype(BF))
        if block is None:
            inner[AT_H1 + f * 4 : AT_H1 + f * 4 + 4] = slope.astype(BF)
    narrow = jnp.concatenate(narrow, axis=0)
    first = dot_nt(narrow.reshape(FRAMES * 4 * ITEMS_HERE, E), p1[...]).astype(BF)
    value, slope = silu_and_slope(dot_nn(first, e2[...]))
    value = value.astype(BF).reshape(FRAMES * 4, ITEMS_HERE, E)
    if block is None:
        inner[AT_N1 : AT_N1 + 16] = narrow
        o1[...] = first
        inner[AT_G2 : AT_G2 + 16] = value
        inner[AT_D2 : AT_D2 + 16] = slope.astype(BF).reshape(FRAMES * 4, ITEMS_HERE, E)
        weights[0:192] = p2[...]
        weights[192:384] = e2[...]
        weights[384:576] = p1[...]
    for f in range(FRAMES):
        total = jnp.zeros((ITEMS_HERE, E), F32)
        for cell, tap in LINKS_SECOND:
            total = total + value[f * 4 + cell].astype(F32) * taps2[tap]
        framed2[f + 1] = total
        if block is None:
            inner[AT_SP2 + f] = total.astype(BF)
    narrow = []
    for f in range(FRAMES):
        summed = framed2[f] * frame2[0] + framed2[f + 1] * frame2[1] + framed2[f + 2] * frame2[2]
        value, slope = silu_and_slope(summed)
        narrow.append(value.astype(BF))
        if block is None:
            inner[AT_N2 + f] = value.astype(BF)
            inner[AT_H2 + f] = slope.astype(BF)
    if block is None:
        return
    second = dot_nt(jnp.concatenate(narrow, axis=0), p2[...]).astype(BF)
    pooled = jnp.zeros((ITEMS_HERE, C), F32)
    for f in range(FRAMES):
        live = (f < counts).astype(F32)
        pooled = pooled + live * second[f * ITEMS_HERE : (f + 1) * ITEMS_HERE].astype(F32)
    pooled = pooled / counts.astype(F32)
    _, length = per_user(lengths)
    shared = cot[...] / length[0:4].astype(F32)
    pieces = []
    for k in range(8):
        piece = shared[:, (k // 2) * 128 : (k // 2 + 1) * 128]
        pieces.append(piece if k % 2 else pltpu.roll(piece, 64, 1))
    lane = lax.broadcasted_iota(jnp.int32, (ITEMS_HERE, 128), 1)
    shared = jnp.concatenate(pieces, axis=0)
    high = jnp.concatenate([pooled[:, 128:192], pooled[:, 0:64]], axis=1)
    rows = jnp.concatenate([pooled[:, 0:128], jnp.where(lane < 64, high, shared)], axis=0).astype(BF)
    block[...] = jnp.broadcast_to(rows[None], (CHIPS, 64, 128))


def tower_middle(picked, lengths, cot, project, up, down):
    fetched = dot_nn(picked[:, 0:C], project[...]).astype(BF)
    pre = dot_nn(fetched, up[...])
    scale = 0.7978845608028654
    square = pre * pre
    bent = jnp.tanh(scale * pre * (1.0 + 0.044715 * square))
    gate = 0.5 * (1.0 + bent)
    act = (pre * gate).astype(BF)
    slope = gate + 0.5 * pre * (1.0 - bent * bent) * (scale * (1.0 + 3 * 0.044715 * square))
    _, length = per_user(lengths)
    shared = cot[...] / length[0:4].astype(F32)
    shared_half = shared.astype(BF)
    act_grad = dot_nt(jnp.concatenate([shared_half, shared_half], axis=0), down[...])
    position = lax.broadcasted_iota(jnp.int32, (LENGTH, 1), 0)
    pre_parts, base_parts = [], []
    for u in range(USERS_HERE):
        alive = (position < lengths[u]).astype(F32)
        pre_parts.append(alive * act_grad[u : u + 1] * slope[u * LENGTH : (u + 1) * LENGTH])
        base_parts.append(alive * shared[u : u + 1])
    pre_grad = jnp.concatenate(pre_parts, axis=0).astype(BF)
    return fetched, act, pre_grad, jnp.concatenate(base_parts, axis=0)


def tower(
    core, lengths, own, other, ids_ref, cot, project, up, down,
    sent, picked_out,
):
    ids = jnp.concatenate([column_of(ids_ref[u : u + 1]) for u in range(USERS_HERE)], axis=0)
    owner = ids // ITEMS_HERE
    within = ids - owner * ITEMS_HERE
    chip = owner // 2
    place = chip * ITEMS_HERE + within
    mine = (owner - chip * 2) == core[0]
    lanes = lax.broadcasted_iota(jnp.int32, (ROWS, CHIPS * ITEMS_HERE), 1)
    pick_own = (lanes == jnp.where(mine, place, -1)).astype(F32).astype(BF)
    pick_other = (lanes == jnp.where(mine, -1, place)).astype(F32).astype(BF)

    def rows_of(ref):
        low = ref[:, 0:32, :].reshape(CHIPS * ITEMS_HERE, 128)
        high = ref[:, 32:64, :].reshape(CHIPS * ITEMS_HERE, 128)
        return jnp.concatenate([low, high], axis=1)

    across = lax.broadcasted_iota(jnp.int32, (ROWS, ROWS), 1)
    down_rows = lax.broadcasted_iota(jnp.int32, (ROWS, ROWS), 0)
    owner_row = jnp.sum(jnp.where(across == down_rows, owner.astype(F32), 0.0), axis=0, keepdims=True).astype(jnp.int32)
    earlier = down_rows < across
    rank = jnp.sum(((owner == owner_row) & earlier).astype(F32), axis=0, keepdims=True).astype(jnp.int32)
    slot = owner_row * 8 + rank
    sent_at = lax.broadcasted_iota(jnp.int32, (DEVICES * 8, ROWS), 0)
    put_low = (sent_at == slot).astype(F32).astype(BF)
    put_high = (sent_at == slot + CAPACITY).astype(F32).astype(BF)
    own, other = own.ready(), other.ready()
    picked = (dot_nn(pick_own, rows_of(own)) + dot_nn(pick_other, rows_of(other))).astype(BF)
    picked_out[...] = picked
    picked_out.leave()
    _, _, pre_grad, base = tower_middle(picked, lengths, cot, project, up, down)
    rows_grad = base + dot_nt(pre_grad, up[...])
    rows_coarse = rows_grad.astype(BF)
    rows_fine = (rows_grad - rows_coarse.astype(F32)).astype(BF)
    low = dot_nt(rows_coarse, project[0:128]) + dot_nt(rows_fine, project[0:128])
    high = dot_nt(rows_coarse, project[64:192]) + dot_nt(rows_fine, project[64:192])
    lane = lax.broadcasted_iota(jnp.int32, (ROWS, 128), 1)
    tag = within.astype(F32)
    low = jnp.where(lane < 96, low, jnp.where(lane == 96, tag, 0.0)).astype(BF)
    high = jnp.where(lane >= 32, high, jnp.where(lane == 0, tag, 0.0)).astype(BF)

    back = (dot_nn(put_low, low) + dot_nn(put_high, high)).astype(BF)
    sent[...] = back.reshape(DEVICES, 8, 128)


def tower_sums(
    core, lengths, picked, cot, project, up, down,
    up_keep, up_send, factors, user_vec,
    halves,
):
    picked = picked[...]
    fetched, act, pre_grad, _ = tower_middle(picked, lengths, cot, project, up, down)
    user, length = per_user(lengths)
    at = lax.broadcasted_iota(jnp.int32, (8, ROWS), 1)
    live = ((at // LENGTH == user) & (at - user * LENGTH < length)).astype(F32).astype(BF)
    act_sum = dot_nn(live, act)
    picked_sum = dot_nn(live, picked)
    pieces = [act_sum[0:4, j * 128 : (j + 1) * 128] for j in range(8)]
    pieces += [picked_sum[0:4, j * 128 : (j + 1) * 128] for j in range(2)]
    factors[...] = jnp.concatenate(pieces + [jnp.zeros((8, 128), F32)], axis=0).astype(BF)
    coarse = act_sum.astype(BF)
    fine = (act_sum - coarse.astype(F32)).astype(BF)
    mixed = dot_nn(live, fetched) + dot_nn(coarse, down[...]) + dot_nn(fine, down[...])
    user_vec[...] = (mixed / length.astype(F32))[0:4]
    up_grad = dot_tn(picked, pre_grad).astype(BF)
    for j in range(FH // 128):
        halves[j // 4, (j % 4) * 256 : (j % 4 + 1) * 256] = up_grad[:, j * 128 : (j + 1) * 128]
    up_keep.leave(halves.at[core[0]])
    up_send.leave(halves.at[1 - core[0]])


def conv_backward(
    core, back, inner, taps, weights, o1, x, outer,
    keep, send,
    spatial_grad, wide, small, halves,
):
    taps1, frame1, taps2, frame2 = taps[0:9], taps[9:12], taps[12:21], taps[21:24]
    counts = taps[24:56, 0:1]

    def tile_sum(v):
        return jnp.sum(v.reshape(-1, 8, E), axis=0)

    small[...] = jnp.zeros(small.shape, F32)
    wide[...] = jnp.zeros(wide.shape, F32)
    got = back[...].reshape(DEVICES * 8, 128)
    row = lax.broadcasted_iota(jnp.int32, (DEVICES * 8, 1), 0)
    is_low = (row & 7) < CAPACITY
    got_f = got.astype(F32)
    tag = jnp.where(is_low, got_f[:, 96:97], got_f[:, 0:1]).astype(jnp.int32)
    named = tag == lax.broadcasted_iota(jnp.int32, (DEVICES * 8, ITEMS_HERE), 1)
    low = dot_tn((named & is_low).astype(F32).astype(BF), got)
    high = dot_tn((named & ~is_low).astype(F32).astype(BF), got)
    pooled_grad = jnp.concatenate([low[:, 0:96], high[:, 32:128]], axis=1)
    shared = pooled_grad / counts
    out_grad = jnp.concatenate(
        [(shared * (counts > f).astype(F32)).astype(BF) for f in range(FRAMES)], axis=0
    )
    inner.ready(), weights.ready(), o1.ready()
    p2, e2, p1 = weights[0:192], weights[192:384], weights[384:576]
    wide[576:768, 0:E] = dot_tn(out_grad, inner[AT_N2 : AT_N2 + 4].reshape(FRAMES * ITEMS_HERE, E))
    summed_grad = dot_nn(out_grad, p2).reshape(FRAMES, ITEMS_HERE, E) * inner[AT_H2 : AT_H2 + 4].astype(F32)
    spread = []
    for f in range(FRAMES):
        total = summed_grad[f] * frame2[1]
        if f + 1 < FRAMES:
            total = total + summed_grad[f + 1] * frame2[0]
        if f > 0:
            total = total + summed_grad[f - 1] * frame2[2]
        spread.append(total)
    for k in range(3):
        total = jnp.zeros((8, E), F32)
        for f in range(FRAMES):
            if 0 <= f + k - 1 < FRAMES:
                total = total + tile_sum(inner[AT_SP2 + f + k - 1].astype(F32) * summed_grad[f])
        small[21 + k] = total
    parts = []
    for f in range(FRAMES):
        for cell, tap in LINKS_SECOND:
            small[12 + tap] += tile_sum(inner[AT_G2 + f * 4 + cell].astype(F32) * spread[f])
            parts.append((spread[f] * taps2[tap] * inner[AT_D2 + f * 4 + cell].astype(F32)).astype(BF))
    grown_grad = jnp.concatenate(parts, axis=0)
    wide[384:576, 0:E] = dot_tn(o1[...], grown_grad)
    first_grad = dot_nt(grown_grad, e2).astype(BF)
    wide[192:384, 0:E] = dot_tn(first_grad, inner[AT_N1 : AT_N1 + 16].reshape(FRAMES * 4 * ITEMS_HERE, E))
    narrow_grad = dot_nn(first_grad, p1).reshape(FRAMES, 4, ITEMS_HERE, E)
    summed_grad = [narrow_grad[f] * inner[AT_H1 + f * 4 : AT_H1 + f * 4 + 4].astype(F32) for f in range(FRAMES)]
    for k in range(3):
        total = jnp.zeros((8, E), F32)
        for f in range(FRAMES):
            if 0 <= f + k - 1 < FRAMES:
                total = total + tile_sum(inner[AT_SP1 + f * 4 + 4 * k - 4 : AT_SP1 + f * 4 + 4 * k].astype(F32) * summed_grad[f])
        small[9 + k] = total
    for f in range(FRAMES):
        total = summed_grad[f] * frame1[1]
        if f + 1 < FRAMES:
            total = total + summed_grad[f + 1] * frame1[0]
        if f > 0:
            total = total + summed_grad[f - 1] * frame1[2]
        spatial_grad[f] = total.astype(BF)

    x.ready(), outer.ready()
    half_taps = taps1.astype(BF)

    def grow_back(f, _):
        live = counts > lax.convert_element_type(f, F32)
        x_f = x[pl.ds(f * CELLS, CELLS)]
        x_f = jnp.where(live[None], x_f, jnp.zeros_like(x_f)).reshape(CELLS * ITEMS_HERE, C)
        outs = [spatial_grad[f, cell] for cell in range(4)]
        sums = [None] * 9
        grads = [None] * CELLS
        for out_cell, in_cell, tap in LINKS_FIRST:
            term = outs[out_cell] * half_taps[tap]
            grads[in_cell] = term if grads[in_cell] is None else grads[in_cell] + term
            term = outer[f * CELLS + in_cell] * outs[out_cell]
            sums[tap] = term if sums[tap] is None else sums[tap] + term
        for tap in range(9):
            small[tap] += tile_sum(sums[tap].astype(F32))
        grads = [grads[cell] * outer[(FRAMES + f) * CELLS + cell] for cell in range(CELLS)]
        wide[0:192, 0:E] += dot_tn(x_f, jnp.concatenate(grads, axis=0))
        return 0

    lax.fori_loop(0, FRAMES, grow_back, 0, unroll=True)
    sums = jnp.sum(small[...], axis=1).astype(BF)
    put = lax.broadcasted_iota(jnp.int32, (32, 128), 1) == lax.broadcasted_iota(jnp.int32, (32, 128), 0) + 64
    wide[0:E, 384:512] += dot_tn(sums, put.astype(F32).astype(BF))
    for j in range(4):
        halves[j // 2, (j % 2) * 768 : (j % 2 + 1) * 768] = wide[:, j * 128 : (j + 1) * 128].astype(BF)
    keep[...] = halves[core[0]]
    send[...] = halves[1 - core[0]]


def merge(conv_a, conv_b, up_a, up_b, factors, out):
    conv = (conv_a[...].astype(F32) + conv_b[...].astype(F32)).astype(BF)
    up = (up_a[...].astype(F32) + up_b[...].astype(F32)).astype(BF)
    out[:, 0:24, :] = conv.reshape(CHIPS, 24, 128)
    out[:, 24:40, :] = up.reshape(CHIPS, 16, 128)
    out[:, 40:80, :] = jnp.broadcast_to(factors[0:40][None], (CHIPS, 40, 128))


def sum_chips(third, out, factors):
    factors[...] = third[:, 40:80, :]
    factors.leave()
    total = jnp.sum(third[:, 0:40, :].astype(F32), axis=0).astype(BF)
    out[...] = jnp.broadcast_to(total[None], (CHIPS, 40, 128))


def finish_low_rank(own, other, factors, factors_other, grad_down, item_base):
    row = lax.broadcasted_iota(jnp.int32, (CHIPS * 8, 128), 0) & 7
    lane = lax.broadcasted_iota(jnp.int32, (CHIPS * 8, 128), 1)
    even = []
    for src in (own, other):
        parts = []
        for k in range(4):
            got = src[:, 32 + 8 * k : 40 + 8 * k, :].reshape(CHIPS * 8, 128).astype(F32)
            left = pltpu.roll(got, 64, 1)
            right = pltpu.roll(got, CHIPS * 8 - 4, 0)
            parts.append(jnp.where(row < 4, jnp.where(lane < 64, left, right), 0.0))
        even.append(jnp.concatenate(parts, axis=1))
    odd = jnp.concatenate([pltpu.roll(v, 4, 0) for v in even], axis=0).astype(BF)
    even = jnp.concatenate(even, axis=0).astype(BF)
    for j in range(5):
        cut = slice(8 * j, 8 * j + 8)
        left = jnp.concatenate(
            [src[:, cut, :].reshape(CHIPS * 8, 128) for src in (factors, factors_other)], axis=0
        )
        first, second = dot_tn(left, even), dot_tn(left, odd)
        if j < 4:
            grad_down[j * 256 : j * 256 + 128] = first
            grad_down[j * 256 + 128 : j * 256 + 256] = second
        else:
            item_base[0:128] = first
            item_base[128:C] = second[0:64]


def finish(
    core, mine, theirs, item_base, project, up,
    ge1, gs1, gt1, gp1, ge2, gs2, gt2, gp2, grad_item, grad_up,
    halves, part_sems,
):
    halves[core[0]] = mine[...]
    halves[1 - core[0]] = theirs[...]
    for j in range(4):
        width = min(128, E - j * 128)
        part = halves[j // 2, :, 0:24, :].reshape(1536, 128)[(j % 2) * 768 : (j % 2 + 1) * 768].astype(F32)
        cut = slice(j * 128, j * 128 + width)
        for i, out in enumerate((ge1, gp1, ge2, gp2)):
            out[:, cut] = part[i * 192 : (i + 1) * 192, 0:width]
    same = lax.broadcasted_iota(jnp.int32, (E, E), 0) == lax.broadcasted_iota(jnp.int32, (E, E), 1)
    for out in (ge1, gp1, ge2, gp2):
        out.leave()
    small = dot_tn(part[0:E].astype(BF), same.astype(F32).astype(BF))
    gs1[...] = small[64:73]
    gt1[...] = small[73:76]
    gs2[...] = small[76:85]
    gt2[...] = small[85:88]
    item = item_base[...]
    parts = []
    for j in range(FH // 128):
        part = halves[j // 4, :, 24:40, :].reshape(1024, 128)[(j % 4) * 256 : (j % 4) * 256 + C]
        cut = slice(j * 128, (j + 1) * 128)
        grad_up[:, cut] = dot_tn(project[...], part)
        item = item + dot_nt(part, up[:, cut])
        if j % 2:
            parts.append(grad_up.leave_part((slice(None), pl.ds((j - 1) * 128, 256)), part_sems.at[j // 2]))
    grad_item[...] = item
    grad_item.leave()
    for part in parts:
        part.wait()


def shape(dims, dtype=BF):
    return jax.ShapeDtypeStruct(dims, dtype)


class Arriving:
    def __init__(self, copy, ref):
        self.copy, self.ref, self.begun = copy, ref, False

    def begin(self):
        if not self.begun:
            self.copy.start()
            self.begun = True

    def ready(self):
        if self.copy is not None:
            self.begin()
            self.copy.wait()
            self.copy = None
        return self.ref

    def __getitem__(self, index):
        return self.ready()[index]


class Leaving:
    def __init__(self, ref, target, semaphore):
        self.ref, self.target, self.semaphore, self.copy = ref, target, semaphore, None

    def __setitem__(self, index, value):
        self.ref[index] = value

    def leave_part(self, index, semaphore):
        part = pltpu.make_async_copy(self.ref.at[index], self.target.at[index], semaphore)
        part.start()
        return part

    def leave(self, source=None):
        source = self.ref if source is None else source
        self.copy = pltpu.make_async_copy(source, self.target, self.semaphore)
        self.copy.start()


def call(kernel, outs, places, out_places, scratch=(), unstaged=(), megabytes=58, aliases=None):
    staged_in = [i for i, p in enumerate(places) if p in "hw"]
    staged_out = [i for i, p in enumerate(out_places) if p in "hw"]
    spaces = {"s": pltpu.SMEM, "v": pltpu.VMEM, "h": pl.ANY, "w": pl.ANY}

    def run(*args):
        stages = [pltpu.VMEM(args[i].shape, args[i].dtype) for i in staged_in]
        stages += [pltpu.VMEM((16, 128) if i in unstaged else outs[i].shape, outs[i].dtype) for i in staged_out]
        sems = [pltpu.SemaphoreType.DMA((max(len(v), 1),)) for v in (staged_in, staged_out)]

        def body(*refs):
            ins, rest = list(refs[: len(args)]), list(refs[len(args) :])
            results, rest = rest[: len(outs)], rest[len(outs) :]
            own, rest = rest[: len(scratch)], rest[len(scratch) :]
            sem_in, sem_out = rest[-2:]
            for k, i in enumerate(staged_in):
                copy = pltpu.make_async_copy(ins[i], rest[k], sem_in.at[k])
                ins[i] = Arriving(copy, rest[k])
                if places[i] == "h":
                    ins[i].begin()
            for k, i in enumerate(staged_out):
                results[i] = Leaving(rest[len(staged_in) + k], results[i], sem_out.at[k])
            kernel(*ins, *results, *own)
            for i in staged_in:
                ins[i].ready()
            for i in staged_out:
                if results[i].copy is None and out_places[i] == "h":
                    results[i].leave()
            for i in staged_out:
                if results[i].copy is not None:
                    results[i].copy.wait()

        return pl.pallas_call(
            body,
            out_shape=outs,
            in_specs=[pl.BlockSpec(memory_space=spaces[p]) for p in places],
            out_specs=[pl.BlockSpec(memory_space=spaces[p]) for p in out_places],
            scratch_shapes=list(scratch) + stages + sems,
            input_output_aliases=aliases or {},
            cost_estimate=pl.CostEstimate(flops=10**9, bytes_accessed=10**7, transcendentals=10**6),
            compiler_params=pltpu.CompilerParams(vmem_limit_bytes=megabytes * 1024 * 1024),
        )(*args)

    return run


def local(
    clips, clip_counts, histories, lengths, user_cotangent,
    expand_first, spatial_first, temporal_first, project_first,
    expand_second, spatial_second, temporal_second, project_second,
    item_project, tower_up, tower_down,
):
    same_core = [[i for i in range(DEVICES) if i % 2 == c] for c in range(2)]
    core = (lax.axis_index("seq") % 2).reshape(1)

    def across_chips(v):
        return lax.all_to_all(v, AXES, 0, 0, axis_index_groups=same_core, tiled=True)

    def swap(v):
        return lax.ppermute(v, "seq", [(i, i ^ 1) for i in range(8)])

    x = clips.reshape(ITEMS_HERE, FRAMES * CELLS, C).transpose(1, 0, 2)
    counts = clip_counts.reshape(1, ITEMS_HERE)
    weights = (
        spatial_first, temporal_first, project_first.T,
        expand_second, spatial_second, temporal_second, project_second.T,
    )
    n = ITEMS_HERE
    framed = [pltpu.VMEM((FRAMES + 2, 4, n, E), F32), pltpu.VMEM((FRAMES + 2, n, E), F32)]
    (block,) = call(conv_forward, [shape((CHIPS, 64, 128))], "svvvvvvvvvvv", "v", framed, megabytes=24)(
        lengths, x, counts, user_cotangent, expand_first, *weights
    )
    kept = call(
        conv_forward,
        [shape((56, E), F32), shape((576, E)), shape((2 * 64, n, E)), shape((INNER, n, E)), shape((512, C))],
        "shvvhvvhhvvh",
        "h" * 5,
        framed,
    )(lengths, x, counts, user_cotangent, expand_first, *weights)
    own = across_chips(block)
    own, (taps, kept_weights, outer, inner, o1) = lax.optimization_barrier((own, kept))
    other = swap(own)
    sent, picked = call(tower, [shape((DEVICES, 8, 128)), shape((ROWS, 256))], "sshhvvhhh", "hh")(
        core, lengths, own, other, histories, user_cotangent, item_project, tower_up, tower_down
    )
    back = lax.all_to_all(sent, AXES, 0, 0, tiled=True)
    up_keep, up_send, factors, user_vec = call(
        tower_sums,
        [shape((1024, 128)), shape((1024, 128)), shape((48, 128)), shape((USERS_HERE, D), F32)],
        "sshvhhh",
        "hhhv",
        [pltpu.VMEM((2, 1024, 128), BF)],
        unstaged=(0, 1),
    )(core, lengths, picked, user_cotangent, item_project, tower_up, tower_down)
    back, up_send = lax.optimization_barrier((back, up_send))
    up_other = swap(up_send)
    conv_keep, conv_send = call(
        conv_backward,
        [shape((1536, 128)), shape((1536, 128))],
        "sv" + "h" * 6,
        "vv",
        [
            pltpu.VMEM((4, 4, n, E), BF),
            pltpu.VMEM((768, 512), F32),
            pltpu.VMEM((32, 8, E), F32),
            pltpu.VMEM((2, 1536, 128), BF),
        ],
        megabytes=50,
    )(core, back, inner, taps, kept_weights, o1, x, outer)
    (third,) = call(merge, [shape((CHIPS, 80, 128))], "vvvvv", "v", megabytes=16)(
        conv_keep, swap(conv_send), up_keep, up_other, factors
    )
    third = across_chips(third)
    fourth, factors = call(
        sum_chips, [shape((CHIPS, 40, 128)), shape((CHIPS, 40, 128))], "v", "vh", megabytes=16
    )(third)
    fourth = across_chips(fourth)
    grad_down, item_base = call(finish_low_rank, [shape((FH, D), F32), shape((C, D), F32)], "hhhh", "hh")(
        own, other, factors, swap(factors)
    )
    fourth, item_base = lax.optimization_barrier((fourth, item_base))
    *conv_grads, grad_item, grad_up = call(
        finish,
        [shape((C, E), F32), shape((9, E), F32), shape((3, E), F32), shape((C, E), F32)] * 2
        + [shape((C, D), F32), shape((D, FH), F32)],
        "svvhhh",
        "hvvhhvvhhw",
        [pltpu.VMEM((2, CHIPS, 40, 128), BF), pltpu.SemaphoreType.DMA((4,))],
        megabytes=32,
        aliases={3: 8},
    )(core, fourth, swap(fourth), item_base, item_project, tower_up)
    conv_grads[3] = conv_grads[3].T
    conv_grads[7] = conv_grads[7].T
    return (user_vec, *conv_grads, grad_item, grad_up, grad_down)


def solution(mesh):
    spread = P(AXES)
    return jax.shard_map(
        local,
        mesh=mesh,
        in_specs=(spread,) * 5 + (P(),) * 11,
        out_specs=(spread,) + (P(),) * 11,
        check_vma=False,
    )
```

```python
import jax
import jax.numpy as jnp
from jax import lax
from jax.experimental import pallas as pl
from jax.experimental.pallas import tpu as pltpu
from jax.sharding import PartitionSpec as P

BF = jnp.bfloat16
F32 = jnp.float32
AXES = ("bulk", "seq")
C, E, D, FH = 192, 432, 512, 1024
FRAMES, SIDE, ITEMS_HERE, USERS_HERE, LENGTH = 4, 4, 32, 4, 64
DEVICES, CHIPS, CAPACITY = 128, 64, 4
ROWS = USERS_HERE * LENGTH
CELLS = SIDE * SIDE
HALF = 2
LINKS_FIRST = [
    (HALF * p + q, SIDE * (2 * p + a - 1) + 2 * q + b - 1, 3 * a + b)
    for p in range(HALF)
    for q in range(HALF)
    for a in range(3)
    for b in range(3)
    if 0 <= 2 * p + a - 1 < SIDE and 0 <= 2 * q + b - 1 < SIDE
]
LINKS_SECOND = [(0, 4), (1, 5), (2, 7), (3, 8)]


AT_N2, AT_H2, AT_SP2, AT_G2, AT_D2, AT_N1, AT_H1, AT_SP1, INNER = 0, 4, 8, 12, 28, 44, 60, 76, 92


def dot_nn(a, b):
    return lax.dot_general(a, b, (((1,), (0,)), ((), ())), preferred_element_type=F32)


def dot_nt(a, b):
    return lax.dot_general(a, b, (((1,), (1,)), ((), ())), preferred_element_type=F32)


def dot_tn(a, b):
    return lax.dot_general(a, b, (((0,), (0,)), ((), ())), preferred_element_type=F32)


def silu_and_slope(v):
    gate = 0.5 * jnp.tanh(0.5 * v) + 0.5
    value = v * gate
    return value, gate + value - value * gate


def column_of(row):
    n = row.shape[1]
    same = lax.broadcasted_iota(jnp.int32, (n, n), 0) == lax.broadcasted_iota(jnp.int32, (n, n), 1)
    return jnp.sum(jnp.where(same, row.astype(F32), 0.0), axis=1, keepdims=True).astype(jnp.int32)


def per_user(lengths):
    user = lax.broadcasted_iota(jnp.int32, (8, 1), 0)
    length = jnp.ones((8, 1), jnp.int32)
    for u in range(USERS_HERE):
        length = jnp.where(user == u, lengths[u], length)
    return user, length


def prepare_tower(lengths, cot, project, up, down, mixer, rows):
    mixer[...] = dot_nn(project[...], up[...]).astype(BF)
    _, length = per_user(lengths)
    shared = cot[...] / length[0:4].astype(F32)
    shared = jnp.concatenate([shared, shared], axis=0)
    coarse = shared.astype(BF)
    fine = (shared - coarse.astype(F32)).astype(BF)
    rows[:, 0:FH] = dot_nt(coarse, down[...])
    for at, part in ((FH, project[0:128]), (FH + 128, project[64:192])):
        rows[:, at : at + 128] = dot_nt(coarse, part) + dot_nt(fine, part)


def conv_forward(
    lengths, x, counts_row, cot, e1, s1, t1, p1, e2, s2, t2, p2, *rest,
):
    *kept, framed1, framed2 = rest
    block = None
    if len(kept) == 1:
        (block,) = kept
    else:
        project, up, down, mixer, per_user_rows, *kept = kept
        prepare_tower(lengths, cot, project, up, down, mixer, per_user_rows)
        taps, weights, outer, inner, o1 = kept
    counts = column_of(counts_row[...])
    zero4 = jnp.zeros((HALF * HALF, ITEMS_HERE, E), F32)
    framed1[0] = zero4
    framed1[FRAMES + 1] = zero4
    zero1 = jnp.zeros((ITEMS_HERE, E), F32)
    framed2[0] = zero1
    framed2[FRAMES + 1] = zero1
    taps1 = s1[...].astype(F32)
    taps2 = s2[...].astype(F32)
    frame1 = t1[...].astype(F32)
    frame2 = t2[...].astype(F32)
    if block is None:
        taps[...] = jnp.zeros((56, E), F32)
        for at, ref in ((0, s1), (9, t1), (12, s2), (21, t2)):
            taps[at : at + ref.shape[0]] = ref[...].astype(F32)
        taps[24:56, 0:128] = jnp.broadcast_to(counts.astype(F32), (ITEMS_HERE, 128))

    if block is None:
        x.ready(), e1.ready()

    def grow(f, _):
        live = f < counts
        x_f = x[pl.ds(f * CELLS, CELLS)]
        x_f = jnp.where(live[None], x_f, jnp.zeros_like(x_f))
        pre = dot_nn(x_f.reshape(CELLS * ITEMS_HERE, C), e1[...])
        value, slope = silu_and_slope(pre)
        value = value.astype(BF).reshape(CELLS, ITEMS_HERE, E)
        if block is None:
            outer[pl.ds(f * CELLS, CELLS)] = value
            outer[pl.ds((FRAMES + f) * CELLS, CELLS)] = slope.astype(BF).reshape(CELLS, ITEMS_HERE, E)
        outs = [jnp.zeros((ITEMS_HERE, E), F32)] * 4
        for out_cell, in_cell, tap in LINKS_FIRST:
            outs[out_cell] = outs[out_cell] + value[in_cell].astype(F32) * taps1[tap]
        for out_cell in range(4):
            framed1[f + 1, out_cell] = outs[out_cell]
            if block is None:
                inner[AT_SP1 + f * 4 + out_cell] = outs[out_cell].astype(BF)
        return 0

    lax.fori_loop(0, FRAMES, grow, 0, unroll=True)
    narrow = []
    for f in range(FRAMES):
        summed = framed1[f] * frame1[0] + framed1[f + 1] * frame1[1] + framed1[f + 2] * frame1[2]
        value, slope = silu_and_slope(summed)
        narrow.append(value.astype(BF))
        if block is None:
            inner[AT_H1 + f * 4 : AT_H1 + f * 4 + 4] = slope.astype(BF)
    narrow = jnp.concatenate(narrow, axis=0)
    first = dot_nt(narrow.reshape(FRAMES * 4 * ITEMS_HERE, E), p1[...]).astype(BF)
    value, slope = silu_and_slope(dot_nn(first, e2[...]))
    value = value.astype(BF).reshape(FRAMES * 4, ITEMS_HERE, E)
    if block is None:
        inner[AT_N1 : AT_N1 + 16] = narrow
        o1[...] = first
        inner[AT_G2 : AT_G2 + 16] = value
        inner[AT_D2 : AT_D2 + 16] = slope.astype(BF).reshape(FRAMES * 4, ITEMS_HERE, E)
        weights[0:192] = p2[...]
        weights[192:384] = e2[...]
        weights[384:576] = p1[...]
    for f in range(FRAMES):
        total = jnp.zeros((ITEMS_HERE, E), F32)
        for cell, tap in LINKS_SECOND:
            total = total + value[f * 4 + cell].astype(F32) * taps2[tap]
        framed2[f + 1] = total
        if block is None:
            inner[AT_SP2 + f] = total.astype(BF)
    narrow = []
    for f in range(FRAMES):
        summed = framed2[f] * frame2[0] + framed2[f + 1] * frame2[1] + framed2[f + 2] * frame2[2]
        value, slope = silu_and_slope(summed)
        narrow.append(value.astype(BF))
        if block is None:
            inner[AT_N2 + f] = value.astype(BF)
            inner[AT_H2 + f] = slope.astype(BF)
    if block is None:
        return
    second = dot_nt(jnp.concatenate(narrow, axis=0), p2[...]).astype(BF)
    pooled = jnp.zeros((ITEMS_HERE, C), F32)
    for f in range(FRAMES):
        live = (f < counts).astype(F32)
        pooled = pooled + live * second[f * ITEMS_HERE : (f + 1) * ITEMS_HERE].astype(F32)
    pooled = pooled / counts.astype(F32)
    _, length = per_user(lengths)
    shared = cot[...] / length[0:4].astype(F32)
    pieces = []
    for k in range(8):
        piece = shared[:, (k // 2) * 128 : (k // 2 + 1) * 128]
        pieces.append(piece if k % 2 else pltpu.roll(piece, 64, 1))
    lane = lax.broadcasted_iota(jnp.int32, (ITEMS_HERE, 128), 1)
    shared = jnp.concatenate(pieces, axis=0)
    high = jnp.concatenate([pooled[:, 128:192], pooled[:, 0:64]], axis=1)
    rows = jnp.concatenate([pooled[:, 0:128], jnp.where(lane < 64, high, shared)], axis=0).astype(BF)
    block[...] = jnp.broadcast_to(rows[None], (CHIPS, 64, 128))


def gelu_and_slope(v):
    scale = 0.7978845608028654
    square = v * v
    bent = jnp.tanh(scale * v * (1.0 + 0.044715 * square))
    gate = 0.5 * (1.0 + bent)
    return v * gate, gate + 0.5 * v * (1.0 - bent * bent) * (scale * (1.0 + 3 * 0.044715 * square))


def for_live_rows(lengths, per_row):
    position = lax.broadcasted_iota(jnp.int32, (LENGTH, 1), 0)
    return jnp.concatenate([(position < lengths[u]).astype(F32) * per_row(u) for u in range(USERS_HERE)], axis=0)


def tower(
    core, lengths, own, other, ids_ref, mixer, rows,
    sent, picked_out,
):
    ids = jnp.concatenate([column_of(ids_ref[u : u + 1]) for u in range(USERS_HERE)], axis=0)
    owner = ids // ITEMS_HERE
    within = ids - owner * ITEMS_HERE
    chip = owner // 2
    place = chip * ITEMS_HERE + within
    mine = (owner - chip * 2) == core[0]
    lanes = lax.broadcasted_iota(jnp.int32, (ROWS, CHIPS * ITEMS_HERE), 1)
    pick_own = (lanes == jnp.where(mine, place, -1)).astype(F32).astype(BF)
    pick_other = (lanes == jnp.where(mine, -1, place)).astype(F32).astype(BF)

    def rows_of(ref):
        low = ref[:, 0:32, :].reshape(CHIPS * ITEMS_HERE, 128)
        high = ref[:, 32:64, :].reshape(CHIPS * ITEMS_HERE, 128)
        return jnp.concatenate([low, high], axis=1)

    across = lax.broadcasted_iota(jnp.int32, (ROWS, ROWS), 1)
    down_rows = lax.broadcasted_iota(jnp.int32, (ROWS, ROWS), 0)
    owner_row = jnp.sum(jnp.where(across == down_rows, owner.astype(F32), 0.0), axis=0, keepdims=True).astype(jnp.int32)
    earlier = down_rows < across
    rank = jnp.sum(((owner == owner_row) & earlier).astype(F32), axis=0, keepdims=True).astype(jnp.int32)
    slot = owner_row * 8 + rank
    sent_at = lax.broadcasted_iota(jnp.int32, (DEVICES * 8, ROWS), 0)
    put_low = (sent_at == slot).astype(F32).astype(BF)
    put_high = (sent_at == slot + CAPACITY).astype(F32).astype(BF)
    own, other = own.ready(), other.ready()
    picked = (dot_nn(pick_own, rows_of(own)) + dot_nn(pick_other, rows_of(other))).astype(BF)
    picked_out[...] = picked
    picked_out.leave()
    _, slope = gelu_and_slope(dot_nn(picked[:, 0:C], mixer[...]))
    pre_grad = for_live_rows(lengths, lambda u: rows[u : u + 1, 0:FH] * slope[u * LENGTH : (u + 1) * LENGTH]).astype(BF)
    low = dot_nt(pre_grad, mixer[0:128]) + for_live_rows(lengths, lambda u: rows[u : u + 1, FH : FH + 128])
    high = dot_nt(pre_grad, mixer[64:192]) + for_live_rows(lengths, lambda u: rows[u : u + 1, FH + 128 : FH + 256])
    lane = lax.broadcasted_iota(jnp.int32, (ROWS, 128), 1)
    tag = within.astype(F32)
    low = jnp.where(lane < 96, low, jnp.where(lane == 96, tag, 0.0)).astype(BF)
    high = jnp.where(lane >= 32, high, jnp.where(lane == 0, tag, 0.0)).astype(BF)

    back = (dot_nn(put_low, low) + dot_nn(put_high, high)).astype(BF)
    sent[...] = back.reshape(DEVICES, 8, 128)


def tower_sums(
    core, lengths, picked, rows, project, up, down,
    up_keep, up_send, factors, user_vec,
    halves,
):
    picked = picked[...]
    fetched = dot_nn(picked[:, 0:C], project[...]).astype(BF)
    act, slope = gelu_and_slope(dot_nn(fetched, up[...]))
    act = act.astype(BF)
    pre_grad = for_live_rows(lengths, lambda u: rows[u : u + 1, 0:FH] * slope[u * LENGTH : (u + 1) * LENGTH]).astype(BF)
    user, length = per_user(lengths)
    at = lax.broadcasted_iota(jnp.int32, (8, ROWS), 1)
    live = ((at // LENGTH == user) & (at - user * LENGTH < length)).astype(F32).astype(BF)
    act_sum = dot_nn(live, act)
    picked_sum = dot_nn(live, picked)
    pieces = [act_sum[0:4, j * 128 : (j + 1) * 128] for j in range(8)]
    pieces += [picked_sum[0:4, j * 128 : (j + 1) * 128] for j in range(2)]
    factors[...] = jnp.concatenate(pieces + [jnp.zeros((8, 128), F32)], axis=0).astype(BF)
    coarse = act_sum.astype(BF)
    fine = (act_sum - coarse.astype(F32)).astype(BF)
    mixed = dot_nn(live, fetched) + dot_nn(coarse, down[...]) + dot_nn(fine, down[...])
    user_vec[...] = (mixed / length.astype(F32))[0:4]
    up_grad = dot_tn(picked, pre_grad).astype(BF)
    for j in range(FH // 128):
        halves[j // 4, (j % 4) * 256 : (j % 4 + 1) * 256] = up_grad[:, j * 128 : (j + 1) * 128]
    up_keep.leave(halves.at[core[0]])
    up_send.leave(halves.at[1 - core[0]])


def conv_backward(
    core, back, inner, taps, weights, o1, x, outer,
    keep, send,
    spatial_grad, wide, small, halves,
):
    taps1, frame1, taps2, frame2 = taps[0:9], taps[9:12], taps[12:21], taps[21:24]
    counts = taps[24:56, 0:1]

    def tile_sum(v):
        return jnp.sum(v.reshape(-1, 8, E), axis=0)

    small[...] = jnp.zeros(small.shape, F32)
    wide[...] = jnp.zeros(wide.shape, F32)
    got = back[...].reshape(DEVICES * 8, 128)
    row = lax.broadcasted_iota(jnp.int32, (DEVICES * 8, 1), 0)
    is_low = (row & 7) < CAPACITY
    got_f = got.astype(F32)
    tag = jnp.where(is_low, got_f[:, 96:97], got_f[:, 0:1]).astype(jnp.int32)
    named = tag == lax.broadcasted_iota(jnp.int32, (DEVICES * 8, ITEMS_HERE), 1)
    low = dot_tn((named & is_low).astype(F32).astype(BF), got)
    high = dot_tn((named & ~is_low).astype(F32).astype(BF), got)
    pooled_grad = jnp.concatenate([low[:, 0:96], high[:, 32:128]], axis=1)
    shared = pooled_grad / counts
    out_grad = jnp.concatenate(
        [(shared * (counts > f).astype(F32)).astype(BF) for f in range(FRAMES)], axis=0
    )
    inner.ready(), weights.ready(), o1.ready()
    p2, e2, p1 = weights[0:192], weights[192:384], weights[384:576]
    wide[576:768, 0:E] = dot_tn(out_grad, inner[AT_N2 : AT_N2 + 4].reshape(FRAMES * ITEMS_HERE, E))
    summed_grad = dot_nn(out_grad, p2).reshape(FRAMES, ITEMS_HERE, E) * inner[AT_H2 : AT_H2 + 4].astype(F32)
    spread = []
    for f in range(FRAMES):
        total = summed_grad[f] * frame2[1]
        if f + 1 < FRAMES:
            total = total + summed_grad[f + 1] * frame2[0]
        if f > 0:
            total = total + summed_grad[f - 1] * frame2[2]
        spread.append(total)
    for k in range(3):
        total = jnp.zeros((8, E), F32)
        for f in range(FRAMES):
            if 0 <= f + k - 1 < FRAMES:
                total = total + tile_sum(inner[AT_SP2 + f + k - 1].astype(F32) * summed_grad[f])
        small[21 + k] = total
    parts = []
    for f in range(FRAMES):
        for cell, tap in LINKS_SECOND:
            small[12 + tap] += tile_sum(inner[AT_G2 + f * 4 + cell].astype(F32) * spread[f])
            parts.append((spread[f] * taps2[tap] * inner[AT_D2 + f * 4 + cell].astype(F32)).astype(BF))
    grown_grad = jnp.concatenate(parts, axis=0)
    wide[384:576, 0:E] = dot_tn(o1[...], grown_grad)
    first_grad = dot_nt(grown_grad, e2).astype(BF)
    wide[192:384, 0:E] = dot_tn(first_grad, inner[AT_N1 : AT_N1 + 16].reshape(FRAMES * 4 * ITEMS_HERE, E))
    narrow_grad = dot_nn(first_grad, p1).reshape(FRAMES, 4, ITEMS_HERE, E)
    summed_grad = [narrow_grad[f] * inner[AT_H1 + f * 4 : AT_H1 + f * 4 + 4].astype(F32) for f in range(FRAMES)]
    for k in range(3):
        total = jnp.zeros((8, E), F32)
        for f in range(FRAMES):
            if 0 <= f + k - 1 < FRAMES:
                total = total + tile_sum(inner[AT_SP1 + f * 4 + 4 * k - 4 : AT_SP1 + f * 4 + 4 * k].astype(F32) * summed_grad[f])
        small[9 + k] = total
    for f in range(FRAMES):
        total = summed_grad[f] * frame1[1]
        if f + 1 < FRAMES:
            total = total + summed_grad[f + 1] * frame1[0]
        if f > 0:
            total = total + summed_grad[f - 1] * frame1[2]
        spatial_grad[f] = total.astype(BF)

    x.ready(), outer.ready()
    half_taps = taps1.astype(BF)

    def grow_back(f, _):
        live = counts > lax.convert_element_type(f, F32)
        x_f = x[pl.ds(f * CELLS, CELLS)]
        x_f = jnp.where(live[None], x_f, jnp.zeros_like(x_f)).reshape(CELLS * ITEMS_HERE, C)
        outs = [spatial_grad[f, cell] for cell in range(4)]
        sums = [None] * 9
        grads = [None] * CELLS
        for out_cell, in_cell, tap in LINKS_FIRST:
            term = outs[out_cell] * half_taps[tap]
            grads[in_cell] = term if grads[in_cell] is None else grads[in_cell] + term
            term = outer[f * CELLS + in_cell] * outs[out_cell]
            sums[tap] = term if sums[tap] is None else sums[tap] + term
        for tap in range(9):
            small[tap] += tile_sum(sums[tap].astype(F32))
        grads = [grads[cell] * outer[(FRAMES + f) * CELLS + cell] for cell in range(CELLS)]
        wide[0:192, 0:E] += dot_tn(x_f, jnp.concatenate(grads, axis=0))
        return 0

    lax.fori_loop(0, FRAMES, grow_back, 0, unroll=True)
    sums = jnp.sum(small[...], axis=1).astype(BF)
    put = lax.broadcasted_iota(jnp.int32, (32, 128), 1) == lax.broadcasted_iota(jnp.int32, (32, 128), 0) + 64
    wide[0:E, 384:512] += dot_tn(sums, put.astype(F32).astype(BF))
    for j in range(4):
        halves[j // 2, (j % 2) * 768 : (j % 2 + 1) * 768] = wide[:, j * 128 : (j + 1) * 128].astype(BF)
    keep[...] = halves[core[0]]
    send[...] = halves[1 - core[0]]


def merge(conv_a, conv_b, up_a, up_b, factors, out):
    conv = (conv_a[...].astype(F32) + conv_b[...].astype(F32)).astype(BF)
    up = (up_a[...].astype(F32) + up_b[...].astype(F32)).astype(BF)
    out[:, 0:24, :] = conv.reshape(CHIPS, 24, 128)
    out[:, 24:40, :] = up.reshape(CHIPS, 16, 128)
    out[:, 40:80, :] = jnp.broadcast_to(factors[0:40][None], (CHIPS, 40, 128))


def sum_chips(third, out, factors):
    factors[...] = third[:, 40:80, :]
    factors.leave()
    total = jnp.sum(third[:, 0:40, :].astype(F32), axis=0).astype(BF)
    out[...] = jnp.broadcast_to(total[None], (CHIPS, 40, 128))


def finish_low_rank(own, other, factors, factors_other, grad_down, item_base):
    row = lax.broadcasted_iota(jnp.int32, (CHIPS * 8, 128), 0) & 7
    lane = lax.broadcasted_iota(jnp.int32, (CHIPS * 8, 128), 1)
    even = []
    for src in (own, other):
        parts = []
        for k in range(4):
            got = src[:, 32 + 8 * k : 40 + 8 * k, :].reshape(CHIPS * 8, 128).astype(F32)
            left = pltpu.roll(got, 64, 1)
            right = pltpu.roll(got, CHIPS * 8 - 4, 0)
            parts.append(jnp.where(row < 4, jnp.where(lane < 64, left, right), 0.0))
        even.append(jnp.concatenate(parts, axis=1))
    odd = jnp.concatenate([pltpu.roll(v, 4, 0) for v in even], axis=0).astype(BF)
    even = jnp.concatenate(even, axis=0).astype(BF)
    for j in range(5):
        cut = slice(8 * j, 8 * j + 8)
        left = jnp.concatenate(
            [src[:, cut, :].reshape(CHIPS * 8, 128) for src in (factors, factors_other)], axis=0
        )
        first, second = dot_tn(left, even), dot_tn(left, odd)
        if j < 4:
            grad_down[j * 256 : j * 256 + 128] = first
            grad_down[j * 256 + 128 : j * 256 + 256] = second
        else:
            item_base[0:128] = first
            item_base[128:C] = second[0:64]


def finish(
    core, mine, theirs, item_base, project, up,
    ge1, gs1, gt1, gp1, ge2, gs2, gt2, gp2, grad_item, grad_up,
    halves, part_sems,
):
    halves[core[0]] = mine[...]
    halves[1 - core[0]] = theirs[...]
    for j in range(4):
        width = min(128, E - j * 128)
        part = halves[j // 2, :, 0:24, :].reshape(1536, 128)[(j % 2) * 768 : (j % 2 + 1) * 768].astype(F32)
        cut = slice(j * 128, j * 128 + width)
        for i, out in enumerate((ge1, gp1, ge2, gp2)):
            out[:, cut] = part[i * 192 : (i + 1) * 192, 0:width]
    same = lax.broadcasted_iota(jnp.int32, (E, E), 0) == lax.broadcasted_iota(jnp.int32, (E, E), 1)
    for out in (ge1, gp1, ge2, gp2):
        out.leave()
    small = dot_tn(part[0:E].astype(BF), same.astype(F32).astype(BF))
    gs1[...] = small[64:73]
    gt1[...] = small[73:76]
    gs2[...] = small[76:85]
    gt2[...] = small[85:88]
    item = item_base[...]
    parts = []
    for j in range(FH // 128):
        part = halves[j // 4, :, 24:40, :].reshape(1024, 128)[(j % 4) * 256 : (j % 4) * 256 + C]
        cut = slice(j * 128, (j + 1) * 128)
        grad_up[:, cut] = dot_tn(project[...], part)
        item = item + dot_nt(part, up[:, cut])
        if j % 2:
            parts.append(grad_up.leave_part((slice(None), pl.ds((j - 1) * 128, 256)), part_sems.at[j // 2]))
    grad_item[...] = item
    grad_item.leave()
    for part in parts:
        part.wait()


def shape(dims, dtype=BF):
    return jax.ShapeDtypeStruct(dims, dtype)


class Arriving:
    def __init__(self, copy, ref):
        self.copy, self.ref, self.begun = copy, ref, False

    def begin(self):
        if not self.begun:
            self.copy.start()
            self.begun = True

    def ready(self):
        if self.copy is not None:
            self.begin()
            self.copy.wait()
            self.copy = None
        return self.ref

    def __getitem__(self, index):
        return self.ready()[index]


class Leaving:
    def __init__(self, ref, target, semaphore):
        self.ref, self.target, self.semaphore, self.copy = ref, target, semaphore, None

    def __setitem__(self, index, value):
        self.ref[index] = value

    def leave_part(self, index, semaphore):
        part = pltpu.make_async_copy(self.ref.at[index], self.target.at[index], semaphore)
        part.start()
        return part

    def leave(self, source=None):
        source = self.ref if source is None else source
        self.copy = pltpu.make_async_copy(source, self.target, self.semaphore)
        self.copy.start()


def call(kernel, outs, places, out_places, scratch=(), unstaged=(), megabytes=58, aliases=None):
    staged_in = [i for i, p in enumerate(places) if p in "hw"]
    staged_out = [i for i, p in enumerate(out_places) if p in "hw"]
    spaces = {"s": pltpu.SMEM, "v": pltpu.VMEM, "h": pl.ANY, "w": pl.ANY}

    def run(*args):
        stages = [pltpu.VMEM(args[i].shape, args[i].dtype) for i in staged_in]
        stages += [pltpu.VMEM((16, 128) if i in unstaged else outs[i].shape, outs[i].dtype) for i in staged_out]
        sems = [pltpu.SemaphoreType.DMA((max(len(v), 1),)) for v in (staged_in, staged_out)]

        def body(*refs):
            ins, rest = list(refs[: len(args)]), list(refs[len(args) :])
            results, rest = rest[: len(outs)], rest[len(outs) :]
            own, rest = rest[: len(scratch)], rest[len(scratch) :]
            sem_in, sem_out = rest[-2:]
            for k, i in enumerate(staged_in):
                copy = pltpu.make_async_copy(ins[i], rest[k], sem_in.at[k])
                ins[i] = Arriving(copy, rest[k])
                if places[i] == "h":
                    ins[i].begin()
            for k, i in enumerate(staged_out):
                results[i] = Leaving(rest[len(staged_in) + k], results[i], sem_out.at[k])
            kernel(*ins, *results, *own)
            for i in staged_in:
                ins[i].ready()
            for i in staged_out:
                if results[i].copy is None and out_places[i] == "h":
                    results[i].leave()
            for i in staged_out:
                if results[i].copy is not None:
                    results[i].copy.wait()

        return pl.pallas_call(
            body,
            out_shape=outs,
            in_specs=[pl.BlockSpec(memory_space=spaces[p]) for p in places],
            out_specs=[pl.BlockSpec(memory_space=spaces[p]) for p in out_places],
            scratch_shapes=list(scratch) + stages + sems,
            input_output_aliases=aliases or {},
            cost_estimate=pl.CostEstimate(flops=10**9, bytes_accessed=10**7, transcendentals=10**6),
            compiler_params=pltpu.CompilerParams(vmem_limit_bytes=megabytes * 1024 * 1024),
        )(*args)

    return run


def local(
    clips, clip_counts, histories, lengths, user_cotangent,
    expand_first, spatial_first, temporal_first, project_first,
    expand_second, spatial_second, temporal_second, project_second,
    item_project, tower_up, tower_down,
):
    same_core = [[i for i in range(DEVICES) if i % 2 == c] for c in range(2)]
    core = (lax.axis_index("seq") % 2).reshape(1)

    def across_chips(v):
        return lax.all_to_all(v, AXES, 0, 0, axis_index_groups=same_core, tiled=True)

    def swap(v):
        return lax.ppermute(v, "seq", [(i, i ^ 1) for i in range(8)])

    x = clips.reshape(ITEMS_HERE, FRAMES * CELLS, C).transpose(1, 0, 2)
    counts = clip_counts.reshape(1, ITEMS_HERE)
    weights = (
        spatial_first, temporal_first, project_first.T,
        expand_second, spatial_second, temporal_second, project_second.T,
    )
    n = ITEMS_HERE
    framed = [pltpu.VMEM((FRAMES + 2, 4, n, E), F32), pltpu.VMEM((FRAMES + 2, n, E), F32)]
    (block,) = call(conv_forward, [shape((CHIPS, 64, 128))], "svvvvvvvvvvv", "v", framed, megabytes=24)(
        lengths, x, counts, user_cotangent, expand_first, *weights
    )
    kept = call(
        conv_forward,
        [
            shape((C, FH)), shape((8, FH + 256), F32),
            shape((56, E), F32), shape((576, E)), shape((2 * 64, n, E)), shape((INNER, n, E)), shape((512, C)),
        ],
        "shvvhvvhhvvhhhh",
        "h" * 7,
        framed,
    )(lengths, x, counts, user_cotangent, expand_first, *weights, item_project, tower_up, tower_down)
    own = across_chips(block)
    own, (mixer, user_rows, taps, kept_weights, outer, inner, o1) = lax.optimization_barrier((own, kept))
    other = swap(own)
    sent, picked = call(tower, [shape((DEVICES, 8, 128)), shape((ROWS, 256))], "sshhvhh", "hh")(
        core, lengths, own, other, histories, mixer, user_rows
    )
    back = lax.all_to_all(sent, AXES, 0, 0, tiled=True)
    up_keep, up_send, factors, user_vec = call(
        tower_sums,
        [shape((1024, 128)), shape((1024, 128)), shape((48, 128)), shape((USERS_HERE, D), F32)],
        "sshhhhh",
        "hhhv",
        [pltpu.VMEM((2, 1024, 128), BF)],
        unstaged=(0, 1),
    )(core, lengths, picked, user_rows, item_project, tower_up, tower_down)
    back, up_send = lax.optimization_barrier((back, up_send))
    up_other = swap(up_send)
    conv_keep, conv_send = call(
        conv_backward,
        [shape((1536, 128)), shape((1536, 128))],
        "sv" + "h" * 6,
        "vv",
        [
            pltpu.VMEM((4, 4, n, E), BF),
            pltpu.VMEM((768, 512), F32),
            pltpu.VMEM((32, 8, E), F32),
            pltpu.VMEM((2, 1536, 128), BF),
        ],
        megabytes=50,
    )(core, back, inner, taps, kept_weights, o1, x, outer)
    (third,) = call(merge, [shape((CHIPS, 80, 128))], "vvvvv", "v", megabytes=16)(
        conv_keep, swap(conv_send), up_keep, up_other, factors
    )
    third = across_chips(third)
    fourth, factors = call(
        sum_chips, [shape((CHIPS, 40, 128)), shape((CHIPS, 40, 128))], "v", "vh", megabytes=16
    )(third)
    fourth = across_chips(fourth)
    grad_down, item_base = call(finish_low_rank, [shape((FH, D), F32), shape((C, D), F32)], "hhhh", "hh")(
        own, other, factors, swap(factors)
    )
    fourth, item_base = lax.optimization_barrier((fourth, item_base))
    *conv_grads, grad_item, grad_up = call(
        finish,
        [shape((C, E), F32), shape((9, E), F32), shape((3, E), F32), shape((C, E), F32)] * 2
        + [shape((C, D), F32), shape((D, FH), F32)],
        "svvhhh",
        "hvvhhvvhhw",
        [pltpu.VMEM((2, CHIPS, 40, 128), BF), pltpu.SemaphoreType.DMA((4,))],
        megabytes=32,
        aliases={3: 8},
    )(core, fourth, swap(fourth), item_base, item_project, tower_up)
    conv_grads[3] = conv_grads[3].T
    conv_grads[7] = conv_grads[7].T
    return (user_vec, *conv_grads, grad_item, grad_up, grad_down)


def solution(mesh):
    spread = P(AXES)
    return jax.shard_map(
        local,
        mesh=mesh,
        in_specs=(spread,) * 5 + (P(),) * 11,
        out_specs=(spread,) + (P(),) * 11,
        check_vma=False,
    )
```

```python
import jax
import jax.numpy as jnp
from jax import lax
from jax.experimental import pallas as pl
from jax.experimental.pallas import tpu as pltpu
from jax.sharding import PartitionSpec as P

BF = jnp.bfloat16
F32 = jnp.float32
AXES = ("bulk", "seq")
C, E, D, FH = 192, 432, 512, 1024
FRAMES, SIDE, ITEMS_HERE, USERS_HERE, LENGTH = 4, 4, 32, 4, 64
DEVICES, CHIPS, CAPACITY = 128, 64, 4
ROWS = USERS_HERE * LENGTH
CELLS = SIDE * SIDE
HALF = 2
LINKS_FIRST = [
    (HALF * p + q, SIDE * (2 * p + a - 1) + 2 * q + b - 1, 3 * a + b)
    for p in range(HALF)
    for q in range(HALF)
    for a in range(3)
    for b in range(3)
    if 0 <= 2 * p + a - 1 < SIDE and 0 <= 2 * q + b - 1 < SIDE
]
LINKS_SECOND = [(0, 4), (1, 5), (2, 7), (3, 8)]


AT_N2, AT_H2, AT_SP2, AT_G2, AT_D2, AT_N1, AT_H1, AT_SP1, INNER = 0, 4, 8, 12, 28, 44, 60, 76, 92


def dot_nn(a, b):
    return lax.dot_general(a, b, (((1,), (0,)), ((), ())), preferred_element_type=F32)


def dot_nt(a, b):
    return lax.dot_general(a, b, (((1,), (1,)), ((), ())), preferred_element_type=F32)


def dot_tn(a, b):
    return lax.dot_general(a, b, (((0,), (0,)), ((), ())), preferred_element_type=F32)


def silu_and_slope(v):
    gate = 0.5 * jnp.tanh(0.5 * v) + 0.5
    value = v * gate
    return value, gate + value - value * gate


def column_of(row):
    n = row.shape[1]
    same = lax.broadcasted_iota(jnp.int32, (n, n), 0) == lax.broadcasted_iota(jnp.int32, (n, n), 1)
    return jnp.sum(jnp.where(same, row.astype(F32), 0.0), axis=1, keepdims=True).astype(jnp.int32)


def per_user(lengths):
    user = lax.broadcasted_iota(jnp.int32, (8, 1), 0)
    length = jnp.ones((8, 1), jnp.int32)
    for u in range(USERS_HERE):
        length = jnp.where(user == u, lengths[u], length)
    return user, length


def prepare_tower(lengths, cot, project, up, down, mixer, rows):
    mixer[...] = dot_nn(project[...], up[...]).astype(BF)
    _, length = per_user(lengths)
    shared = cot[...] / length[0:4].astype(F32)
    shared = jnp.concatenate([shared, shared], axis=0)
    coarse = shared.astype(BF)
    fine = (shared - coarse.astype(F32)).astype(BF)
    rows[:, 0:FH] = dot_nt(coarse, down[...])
    for at, part in ((FH, project[0:128]), (FH + 128, project[64:192])):
        rows[:, at : at + 128] = dot_nt(coarse, part) + dot_nt(fine, part)


def conv_forward(
    lengths, x, counts_row, cot, e1, s1, t1, p1, e2, s2, t2, p2, *rest,
):
    *kept, framed1, framed2 = rest
    block = None
    if len(kept) == 1:
        (block,) = kept
    else:
        project, up, down, mixer, per_user_rows, *kept = kept
        prepare_tower(lengths, cot, project, up, down, mixer, per_user_rows)
        taps, weights, outer, inner, o1 = kept
    counts = column_of(counts_row[...])
    zero4 = jnp.zeros((HALF * HALF, ITEMS_HERE, E), F32)
    framed1[0] = zero4
    framed1[FRAMES + 1] = zero4
    zero1 = jnp.zeros((ITEMS_HERE, E), F32)
    framed2[0] = zero1
    framed2[FRAMES + 1] = zero1
    taps1 = s1[...].astype(F32)
    taps2 = s2[...].astype(F32)
    frame1 = t1[...].astype(F32)
    frame2 = t2[...].astype(F32)
    if block is None:
        taps[...] = jnp.zeros((56, E), F32)
        for at, ref in ((0, s1), (9, t1), (12, s2), (21, t2)):
            taps[at : at + ref.shape[0]] = ref[...].astype(F32)
        taps[24:56, 0:128] = jnp.broadcast_to(counts.astype(F32), (ITEMS_HERE, 128))

    if block is None:
        x.ready(), e1.ready()

    def grow(f, _):
        live = f < counts
        x_f = x[pl.ds(f * CELLS, CELLS)]
        x_f = jnp.where(live[None], x_f, jnp.zeros_like(x_f))
        pre = dot_nn(x_f.reshape(CELLS * ITEMS_HERE, C), e1[...])
        value, slope = silu_and_slope(pre)
        value = value.astype(BF).reshape(CELLS, ITEMS_HERE, E)
        if block is None:
            outer[pl.ds(f * CELLS, CELLS)] = value
            outer[pl.ds((FRAMES + f) * CELLS, CELLS)] = slope.astype(BF).reshape(CELLS, ITEMS_HERE, E)
        outs = [jnp.zeros((ITEMS_HERE, E), F32)] * 4
        for out_cell, in_cell, tap in LINKS_FIRST:
            outs[out_cell] = outs[out_cell] + value[in_cell].astype(F32) * taps1[tap]
        for out_cell in range(4):
            framed1[f + 1, out_cell] = outs[out_cell]
            if block is None:
                inner[AT_SP1 + f * 4 + out_cell] = outs[out_cell].astype(BF)
        return 0

    lax.fori_loop(0, FRAMES, grow, 0, unroll=True)
    narrow = []
    for f in range(FRAMES):
        summed = framed1[f] * frame1[0] + framed1[f + 1] * frame1[1] + framed1[f + 2] * frame1[2]
        value, slope = silu_and_slope(summed)
        narrow.append(value.astype(BF))
        if block is None:
            inner[AT_H1 + f * 4 : AT_H1 + f * 4 + 4] = slope.astype(BF)
    narrow = jnp.concatenate(narrow, axis=0)
    first = dot_nt(narrow.reshape(FRAMES * 4 * ITEMS_HERE, E), p1[...]).astype(BF)
    value, slope = silu_and_slope(dot_nn(first, e2[...]))
    value = value.astype(BF).reshape(FRAMES * 4, ITEMS_HERE, E)
    if block is None:
        inner[AT_N1 : AT_N1 + 16] = narrow
        o1[...] = first
        inner[AT_G2 : AT_G2 + 16] = value
        inner[AT_D2 : AT_D2 + 16] = slope.astype(BF).reshape(FRAMES * 4, ITEMS_HERE, E)
        weights[0:192] = p2[...]
        weights[192:384] = e2[...]
        weights[384:576] = p1[...]
    for f in range(FRAMES):
        total = jnp.zeros((ITEMS_HERE, E), F32)
        for cell, tap in LINKS_SECOND:
            total = total + value[f * 4 + cell].astype(F32) * taps2[tap]
        framed2[f + 1] = total
        if block is None:
            inner[AT_SP2 + f] = total.astype(BF)
    narrow = []
    for f in range(FRAMES):
        summed = framed2[f] * frame2[0] + framed2[f + 1] * frame2[1] + framed2[f + 2] * frame2[2]
        value, slope = silu_and_slope(summed)
        narrow.append(value.astype(BF))
        if block is None:
            inner[AT_N2 + f] = value.astype(BF)
            inner[AT_H2 + f] = slope.astype(BF)
    if block is None:
        return
    second = dot_nt(jnp.concatenate(narrow, axis=0), p2[...]).astype(BF)
    pooled = jnp.zeros((ITEMS_HERE, C), F32)
    for f in range(FRAMES):
        live = (f < counts).astype(F32)
        pooled = pooled + live * second[f * ITEMS_HERE : (f + 1) * ITEMS_HERE].astype(F32)
    pooled = pooled / counts.astype(F32)
    _, length = per_user(lengths)
    shared = cot[...] / length[0:4].astype(F32)
    pieces = []
    for k in range(8):
        piece = shared[:, (k // 2) * 128 : (k // 2 + 1) * 128]
        pieces.append(piece if k % 2 else pltpu.roll(piece, 64, 1))
    lane = lax.broadcasted_iota(jnp.int32, (ITEMS_HERE, 128), 1)
    shared = jnp.concatenate(pieces, axis=0)
    high = jnp.concatenate([pooled[:, 128:192], pooled[:, 0:64]], axis=1)
    rows = jnp.concatenate([pooled[:, 0:128], jnp.where(lane < 64, high, shared)], axis=0).astype(BF)
    block[...] = jnp.broadcast_to(rows[None], (CHIPS, 64, 128))


def gelu_and_slope(v):
    scale = 0.7978845608028654
    square = v * v
    bent = jnp.tanh(scale * v * (1.0 + 0.044715 * square))
    gate = 0.5 * (1.0 + bent)
    return v * gate, gate + 0.5 * v * (1.0 - bent * bent) * (scale * (1.0 + 3 * 0.044715 * square))


def for_live_rows(lengths, per_row):
    position = lax.broadcasted_iota(jnp.int32, (LENGTH, 1), 0)
    return jnp.concatenate([(position < lengths[u]).astype(F32) * per_row(u) for u in range(USERS_HERE)], axis=0)


def tower(
    core, lengths, own, other, ids_ref, mixer, rows,
    sent, picked_out,
):
    ids = jnp.concatenate([column_of(ids_ref[u : u + 1]) for u in range(USERS_HERE)], axis=0)
    owner = ids // ITEMS_HERE
    within = ids - owner * ITEMS_HERE
    chip = owner // 2
    place = chip * ITEMS_HERE + within
    mine = (owner - chip * 2) == core[0]
    lanes = lax.broadcasted_iota(jnp.int32, (ROWS, CHIPS * ITEMS_HERE), 1)
    pick_own = (lanes == jnp.where(mine, place, -1)).astype(F32).astype(BF)
    pick_other = (lanes == jnp.where(mine, -1, place)).astype(F32).astype(BF)

    def rows_of(ref):
        low = ref[:, 0:32, :].reshape(CHIPS * ITEMS_HERE, 128)
        high = ref[:, 32:64, :].reshape(CHIPS * ITEMS_HERE, 128)
        return jnp.concatenate([low, high], axis=1)

    across = lax.broadcasted_iota(jnp.int32, (ROWS, ROWS), 1)
    down_rows = lax.broadcasted_iota(jnp.int32, (ROWS, ROWS), 0)
    owner_row = jnp.sum(jnp.where(across == down_rows, owner.astype(F32), 0.0), axis=0, keepdims=True).astype(jnp.int32)
    earlier = down_rows < across
    rank = jnp.sum(((owner == owner_row) & earlier).astype(F32), axis=0, keepdims=True).astype(jnp.int32)
    slot = owner_row * 8 + rank
    sent_at = lax.broadcasted_iota(jnp.int32, (DEVICES * 8, ROWS), 0)
    put_low = (sent_at == slot).astype(F32).astype(BF)
    put_high = (sent_at == slot + CAPACITY).astype(F32).astype(BF)
    own, other = own.ready(), other.ready()
    picked = dot_nn(pick_own, rows_of(own)).astype(BF) + dot_nn(pick_other, rows_of(other)).astype(BF)
    picked_out[...] = picked
    picked_out.leave()
    _, slope = gelu_and_slope(dot_nn(picked[:, 0:C], mixer[...]))
    pre_grad = for_live_rows(lengths, lambda u: rows[u : u + 1, 0:FH] * slope[u * LENGTH : (u + 1) * LENGTH]).astype(BF)
    low = dot_nt(pre_grad, mixer[0:128]) + for_live_rows(lengths, lambda u: rows[u : u + 1, FH : FH + 128])
    high = dot_nt(pre_grad, mixer[64:192]) + for_live_rows(lengths, lambda u: rows[u : u + 1, FH + 128 : FH + 256])
    lane = lax.broadcasted_iota(jnp.int32, (ROWS, 128), 1)
    tag = within.astype(F32)
    low = jnp.where(lane < 96, low, jnp.where(lane == 96, tag, 0.0)).astype(BF)
    high = jnp.where(lane >= 32, high, jnp.where(lane == 0, tag, 0.0)).astype(BF)

    back = (dot_nn(put_low, low) + dot_nn(put_high, high)).astype(BF)
    sent[...] = back.reshape(DEVICES, 8, 128)


def tower_sums(
    core, lengths, picked, rows, project, up, down,
    up_keep, up_send, factors, user_vec,
    halves,
):
    picked = picked[...]
    fetched = dot_nn(picked[:, 0:C], project[...]).astype(BF)
    act, slope = gelu_and_slope(dot_nn(fetched, up[...]))
    act = act.astype(BF)
    pre_grad = for_live_rows(lengths, lambda u: rows[u : u + 1, 0:FH] * slope[u * LENGTH : (u + 1) * LENGTH]).astype(BF)
    user, length = per_user(lengths)
    at = lax.broadcasted_iota(jnp.int32, (8, ROWS), 1)
    live = ((at // LENGTH == user) & (at - user * LENGTH < length)).astype(F32).astype(BF)
    act_sum = dot_nn(live, act)
    picked_sum = dot_nn(live, picked)
    pieces = [act_sum[0:4, j * 128 : (j + 1) * 128] for j in range(8)]
    pieces += [picked_sum[0:4, j * 128 : (j + 1) * 128] for j in range(2)]
    factors[...] = jnp.concatenate(pieces + [jnp.zeros((8, 128), F32)], axis=0).astype(BF)
    coarse = act_sum.astype(BF)
    fine = (act_sum - coarse.astype(F32)).astype(BF)
    mixed = dot_nn(live, fetched) + dot_nn(coarse, down[...]) + dot_nn(fine, down[...])
    user_vec[...] = (mixed / length.astype(F32))[0:4]
    up_grad = dot_tn(picked, pre_grad).astype(BF)
    for j in range(FH // 128):
        halves[j // 4, (j % 4) * 256 : (j % 4 + 1) * 256] = up_grad[:, j * 128 : (j + 1) * 128]
    up_keep.leave(halves.at[core[0]])
    up_send.leave(halves.at[1 - core[0]])


def conv_backward(
    core, back, inner, taps, weights, o1, x, outer,
    keep, send,
    spatial_grad, wide, small, halves,
):
    taps1, frame1, taps2, frame2 = taps[0:9], taps[9:12], taps[12:21], taps[21:24]
    counts = taps[24:56, 0:1]

    def tile_sum(v):
        return jnp.sum(v.reshape(-1, 8, E), axis=0)

    small[...] = jnp.zeros(small.shape, F32)
    wide[...] = jnp.zeros(wide.shape, F32)
    got = back[...].reshape(DEVICES * 8, 128)
    row = lax.broadcasted_iota(jnp.int32, (DEVICES * 8, 1), 0)
    is_low = (row & 7) < CAPACITY
    got_f = got.astype(F32)
    tag = jnp.where(is_low, got_f[:, 96:97], got_f[:, 0:1]).astype(jnp.int32)
    named = tag == lax.broadcasted_iota(jnp.int32, (DEVICES * 8, ITEMS_HERE), 1)
    low = dot_tn((named & is_low).astype(F32).astype(BF), got)
    high = dot_tn((named & ~is_low).astype(F32).astype(BF), got)
    pooled_grad = jnp.concatenate([low[:, 0:96], high[:, 32:128]], axis=1)
    shared = pooled_grad / counts
    out_grad = jnp.concatenate(
        [(shared * (counts > f).astype(F32)).astype(BF) for f in range(FRAMES)], axis=0
    )
    inner.ready(), weights.ready(), o1.ready()
    p2, e2, p1 = weights[0:192], weights[192:384], weights[384:576]
    wide[576:768, 0:E] = dot_tn(out_grad, inner[AT_N2 : AT_N2 + 4].reshape(FRAMES * ITEMS_HERE, E))
    summed_grad = dot_nn(out_grad, p2).reshape(FRAMES, ITEMS_HERE, E) * inner[AT_H2 : AT_H2 + 4].astype(F32)
    spread = []
    for f in range(FRAMES):
        total = summed_grad[f] * frame2[1]
        if f + 1 < FRAMES:
            total = total + summed_grad[f + 1] * frame2[0]
        if f > 0:
            total = total + summed_grad[f - 1] * frame2[2]
        spread.append(total)
    for k in range(3):
        total = jnp.zeros((8, E), F32)
        for f in range(FRAMES):
            if 0 <= f + k - 1 < FRAMES:
                total = total + tile_sum(inner[AT_SP2 + f + k - 1].astype(F32) * summed_grad[f])
        small[21 + k] = total
    parts = []
    for f in range(FRAMES):
        for cell, tap in LINKS_SECOND:
            small[12 + tap] += tile_sum(inner[AT_G2 + f * 4 + cell].astype(F32) * spread[f])
            parts.append((spread[f] * taps2[tap] * inner[AT_D2 + f * 4 + cell].astype(F32)).astype(BF))
    grown_grad = jnp.concatenate(parts, axis=0)
    wide[384:576, 0:E] = dot_tn(o1[...], grown_grad)
    first_grad = dot_nt(grown_grad, e2).astype(BF)
    wide[192:384, 0:E] = dot_tn(first_grad, inner[AT_N1 : AT_N1 + 16].reshape(FRAMES * 4 * ITEMS_HERE, E))
    narrow_grad = dot_nn(first_grad, p1).reshape(FRAMES, 4, ITEMS_HERE, E)
    summed_grad = [narrow_grad[f] * inner[AT_H1 + f * 4 : AT_H1 + f * 4 + 4].astype(F32) for f in range(FRAMES)]
    for k in range(3):
        total = jnp.zeros((8, E), F32)
        for f in range(FRAMES):
            if 0 <= f + k - 1 < FRAMES:
                total = total + tile_sum(inner[AT_SP1 + f * 4 + 4 * k - 4 : AT_SP1 + f * 4 + 4 * k].astype(F32) * summed_grad[f])
        small[9 + k] = total
    for f in range(FRAMES):
        total = summed_grad[f] * frame1[1]
        if f + 1 < FRAMES:
            total = total + summed_grad[f + 1] * frame1[0]
        if f > 0:
            total = total + summed_grad[f - 1] * frame1[2]
        spatial_grad[f] = total.astype(BF)

    x.ready(), outer.ready()
    half_taps = taps1.astype(BF)

    def grow_back(f, _):
        live = counts > lax.convert_element_type(f, F32)
        x_f = x[pl.ds(f * CELLS, CELLS)]
        x_f = jnp.where(live[None], x_f, jnp.zeros_like(x_f)).reshape(CELLS * ITEMS_HERE, C)
        outs = [spatial_grad[f, cell] for cell in range(4)]
        sums = [None] * 9
        grads = [None] * CELLS
        for out_cell, in_cell, tap in LINKS_FIRST:
            term = outs[out_cell] * half_taps[tap]
            grads[in_cell] = term if grads[in_cell] is None else grads[in_cell] + term
            term = outer[f * CELLS + in_cell] * outs[out_cell]
            sums[tap] = term if sums[tap] is None else sums[tap] + term
        for tap in range(9):
            small[tap] += tile_sum(sums[tap].astype(F32))
        grads = [grads[cell] * outer[(FRAMES + f) * CELLS + cell] for cell in range(CELLS)]
        wide[0:192, 0:E] += dot_tn(x_f, jnp.concatenate(grads, axis=0))
        return 0

    lax.fori_loop(0, FRAMES, grow_back, 0, unroll=True)
    sums = jnp.sum(small[...], axis=1).astype(BF)
    put = lax.broadcasted_iota(jnp.int32, (32, 128), 1) == lax.broadcasted_iota(jnp.int32, (32, 128), 0) + 64
    wide[0:E, 384:512] += dot_tn(sums, put.astype(F32).astype(BF))
    for j in range(4):
        halves[j // 2, (j % 2) * 768 : (j % 2 + 1) * 768] = wide[:, j * 128 : (j + 1) * 128].astype(BF)
    keep[...] = halves[core[0]]
    send[...] = halves[1 - core[0]]


def merge(conv_a, conv_b, up_a, up_b, factors, out):
    conv = (conv_a[...].astype(F32) + conv_b[...].astype(F32)).astype(BF)
    up = (up_a[...].astype(F32) + up_b[...].astype(F32)).astype(BF)
    out[:, 0:24, :] = conv.reshape(CHIPS, 24, 128)
    out[:, 24:40, :] = up.reshape(CHIPS, 16, 128)
    out[:, 40:80, :] = jnp.broadcast_to(factors[0:40][None], (CHIPS, 40, 128))


def sum_chips(third, out, factors):
    factors[...] = third[:, 40:80, :]
    factors.leave()
    total = jnp.sum(third[:, 0:40, :].astype(F32), axis=0).astype(BF)
    out[...] = jnp.broadcast_to(total[None], (CHIPS, 40, 128))


def finish_low_rank(own, other, factors, factors_other, grad_down, item_base):
    row = lax.broadcasted_iota(jnp.int32, (CHIPS * 8, 128), 0) & 7
    lane = lax.broadcasted_iota(jnp.int32, (CHIPS * 8, 128), 1)
    even = []
    for src in (own, other):
        parts = []
        for k in range(4):
            got = src[:, 32 + 8 * k : 40 + 8 * k, :].reshape(CHIPS * 8, 128).astype(F32)
            left = pltpu.roll(got, 64, 1)
            right = pltpu.roll(got, CHIPS * 8 - 4, 0)
            parts.append(jnp.where(row < 4, jnp.where(lane < 64, left, right), 0.0))
        even.append(jnp.concatenate(parts, axis=1))
    odd = jnp.concatenate([pltpu.roll(v, 4, 0) for v in even], axis=0).astype(BF)
    even = jnp.concatenate(even, axis=0).astype(BF)
    for j in range(5):
        cut = slice(8 * j, 8 * j + 8)
        left = jnp.concatenate(
            [src[:, cut, :].reshape(CHIPS * 8, 128) for src in (factors, factors_other)], axis=0
        )
        first, second = dot_tn(left, even), dot_tn(left, odd)
        if j < 4:
            grad_down[j * 256 : j * 256 + 128] = first
            grad_down[j * 256 + 128 : j * 256 + 256] = second
        else:
            item_base[0:128] = first
            item_base[128:C] = second[0:64]


def finish(
    core, mine, theirs, item_base, project, up,
    ge1, gs1, gt1, gp1, ge2, gs2, gt2, gp2, grad_item, grad_up,
    halves, part_sems,
):
    halves[core[0]] = mine[...]
    halves[1 - core[0]] = theirs[...]
    for j in range(4):
        width = min(128, E - j * 128)
        part = halves[j // 2, :, 0:24, :].reshape(1536, 128)[(j % 2) * 768 : (j % 2 + 1) * 768].astype(F32)
        cut = slice(j * 128, j * 128 + width)
        for i, out in enumerate((ge1, gp1, ge2, gp2)):
            out[:, cut] = part[i * 192 : (i + 1) * 192, 0:width]
    same = lax.broadcasted_iota(jnp.int32, (E, E), 0) == lax.broadcasted_iota(jnp.int32, (E, E), 1)
    for out in (ge1, gp1, ge2, gp2):
        out.leave()
    small = dot_tn(part[0:E].astype(BF), same.astype(F32).astype(BF))
    gs1[...] = small[64:73]
    gt1[...] = small[73:76]
    gs2[...] = small[76:85]
    gt2[...] = small[85:88]
    item = item_base[...]
    wide, parts = [], []
    for j in range(FH // 128):
        wide.append(halves[j // 4, :, 24:40, :].reshape(1024, 128)[(j % 4) * 256 : (j % 4) * 256 + C])
    for j in range(4):
        part = jnp.concatenate(wide[2 * j : 2 * j + 2], axis=1)
        grad_up[:, j * 256 : (j + 1) * 256] = dot_tn(project[...], part)
        parts.append(grad_up.leave_part((slice(None), pl.ds(j * 256, 256)), part_sems.at[j]))
    item = item + dot_nt(jnp.concatenate(wide, axis=1), up[...])
    grad_item[...] = item
    grad_item.leave()
    for part in parts:
        part.wait()


def shape(dims, dtype=BF):
    return jax.ShapeDtypeStruct(dims, dtype)


class Arriving:
    def __init__(self, copy, ref):
        self.copy, self.ref, self.begun = copy, ref, False

    def begin(self):
        if not self.begun:
            self.copy.start()
            self.begun = True

    def ready(self):
        if self.copy is not None:
            self.begin()
            self.copy.wait()
            self.copy = None
        return self.ref

    def __getitem__(self, index):
        return self.ready()[index]


class Leaving:
    def __init__(self, ref, target, semaphore):
        self.ref, self.target, self.semaphore, self.copy = ref, target, semaphore, None

    def __setitem__(self, index, value):
        self.ref[index] = value

    def leave_part(self, index, semaphore):
        part = pltpu.make_async_copy(self.ref.at[index], self.target.at[index], semaphore)
        part.start()
        return part

    def leave(self, source=None):
        source = self.ref if source is None else source
        self.copy = pltpu.make_async_copy(source, self.target, self.semaphore)
        self.copy.start()


def call(kernel, outs, places, out_places, scratch=(), unstaged=(), megabytes=58, aliases=None):
    staged_in = [i for i, p in enumerate(places) if p in "hw"]
    staged_out = [i for i, p in enumerate(out_places) if p in "hw"]
    spaces = {"s": pltpu.SMEM, "v": pltpu.VMEM, "h": pl.ANY, "w": pl.ANY}

    def run(*args):
        stages = [pltpu.VMEM(args[i].shape, args[i].dtype) for i in staged_in]
        stages += [pltpu.VMEM((16, 128) if i in unstaged else outs[i].shape, outs[i].dtype) for i in staged_out]
        sems = [pltpu.SemaphoreType.DMA((max(len(v), 1),)) for v in (staged_in, staged_out)]

        def body(*refs):
            ins, rest = list(refs[: len(args)]), list(refs[len(args) :])
            results, rest = rest[: len(outs)], rest[len(outs) :]
            own, rest = rest[: len(scratch)], rest[len(scratch) :]
            sem_in, sem_out = rest[-2:]
            for k, i in enumerate(staged_in):
                copy = pltpu.make_async_copy(ins[i], rest[k], sem_in.at[k])
                ins[i] = Arriving(copy, rest[k])
                if places[i] == "h":
                    ins[i].begin()
            for k, i in enumerate(staged_out):
                results[i] = Leaving(rest[len(staged_in) + k], results[i], sem_out.at[k])
            kernel(*ins, *results, *own)
            for i in staged_in:
                ins[i].ready()
            for i in staged_out:
                if results[i].copy is None and out_places[i] == "h":
                    results[i].leave()
            for i in staged_out:
                if results[i].copy is not None:
                    results[i].copy.wait()

        return pl.pallas_call(
            body,
            out_shape=outs,
            in_specs=[pl.BlockSpec(memory_space=spaces[p]) for p in places],
            out_specs=[pl.BlockSpec(memory_space=spaces[p]) for p in out_places],
            scratch_shapes=list(scratch) + stages + sems,
            input_output_aliases=aliases or {},
            cost_estimate=pl.CostEstimate(flops=10**9, bytes_accessed=10**7, transcendentals=10**6),
            compiler_params=pltpu.CompilerParams(vmem_limit_bytes=megabytes * 1024 * 1024),
        )(*args)

    return run


def local(
    clips, clip_counts, histories, lengths, user_cotangent,
    expand_first, spatial_first, temporal_first, project_first,
    expand_second, spatial_second, temporal_second, project_second,
    item_project, tower_up, tower_down,
):
    same_core = [[i for i in range(DEVICES) if i % 2 == c] for c in range(2)]
    core = (lax.axis_index("seq") % 2).reshape(1)

    def across_chips(v):
        return lax.all_to_all(v, AXES, 0, 0, axis_index_groups=same_core, tiled=True)

    def swap(v):
        return lax.ppermute(v, "seq", [(i, i ^ 1) for i in range(8)])

    x = clips.reshape(ITEMS_HERE, FRAMES * CELLS, C).transpose(1, 0, 2)
    counts = clip_counts.reshape(1, ITEMS_HERE)
    weights = (
        spatial_first, temporal_first, project_first.T,
        expand_second, spatial_second, temporal_second, project_second.T,
    )
    n = ITEMS_HERE
    framed = [pltpu.VMEM((FRAMES + 2, 4, n, E), F32), pltpu.VMEM((FRAMES + 2, n, E), F32)]
    (block,) = call(conv_forward, [shape((CHIPS, 64, 128))], "svvvvvvvvvvv", "v", framed, megabytes=24)(
        lengths, x, counts, user_cotangent, expand_first, *weights
    )
    kept = call(
        conv_forward,
        [
            shape((C, FH)), shape((8, FH + 256), F32),
            shape((56, E), F32), shape((576, E)), shape((2 * 64, n, E)), shape((INNER, n, E)), shape((512, C)),
        ],
        "shvvhvvhhvvhhhh",
        "h" * 7,
        framed,
    )(lengths, x, counts, user_cotangent, expand_first, *weights, item_project, tower_up, tower_down)
    own = across_chips(block)
    own, (mixer, user_rows, taps, kept_weights, outer, inner, o1) = lax.optimization_barrier((own, kept))
    other = swap(own)
    sent, picked = call(tower, [shape((DEVICES, 8, 128)), shape((ROWS, 256))], "sshhvhh", "hh")(
        core, lengths, own, other, histories, mixer, user_rows
    )
    back = lax.all_to_all(sent, AXES, 0, 0, tiled=True)
    up_keep, up_send, factors, user_vec = call(
        tower_sums,
        [shape((1024, 128)), shape((1024, 128)), shape((48, 128)), shape((USERS_HERE, D), F32)],
        "sshhhhh",
        "hhhv",
        [pltpu.VMEM((2, 1024, 128), BF)],
        unstaged=(0, 1),
    )(core, lengths, picked, user_rows, item_project, tower_up, tower_down)
    back, up_send = lax.optimization_barrier((back, up_send))
    up_other = swap(up_send)
    conv_keep, conv_send = call(
        conv_backward,
        [shape((1536, 128)), shape((1536, 128))],
        "sv" + "h" * 6,
        "vv",
        [
            pltpu.VMEM((4, 4, n, E), BF),
            pltpu.VMEM((768, 512), F32),
            pltpu.VMEM((32, 8, E), F32),
            pltpu.VMEM((2, 1536, 128), BF),
        ],
        megabytes=50,
    )(core, back, inner, taps, kept_weights, o1, x, outer)
    (third,) = call(merge, [shape((CHIPS, 80, 128))], "vvvvv", "v", megabytes=16)(
        conv_keep, swap(conv_send), up_keep, up_other, factors
    )
    third = across_chips(third)
    fourth, factors = call(
        sum_chips, [shape((CHIPS, 40, 128)), shape((CHIPS, 40, 128))], "v", "vh", megabytes=16
    )(third)
    fourth = across_chips(fourth)
    grad_down, item_base = call(finish_low_rank, [shape((FH, D), F32), shape((C, D), F32)], "hhhh", "hh")(
        own, other, factors, swap(factors)
    )
    fourth, item_base = lax.optimization_barrier((fourth, item_base))
    *conv_grads, grad_item, grad_up = call(
        finish,
        [shape((C, E), F32), shape((9, E), F32), shape((3, E), F32), shape((C, E), F32)] * 2
        + [shape((C, D), F32), shape((D, FH), F32)],
        "svvhhh",
        "hvvhhvvhhw",
        [pltpu.VMEM((2, CHIPS, 40, 128), BF), pltpu.SemaphoreType.DMA((4,))],
        megabytes=32,
        aliases={3: 8},
    )(core, fourth, swap(fourth), item_base, item_project, tower_up)
    conv_grads[3] = conv_grads[3].T
    conv_grads[7] = conv_grads[7].T
    return (user_vec, *conv_grads, grad_item, grad_up, grad_down)


def solution(mesh):
    spread = P(AXES)
    return jax.shard_map(
        local,
        mesh=mesh,
        in_specs=(spread,) * 5 + (P(),) * 11,
        out_specs=(spread,) + (P(),) * 11,
        check_vma=False,
    )
```

```python
import jax
import jax.numpy as jnp
from jax import lax
from jax.experimental import pallas as pl
from jax.experimental.pallas import tpu as pltpu
from jax.sharding import PartitionSpec as P

BF = jnp.bfloat16
F32 = jnp.float32
AXES = ("bulk", "seq")
C, E, D, FH = 192, 432, 512, 1024
FRAMES, SIDE, ITEMS_HERE, USERS_HERE, LENGTH = 4, 4, 32, 4, 64
DEVICES, CHIPS, CAPACITY = 128, 64, 4
ROWS = USERS_HERE * LENGTH
CELLS = SIDE * SIDE
HALF = 2
LINKS_FIRST = [
    (HALF * p + q, SIDE * (2 * p + a - 1) + 2 * q + b - 1, 3 * a + b)
    for p in range(HALF)
    for q in range(HALF)
    for a in range(3)
    for b in range(3)
    if 0 <= 2 * p + a - 1 < SIDE and 0 <= 2 * q + b - 1 < SIDE
]
LINKS_SECOND = [(0, 4), (1, 5), (2, 7), (3, 8)]


AT_N2, AT_H2, AT_SP2, AT_G2, AT_D2, AT_N1, AT_H1, AT_SP1, INNER = 0, 4, 8, 12, 28, 44, 60, 76, 92


def dot_nn(a, b):
    return lax.dot_general(a, b, (((1,), (0,)), ((), ())), preferred_element_type=F32)


def dot_nt(a, b):
    return lax.dot_general(a, b, (((1,), (1,)), ((), ())), preferred_element_type=F32)


def dot_tn(a, b):
    return lax.dot_general(a, b, (((0,), (0,)), ((), ())), preferred_element_type=F32)


def silu_and_slope(v):
    gate = 0.5 * jnp.tanh(0.5 * v) + 0.5
    value = v * gate
    return value, gate + value - value * gate


def column_of(row):
    n = row.shape[1]
    same = lax.broadcasted_iota(jnp.int32, (n, n), 0) == lax.broadcasted_iota(jnp.int32, (n, n), 1)
    return jnp.sum(jnp.where(same, row.astype(F32), 0.0), axis=1, keepdims=True).astype(jnp.int32)


def per_user(lengths):
    user = lax.broadcasted_iota(jnp.int32, (8, 1), 0)
    length = jnp.ones((8, 1), jnp.int32)
    for u in range(USERS_HERE):
        length = jnp.where(user == u, lengths[u], length)
    return user, length


def prepare_tower(lengths, cot, project, up, down, mixer, rows):
    mixer[...] = dot_nn(project[...], up[...]).astype(BF)
    _, length = per_user(lengths)
    shared = cot[...] / length[0:4].astype(F32)
    shared = jnp.concatenate([shared, shared], axis=0)
    coarse = shared.astype(BF)
    fine = (shared - coarse.astype(F32)).astype(BF)
    rows[:, 0:FH] = dot_nt(coarse, down[...])
    for at, part in ((FH, project[0:128]), (FH + 128, project[64:192])):
        rows[:, at : at + 128] = dot_nt(coarse, part) + dot_nt(fine, part)


def conv_forward(
    lengths, x, counts_row, cot, e1, s1, t1, p1, e2, s2, t2, p2, *rest,
):
    *kept, framed1, framed2 = rest
    block = None
    if len(kept) == 1:
        (block,) = kept
    else:
        project, up, down, mixer, per_user_rows, *kept = kept
        prepare_tower(lengths, cot, project, up, down, mixer, per_user_rows)
        taps, weights, outer, inner, o1 = kept
    counts = column_of(counts_row[...])
    zero4 = jnp.zeros((HALF * HALF, ITEMS_HERE, E), F32)
    framed1[0] = zero4
    framed1[FRAMES + 1] = zero4
    zero1 = jnp.zeros((ITEMS_HERE, E), F32)
    framed2[0] = zero1
    framed2[FRAMES + 1] = zero1
    half_taps = s1[...]
    taps2 = s2[...].astype(F32)
    frame1 = t1[...].astype(F32)
    frame2 = t2[...].astype(F32)
    if block is None:
        taps[...] = jnp.zeros((56, E), F32)
        for at, ref in ((0, s1), (9, t1), (12, s2), (21, t2)):
            taps[at : at + ref.shape[0]] = ref[...].astype(F32)
        taps[24:56, 0:128] = jnp.broadcast_to(counts.astype(F32), (ITEMS_HERE, 128))

    if block is None:
        x.ready(), e1.ready()

    def grow(f, _):
        live = f < counts
        x_f = x[pl.ds(f * CELLS, CELLS)]
        x_f = jnp.where(live[None], x_f, jnp.zeros_like(x_f))
        pre = dot_nn(x_f.reshape(CELLS * ITEMS_HERE, C), e1[...])
        value, slope = silu_and_slope(pre)
        value = value.astype(BF).reshape(CELLS, ITEMS_HERE, E)
        if block is None:
            outer[pl.ds(f * CELLS, CELLS)] = value
            outer[pl.ds((FRAMES + f) * CELLS, CELLS)] = slope.astype(BF).reshape(CELLS, ITEMS_HERE, E)
        outs = [None] * 4
        for out_cell, in_cell, tap in LINKS_FIRST:
            term = value[in_cell] * half_taps[tap]
            outs[out_cell] = term if outs[out_cell] is None else outs[out_cell] + term
        outs = [v.astype(F32) for v in outs]
        for out_cell in range(4):
            framed1[f + 1, out_cell] = outs[out_cell]
            if block is None:
                inner[AT_SP1 + f * 4 + out_cell] = outs[out_cell].astype(BF)
        return 0

    lax.fori_loop(0, FRAMES, grow, 0, unroll=True)
    narrow = []
    for f in range(FRAMES):
        summed = framed1[f] * frame1[0] + framed1[f + 1] * frame1[1] + framed1[f + 2] * frame1[2]
        value, slope = silu_and_slope(summed)
        narrow.append(value.astype(BF))
        if block is None:
            inner[AT_H1 + f * 4 : AT_H1 + f * 4 + 4] = slope.astype(BF)
    narrow = jnp.concatenate(narrow, axis=0)
    first = dot_nt(narrow.reshape(FRAMES * 4 * ITEMS_HERE, E), p1[...]).astype(BF)
    value, slope = silu_and_slope(dot_nn(first, e2[...]))
    value = value.astype(BF).reshape(FRAMES * 4, ITEMS_HERE, E)
    if block is None:
        inner[AT_N1 : AT_N1 + 16] = narrow
        o1[...] = first
        inner[AT_G2 : AT_G2 + 16] = value
        inner[AT_D2 : AT_D2 + 16] = slope.astype(BF).reshape(FRAMES * 4, ITEMS_HERE, E)
        weights[0:192] = p2[...]
        weights[192:384] = e2[...]
        weights[384:576] = p1[...]
    for f in range(FRAMES):
        total = jnp.zeros((ITEMS_HERE, E), F32)
        for cell, tap in LINKS_SECOND:
            total = total + value[f * 4 + cell].astype(F32) * taps2[tap]
        framed2[f + 1] = total
        if block is None:
            inner[AT_SP2 + f] = total.astype(BF)
    narrow = []
    for f in range(FRAMES):
        summed = framed2[f] * frame2[0] + framed2[f + 1] * frame2[1] + framed2[f + 2] * frame2[2]
        value, slope = silu_and_slope(summed)
        narrow.append(value.astype(BF))
        if block is None:
            inner[AT_N2 + f] = value.astype(BF)
            inner[AT_H2 + f] = slope.astype(BF)
    if block is None:
        return
    second = dot_nt(jnp.concatenate(narrow, axis=0), p2[...]).astype(BF)
    pooled = jnp.zeros((ITEMS_HERE, C), F32)
    for f in range(FRAMES):
        live = (f < counts).astype(F32)
        pooled = pooled + live * second[f * ITEMS_HERE : (f + 1) * ITEMS_HERE].astype(F32)
    pooled = pooled / counts.astype(F32)
    _, length = per_user(lengths)
    shared = cot[...] / length[0:4].astype(F32)
    pieces = []
    for k in range(8):
        piece = shared[:, (k // 2) * 128 : (k // 2 + 1) * 128]
        pieces.append(piece if k % 2 else pltpu.roll(piece, 64, 1))
    lane = lax.broadcasted_iota(jnp.int32, (ITEMS_HERE, 128), 1)
    shared = jnp.concatenate(pieces, axis=0)
    high = jnp.concatenate([pooled[:, 128:192], pooled[:, 0:64]], axis=1)
    rows = jnp.concatenate([pooled[:, 0:128], jnp.where(lane < 64, high, shared)], axis=0).astype(BF)
    block[...] = jnp.broadcast_to(rows[None], (CHIPS, 64, 128))


def gelu_and_slope(v):
    scale = 0.7978845608028654
    square = v * v
    bent = jnp.tanh(scale * v * (1.0 + 0.044715 * square))
    gate = 0.5 * (1.0 + bent)
    return v * gate, gate + 0.5 * v * (1.0 - bent * bent) * (scale * (1.0 + 3 * 0.044715 * square))


def for_live_rows(lengths, per_row):
    position = lax.broadcasted_iota(jnp.int32, (LENGTH, 1), 0)
    return jnp.concatenate([(position < lengths[u]).astype(F32) * per_row(u) for u in range(USERS_HERE)], axis=0)


def tower(
    core, lengths, own, other, ids_ref, mixer, rows,
    sent, picked_out,
):
    ids = jnp.concatenate([column_of(ids_ref[u : u + 1]) for u in range(USERS_HERE)], axis=0)
    owner = ids // ITEMS_HERE
    within = ids - owner * ITEMS_HERE
    chip = owner // 2
    place = chip * ITEMS_HERE + within
    mine = (owner - chip * 2) == core[0]
    lanes = lax.broadcasted_iota(jnp.int32, (ROWS, CHIPS * ITEMS_HERE), 1)
    pick_own = (lanes == jnp.where(mine, place, -1)).astype(F32).astype(BF)
    pick_other = (lanes == jnp.where(mine, -1, place)).astype(F32).astype(BF)

    def rows_of(ref):
        low = ref[:, 0:32, :].reshape(CHIPS * ITEMS_HERE, 128)
        high = ref[:, 32:64, :].reshape(CHIPS * ITEMS_HERE, 128)
        return jnp.concatenate([low, high], axis=1)

    across = lax.broadcasted_iota(jnp.int32, (ROWS, ROWS), 1)
    down_rows = lax.broadcasted_iota(jnp.int32, (ROWS, ROWS), 0)
    owner_row = jnp.sum(jnp.where(across == down_rows, owner.astype(F32), 0.0), axis=0, keepdims=True).astype(jnp.int32)
    earlier = down_rows < across
    rank = jnp.sum(((owner == owner_row) & earlier).astype(F32), axis=0, keepdims=True).astype(jnp.int32)
    slot = owner_row * 8 + rank
    sent_at = lax.broadcasted_iota(jnp.int32, (DEVICES * 8, ROWS), 0)
    put_low = (sent_at == slot).astype(F32).astype(BF)
    put_high = (sent_at == slot + CAPACITY).astype(F32).astype(BF)
    own, other = own.ready(), other.ready()
    picked = dot_nn(pick_own, rows_of(own)).astype(BF) + dot_nn(pick_other, rows_of(other)).astype(BF)
    picked_out[...] = picked
    picked_out.leave()
    _, slope = gelu_and_slope(dot_nn(picked[:, 0:C], mixer[...]))
    pre_grad = for_live_rows(lengths, lambda u: rows[u : u + 1, 0:FH] * slope[u * LENGTH : (u + 1) * LENGTH]).astype(BF)
    low = dot_nt(pre_grad, mixer[0:128]) + for_live_rows(lengths, lambda u: rows[u : u + 1, FH : FH + 128])
    high = dot_nt(pre_grad, mixer[64:192]) + for_live_rows(lengths, lambda u: rows[u : u + 1, FH + 128 : FH + 256])
    lane = lax.broadcasted_iota(jnp.int32, (ROWS, 128), 1)
    tag = within.astype(F32)
    low = jnp.where(lane < 96, low, jnp.where(lane == 96, tag, 0.0)).astype(BF)
    high = jnp.where(lane >= 32, high, jnp.where(lane == 0, tag, 0.0)).astype(BF)

    back = (dot_nn(put_low, low) + dot_nn(put_high, high)).astype(BF)
    sent[...] = back.reshape(DEVICES, 8, 128)


def tower_sums(
    core, lengths, picked, rows, project, up, down,
    up_keep, up_send, factors, user_vec,
    halves,
):
    picked = picked[...]
    fetched = dot_nn(picked[:, 0:C], project[...]).astype(BF)
    act, slope = gelu_and_slope(dot_nn(fetched, up[...]))
    act = act.astype(BF)
    pre_grad = for_live_rows(lengths, lambda u: rows[u : u + 1, 0:FH] * slope[u * LENGTH : (u + 1) * LENGTH]).astype(BF)
    user, length = per_user(lengths)
    at = lax.broadcasted_iota(jnp.int32, (8, ROWS), 1)
    live = ((at // LENGTH == user) & (at - user * LENGTH < length)).astype(F32).astype(BF)
    act_sum = dot_nn(live, act)
    picked_sum = dot_nn(live, picked)
    pieces = [act_sum[0:4, j * 128 : (j + 1) * 128] for j in range(8)]
    pieces += [picked_sum[0:4, j * 128 : (j + 1) * 128] for j in range(2)]
    factors[...] = jnp.concatenate(pieces + [jnp.zeros((8, 128), F32)], axis=0).astype(BF)
    coarse = act_sum.astype(BF)
    fine = (act_sum - coarse.astype(F32)).astype(BF)
    mixed = dot_nn(live, fetched) + dot_nn(coarse, down[...]) + dot_nn(fine, down[...])
    user_vec[...] = (mixed / length.astype(F32))[0:4]
    up_grad = dot_tn(picked, pre_grad).astype(BF)
    for j in range(FH // 128):
        halves[j // 4, (j % 4) * 256 : (j % 4 + 1) * 256] = up_grad[:, j * 128 : (j + 1) * 128]
    up_keep.leave(halves.at[core[0]])
    up_send.leave(halves.at[1 - core[0]])


def conv_backward(
    core, back, inner, taps, weights, o1, x, outer,
    keep, send,
    spatial_grad, wide, small, halves,
):
    taps1, frame1, taps2, frame2 = taps[0:9], taps[9:12], taps[12:21], taps[21:24]
    counts = taps[24:56, 0:1]

    def tile_sum(v):
        return jnp.sum(v.reshape(-1, 8, E), axis=0)

    small[...] = jnp.zeros(small.shape, F32)
    wide[...] = jnp.zeros(wide.shape, F32)
    got = back[...].reshape(DEVICES * 8, 128)
    row = lax.broadcasted_iota(jnp.int32, (DEVICES * 8, 1), 0)
    is_low = (row & 7) < CAPACITY
    got_f = got.astype(F32)
    tag = jnp.where(is_low, got_f[:, 96:97], got_f[:, 0:1]).astype(jnp.int32)
    named = tag == lax.broadcasted_iota(jnp.int32, (DEVICES * 8, ITEMS_HERE), 1)
    low = dot_tn((named & is_low).astype(F32).astype(BF), got)
    high = dot_tn((named & ~is_low).astype(F32).astype(BF), got)
    pooled_grad = jnp.concatenate([low[:, 0:96], high[:, 32:128]], axis=1)
    shared = pooled_grad / counts
    out_grad = jnp.concatenate(
        [(shared * (counts > f).astype(F32)).astype(BF) for f in range(FRAMES)], axis=0
    )
    inner.ready(), weights.ready(), o1.ready()
    p2, e2, p1 = weights[0:192], weights[192:384], weights[384:576]
    wide[576:768, 0:E] = dot_tn(out_grad, inner[AT_N2 : AT_N2 + 4].reshape(FRAMES * ITEMS_HERE, E))
    summed_grad = dot_nn(out_grad, p2).reshape(FRAMES, ITEMS_HERE, E) * inner[AT_H2 : AT_H2 + 4].astype(F32)
    spread = []
    for f in range(FRAMES):
        total = summed_grad[f] * frame2[1]
        if f + 1 < FRAMES:
            total = total + summed_grad[f + 1] * frame2[0]
        if f > 0:
            total = total + summed_grad[f - 1] * frame2[2]
        spread.append(total)
    for k in range(3):
        total = jnp.zeros((8, E), F32)
        for f in range(FRAMES):
            if 0 <= f + k - 1 < FRAMES:
                total = total + tile_sum(inner[AT_SP2 + f + k - 1].astype(F32) * summed_grad[f])
        small[21 + k] = total
    parts = []
    for f in range(FRAMES):
        for cell, tap in LINKS_SECOND:
            small[12 + tap] += tile_sum(inner[AT_G2 + f * 4 + cell].astype(F32) * spread[f])
            parts.append((spread[f] * taps2[tap] * inner[AT_D2 + f * 4 + cell].astype(F32)).astype(BF))
    grown_grad = jnp.concatenate(parts, axis=0)
    wide[384:576, 0:E] = dot_tn(o1[...], grown_grad)
    first_grad = dot_nt(grown_grad, e2).astype(BF)
    wide[192:384, 0:E] = dot_tn(first_grad, inner[AT_N1 : AT_N1 + 16].reshape(FRAMES * 4 * ITEMS_HERE, E))
    narrow_grad = dot_nn(first_grad, p1).reshape(FRAMES, 4, ITEMS_HERE, E)
    summed_grad = [narrow_grad[f] * inner[AT_H1 + f * 4 : AT_H1 + f * 4 + 4].astype(F32) for f in range(FRAMES)]
    for k in range(3):
        total = jnp.zeros((8, E), F32)
        for f in range(FRAMES):
            if 0 <= f + k - 1 < FRAMES:
                total = total + tile_sum(inner[AT_SP1 + f * 4 + 4 * k - 4 : AT_SP1 + f * 4 + 4 * k].astype(F32) * summed_grad[f])
        small[9 + k] = total
    for f in range(FRAMES):
        total = summed_grad[f] * frame1[1]
        if f + 1 < FRAMES:
            total = total + summed_grad[f + 1] * frame1[0]
        if f > 0:
            total = total + summed_grad[f - 1] * frame1[2]
        spatial_grad[f] = total.astype(BF)

    x.ready(), outer.ready()
    half_taps = taps1.astype(BF)

    def grow_back(f, _):
        live = counts > lax.convert_element_type(f, F32)
        x_f = x[pl.ds(f * CELLS, CELLS)]
        x_f = jnp.where(live[None], x_f, jnp.zeros_like(x_f)).reshape(CELLS * ITEMS_HERE, C)
        outs = [spatial_grad[f, cell] for cell in range(4)]
        sums = [None] * 9
        grads = [None] * CELLS
        for out_cell, in_cell, tap in LINKS_FIRST:
            term = outs[out_cell] * half_taps[tap]
            grads[in_cell] = term if grads[in_cell] is None else grads[in_cell] + term
            term = outer[f * CELLS + in_cell] * outs[out_cell]
            sums[tap] = term if sums[tap] is None else sums[tap] + term
        for tap in range(9):
            small[tap] += tile_sum(sums[tap].astype(F32))
        grads = [grads[cell] * outer[(FRAMES + f) * CELLS + cell] for cell in range(CELLS)]
        wide[0:192, 0:E] += dot_tn(x_f, jnp.concatenate(grads, axis=0))
        return 0

    lax.fori_loop(0, FRAMES, grow_back, 0, unroll=True)
    sums = jnp.sum(small[...], axis=1).astype(BF)
    put = lax.broadcasted_iota(jnp.int32, (32, 128), 1) == lax.broadcasted_iota(jnp.int32, (32, 128), 0) + 64
    wide[0:E, 384:512] += dot_tn(sums, put.astype(F32).astype(BF))
    for j in range(4):
        halves[j // 2, (j % 2) * 768 : (j % 2 + 1) * 768] = wide[:, j * 128 : (j + 1) * 128].astype(BF)
    keep[...] = halves[core[0]]
    send[...] = halves[1 - core[0]]


def merge(conv_a, conv_b, up_a, up_b, factors, out):
    conv = (conv_a[...].astype(F32) + conv_b[...].astype(F32)).astype(BF)
    up = (up_a[...].astype(F32) + up_b[...].astype(F32)).astype(BF)
    out[:, 0:24, :] = conv.reshape(CHIPS, 24, 128)
    out[:, 24:40, :] = up.reshape(CHIPS, 16, 128)
    out[:, 40:80, :] = jnp.broadcast_to(factors[0:40][None], (CHIPS, 40, 128))


def sum_chips(third, out, factors):
    factors[...] = third[:, 40:80, :]
    factors.leave()
    total = jnp.sum(third[:, 0:40, :].astype(F32), axis=0).astype(BF)
    out[...] = jnp.broadcast_to(total[None], (CHIPS, 40, 128))


def finish_low_rank(own, other, factors, factors_other, grad_down, item_base):
    row = lax.broadcasted_iota(jnp.int32, (CHIPS * 8, 128), 0) & 7
    lane = lax.broadcasted_iota(jnp.int32, (CHIPS * 8, 128), 1)
    even = []
    for src in (own, other):
        parts = []
        for k in range(4):
            got = src[:, 32 + 8 * k : 40 + 8 * k, :].reshape(CHIPS * 8, 128).astype(F32)
            left = pltpu.roll(got, 64, 1)
            right = pltpu.roll(got, CHIPS * 8 - 4, 0)
            parts.append(jnp.where(row < 4, jnp.where(lane < 64, left, right), 0.0))
        even.append(jnp.concatenate(parts, axis=1))
    odd = jnp.concatenate([pltpu.roll(v, 4, 0) for v in even], axis=0).astype(BF)
    even = jnp.concatenate(even, axis=0).astype(BF)
    for j in range(5):
        cut = slice(8 * j, 8 * j + 8)
        left = jnp.concatenate(
            [src[:, cut, :].reshape(CHIPS * 8, 128) for src in (factors, factors_other)], axis=0
        )
        first, second = dot_tn(left, even), dot_tn(left, odd)
        if j < 4:
            grad_down[j * 256 : j * 256 + 128] = first
            grad_down[j * 256 + 128 : j * 256 + 256] = second
        else:
            item_base[0:128] = first
            item_base[128:C] = second[0:64]


def finish(
    core, mine, theirs, item_base, project, up,
    ge1, gs1, gt1, gp1, ge2, gs2, gt2, gp2, grad_item, grad_up,
    halves, part_sems,
):
    halves[core[0]] = mine[...]
    halves[1 - core[0]] = theirs[...]
    for j in range(4):
        width = min(128, E - j * 128)
        part = halves[j // 2, :, 0:24, :].reshape(1536, 128)[(j % 2) * 768 : (j % 2 + 1) * 768].astype(F32)
        cut = slice(j * 128, j * 128 + width)
        for i, out in enumerate((ge1, gp1, ge2, gp2)):
            out[:, cut] = part[i * 192 : (i + 1) * 192, 0:width]
    same = lax.broadcasted_iota(jnp.int32, (E, E), 0) == lax.broadcasted_iota(jnp.int32, (E, E), 1)
    for out in (ge1, gp1, ge2, gp2):
        out.leave()
    small = dot_tn(part[0:E].astype(BF), same.astype(F32).astype(BF))
    gs1[...] = small[64:73]
    gt1[...] = small[73:76]
    gs2[...] = small[76:85]
    gt2[...] = small[85:88]
    item = item_base[...]
    wide, parts = [], []
    for j in range(FH // 128):
        wide.append(halves[j // 4, :, 24:40, :].reshape(1024, 128)[(j % 4) * 256 : (j % 4) * 256 + C])
    for j in range(4):
        part = jnp.concatenate(wide[2 * j : 2 * j + 2], axis=1)
        grad_up[:, j * 256 : (j + 1) * 256] = dot_tn(project[...], part)
        parts.append(grad_up.leave_part((slice(None), pl.ds(j * 256, 256)), part_sems.at[j]))
    item = item + dot_nt(jnp.concatenate(wide, axis=1), up[...])
    grad_item[...] = item
    grad_item.leave()
    for part in parts:
        part.wait()


def shape(dims, dtype=BF):
    return jax.ShapeDtypeStruct(dims, dtype)


class Arriving:
    def __init__(self, copy, ref):
        self.copy, self.ref, self.begun = copy, ref, False

    def begin(self):
        if not self.begun:
            self.copy.start()
            self.begun = True

    def ready(self):
        if self.copy is not None:
            self.begin()
            self.copy.wait()
            self.copy = None
        return self.ref

    def __getitem__(self, index):
        return self.ready()[index]


class Leaving:
    def __init__(self, ref, target, semaphore):
        self.ref, self.target, self.semaphore, self.copy = ref, target, semaphore, None

    def __setitem__(self, index, value):
        self.ref[index] = value

    def leave_part(self, index, semaphore):
        part = pltpu.make_async_copy(self.ref.at[index], self.target.at[index], semaphore)
        part.start()
        return part

    def leave(self, source=None):
        source = self.ref if source is None else source
        self.copy = pltpu.make_async_copy(source, self.target, self.semaphore)
        self.copy.start()


def call(kernel, outs, places, out_places, scratch=(), unstaged=(), megabytes=58, aliases=None):
    staged_in = [i for i, p in enumerate(places) if p in "hw"]
    staged_out = [i for i, p in enumerate(out_places) if p in "hw"]
    spaces = {"s": pltpu.SMEM, "v": pltpu.VMEM, "h": pl.ANY, "w": pl.ANY}

    def run(*args):
        stages = [pltpu.VMEM(args[i].shape, args[i].dtype) for i in staged_in]
        stages += [pltpu.VMEM((16, 128) if i in unstaged else outs[i].shape, outs[i].dtype) for i in staged_out]
        sems = [pltpu.SemaphoreType.DMA((max(len(v), 1),)) for v in (staged_in, staged_out)]

        def body(*refs):
            ins, rest = list(refs[: len(args)]), list(refs[len(args) :])
            results, rest = rest[: len(outs)], rest[len(outs) :]
            own, rest = rest[: len(scratch)], rest[len(scratch) :]
            sem_in, sem_out = rest[-2:]
            for k, i in enumerate(staged_in):
                copy = pltpu.make_async_copy(ins[i], rest[k], sem_in.at[k])
                ins[i] = Arriving(copy, rest[k])
                if places[i] == "h":
                    ins[i].begin()
            for k, i in enumerate(staged_out):
                results[i] = Leaving(rest[len(staged_in) + k], results[i], sem_out.at[k])
            kernel(*ins, *results, *own)
            for i in staged_in:
                ins[i].ready()
            for i in staged_out:
                if results[i].copy is None and out_places[i] == "h":
                    results[i].leave()
            for i in staged_out:
                if results[i].copy is not None:
                    results[i].copy.wait()

        return pl.pallas_call(
            body,
            out_shape=outs,
            in_specs=[pl.BlockSpec(memory_space=spaces[p]) for p in places],
            out_specs=[pl.BlockSpec(memory_space=spaces[p]) for p in out_places],
            scratch_shapes=list(scratch) + stages + sems,
            input_output_aliases=aliases or {},
            cost_estimate=pl.CostEstimate(flops=10**9, bytes_accessed=10**7, transcendentals=10**6),
            compiler_params=pltpu.CompilerParams(vmem_limit_bytes=megabytes * 1024 * 1024),
        )(*args)

    return run


def local(
    clips, clip_counts, histories, lengths, user_cotangent,
    expand_first, spatial_first, temporal_first, project_first,
    expand_second, spatial_second, temporal_second, project_second,
    item_project, tower_up, tower_down,
):
    same_core = [[i for i in range(DEVICES) if i % 2 == c] for c in range(2)]
    core = (lax.axis_index("seq") % 2).reshape(1)

    def across_chips(v):
        return lax.all_to_all(v, AXES, 0, 0, axis_index_groups=same_core, tiled=True)

    def swap(v):
        return lax.ppermute(v, "seq", [(i, i ^ 1) for i in range(8)])

    x = clips.reshape(ITEMS_HERE, FRAMES * CELLS, C).transpose(1, 0, 2)
    counts = clip_counts.reshape(1, ITEMS_HERE)
    weights = (
        spatial_first, temporal_first, project_first.T,
        expand_second, spatial_second, temporal_second, project_second.T,
    )
    n = ITEMS_HERE
    framed = [pltpu.VMEM((FRAMES + 2, 4, n, E), F32), pltpu.VMEM((FRAMES + 2, n, E), F32)]
    (block,) = call(conv_forward, [shape((CHIPS, 64, 128))], "svvvvvvvvvvv", "v", framed, megabytes=24)(
        lengths, x, counts, user_cotangent, expand_first, *weights
    )
    kept = call(
        conv_forward,
        [
            shape((C, FH)), shape((8, FH + 256), F32),
            shape((56, E), F32), shape((576, E)), shape((2 * 64, n, E)), shape((INNER, n, E)), shape((512, C)),
        ],
        "shvvhvvhhvvhhhh",
        "h" * 7,
        framed,
    )(lengths, x, counts, user_cotangent, expand_first, *weights, item_project, tower_up, tower_down)
    own = across_chips(block)
    own, (mixer, user_rows, taps, kept_weights, outer, inner, o1) = lax.optimization_barrier((own, kept))
    other = swap(own)
    sent, picked = call(tower, [shape((DEVICES, 8, 128)), shape((ROWS, 256))], "sshhvhh", "hh")(
        core, lengths, own, other, histories, mixer, user_rows
    )
    back = lax.all_to_all(sent, AXES, 0, 0, tiled=True)
    up_keep, up_send, factors, user_vec = call(
        tower_sums,
        [shape((1024, 128)), shape((1024, 128)), shape((48, 128)), shape((USERS_HERE, D), F32)],
        "sshhhhh",
        "hhhv",
        [pltpu.VMEM((2, 1024, 128), BF)],
        unstaged=(0, 1),
    )(core, lengths, picked, user_rows, item_project, tower_up, tower_down)
    back, up_send = lax.optimization_barrier((back, up_send))
    up_other = swap(up_send)
    conv_keep, conv_send = call(
        conv_backward,
        [shape((1536, 128)), shape((1536, 128))],
        "sv" + "h" * 6,
        "vv",
        [
            pltpu.VMEM((4, 4, n, E), BF),
            pltpu.VMEM((768, 512), F32),
            pltpu.VMEM((32, 8, E), F32),
            pltpu.VMEM((2, 1536, 128), BF),
        ],
        megabytes=50,
    )(core, back, inner, taps, kept_weights, o1, x, outer)
    (third,) = call(merge, [shape((CHIPS, 80, 128))], "vvvvv", "v", megabytes=16)(
        conv_keep, swap(conv_send), up_keep, up_other, factors
    )
    third = across_chips(third)
    fourth, factors = call(
        sum_chips, [shape((CHIPS, 40, 128)), shape((CHIPS, 40, 128))], "v", "vh", megabytes=16
    )(third)
    fourth = across_chips(fourth)
    grad_down, item_base = call(finish_low_rank, [shape((FH, D), F32), shape((C, D), F32)], "hhhh", "hh")(
        own, other, factors, swap(factors)
    )
    fourth, item_base = lax.optimization_barrier((fourth, item_base))
    *conv_grads, grad_item, grad_up = call(
        finish,
        [shape((C, E), F32), shape((9, E), F32), shape((3, E), F32), shape((C, E), F32)] * 2
        + [shape((C, D), F32), shape((D, FH), F32)],
        "svvhhh",
        "hvvhhvvhhw",
        [pltpu.VMEM((2, CHIPS, 40, 128), BF), pltpu.SemaphoreType.DMA((4,))],
        megabytes=32,
        aliases={3: 8},
    )(core, fourth, swap(fourth), item_base, item_project, tower_up)
    conv_grads[3] = conv_grads[3].T
    conv_grads[7] = conv_grads[7].T
    return (user_vec, *conv_grads, grad_item, grad_up, grad_down)


def solution(mesh):
    spread = P(AXES)
    return jax.shard_map(
        local,
        mesh=mesh,
        in_specs=(spread,) * 5 + (P(),) * 11,
        out_specs=(spread,) + (P(),) * 11,
        check_vma=False,
    )
```
